256 devices in a mesh: replica: 32 (over y, x, core), tp: 8 (over z).
Axes of the slice: x: 4, y: 4, z: 8, core: 2. Of those that a mesh axis runs over, the one named last changes fastest.
Arguments:
- features: bfloat16 [2, 1024, 8192], P(None, 'replica', 'tp'), may hold values from -6 to 6
- gain: bfloat16 [8192], P('tp'), may hold values from 0.25 to 1.75
- w_key: bfloat16 [8192, 1024], P(None, 'tp'), may hold values from -0.0625 to 0.0625
- w_value: bfloat16 [8192, 1024], P(None, 'tp'), may hold values from -0.0625 to 0.0625
- pool_a: bfloat16 [1024, 8192, 64], P('replica', 'tp'), may hold values from -0.0625 to 0.0625
- pool_b: bfloat16 [1024, 64, 1024], P('replica', None, 'tp'), may hold values from -0.75 to 0.75
- placement: int32 [1024], replicated, may hold values from 0 to 1023, as said below
- need_lists: int32 [32, 16], replicated, may hold values from 0 to 1023, as said below
- row_adapter: int32 [1024], P('replica'), may hold values from 0 to 47, as said below
- lengths: int32 [1024], P('replica'), may hold values from 2 to 192, as said below
- queries: bfloat16 [2, 1024, 8192], P(None, 'replica', 'tp'), may hold values from -256 to 256
- cache_k: bfloat16 [1024, 192, 1024], P('replica', None, 'tp'), may hold values from -6 to 6
- cache_v: bfloat16 [1024, 192, 1024], P('replica', None, 'tp'), may hold values from -6 to 6
Outputs:
- attention: bfloat16 [2, 1024, 8192], P(None, 'replica', 'tp')
- new_keys: bfloat16 [2, 1024, 1024], P(None, 'replica', 'tp')
- new_values: bfloat16 [2, 1024, 1024], P(None, 'replica', 'tp')
The draws below stay inside these ranges and needn't reach their ends.
Inputs may be any that keep to these rules, and one draw needn't show every extreme that they name: A permutation: adapter a sits in entry placement[a] % 32 of the pool of replica placement[a] // 32. `need_lists`: replica r's list names 16 different adapters stored on replicas other than r; at most 1 of them on one replica, exactly 1 on some. `row_adapter`: every entry below 16 is used by 1 to 2 rows of the replica, some by exactly 2. `lengths`: some row has exactly 192.
All inputs are finite; a program needn't handle non-finite values.
Results may differ from the reference program's by a relative error of at most 0.0056.
Values may be sent and summed in bfloat16 or wider, within the bound.
A program may use at most 128 MiB of HBM per device.

```python
import math
import jax
import jax.numpy as jnp
from jax import lax

D = 8192
KVH = 8
HD = 128
GROUP = 8
R = 64
POOL_REP = 32
NEED = 16
ROWS_REP = 32
STEPS = 2
CACHE = 192
H = 64
KVW = 1024
ADAPTERS = 1024
ROWS_TOTAL = 1024
N_REPLICA = 32


def slot_maps(key):
    placement = jax.random.permutation(key, ADAPTERS).astype(jnp.int32)
    adapter_of_slot = jnp.zeros((ADAPTERS,), jnp.int32).at[placement].set(jnp.arange(ADAPTERS, dtype=jnp.int32))
    return (placement, adapter_of_slot)


def need_table(key):
    placement, adapter_of_slot = slot_maps(key)
    replicas = ADAPTERS // POOL_REP
    inner_key = jax.random.fold_in(key, 1000)
    subkeys = jax.random.split(inner_key, replicas)

    def per_replica(subkey, owner_self):
        key_one, key_two, key_three = jax.random.split(subkey, 3)
        others = (owner_self + 1 + jax.random.permutation(key_one, replicas - 1)) % replicas
        entries = jnp.arange(NEED, dtype=jnp.int32)
        owner_ids = others[entries % (replicas - 1)]
        turns = entries // (replicas - 1)
        offsets = jax.random.randint(key_two, (replicas,), 0, POOL_REP)
        local_ids = (offsets[owner_ids] + turns) % POOL_REP
        chosen = adapter_of_slot[owner_ids * POOL_REP + local_ids]
        return chosen[jax.random.permutation(key_three, NEED)]
    owners = jnp.arange(replicas, dtype=jnp.int32)
    return jax.vmap(per_replica)(subkeys, owners).astype(jnp.int32)


def draw_placement(key, part):
    return slot_maps(key)[0]


def draw_need_lists(key, part):
    return need_table(key)


def draw_row_adapter(key, part):
    key = jax.random.fold_in(key, 3)
    replicas = ROWS_TOTAL // ROWS_REP
    subkeys = jax.random.split(key, replicas)

    def per_replica(subkey):
        key_one, key_two = jax.random.split(subkey)
        menu_local = NEED + jnp.arange(POOL_REP - 1, dtype=jnp.int32)
        menu_listed = 1 + jnp.arange(NEED - 1, dtype=jnp.int32)
        candidates = jnp.concatenate([menu_local, menu_listed])
        extras = candidates[jax.random.permutation(key_one, POOL_REP + NEED - 2)[:ROWS_REP - NEED - 2]]
        fixed_part = jnp.concatenate([jnp.arange(NEED, dtype=jnp.int32), jnp.zeros((1,), jnp.int32), jnp.full((1,), NEED + POOL_REP - 1, jnp.int32)])
        row_ids = jnp.concatenate([fixed_part, extras])
        return row_ids[jax.random.permutation(key_two, ROWS_REP)]
    return jax.vmap(per_replica)(subkeys).reshape(ROWS_TOTAL).astype(jnp.int32)


def draw_lengths(key, part):
    key = jax.random.fold_in(key, 4)
    key_one, key_two = jax.random.split(key)
    replicas = ROWS_TOTAL // ROWS_REP
    levels = jax.random.randint(key_one, (replicas,), 1, 5)
    spans = jnp.repeat(CACHE * levels // 4 - 1, ROWS_REP)
    raw_ints = jax.random.randint(key_two, (ROWS_TOTAL,), 0, 1 << 20)
    lengths = 2 + raw_ints % spans
    return lengths.at[0].set(CACHE).astype(jnp.int32)


def draw_cache_k(key, part):
    key = jax.random.fold_in(key, 5)
    cached_keys = jnp.clip(jax.random.normal(key, (ROWS_TOTAL, CACHE, KVW), jnp.float32), -6.0, 6.0)
    return cached_keys.astype(jnp.bfloat16)


def draw_queries(key, part):
    key = jax.random.fold_in(key, 6)
    key_one = jax.random.fold_in(key, 0)
    full_shape = (STEPS, ROWS_TOTAL, H * HD)
    values = jax.random.normal(key_one, full_shape, jnp.float32)
    return values.astype(jnp.bfloat16)


def block_scale(own_key, extent, cuts, least, top_value):
    level = 1.0
    for position, shards_of in cuts:
        heights = jax.random.uniform(jax.random.fold_in(jax.random.fold_in(own_key, 6), position), (shards_of,), jnp.float32, least / len(cuts), top_value / len(cuts))
        level = level * jnp.repeat(jnp.exp(heights), extent[position] // shards_of).reshape((-1,) + (1,) * (len(extent) - 1 - position))
    return level


def gaussian(stream_key, extent, spread, reach, cuts=(), held_as=jnp.bfloat16):
    drawn = jax.random.normal(stream_key, extent, jnp.float32) * spread
    if len(cuts) > 0:
        drawn = block_scale(stream_key, extent, cuts, -0.22, 0.18) * drawn
    return jnp.clip(drawn, min=-reach, max=reach).astype(held_as)


def setup_inputs(seed: int = 0) -> dict:
    keys = jax.random.split(jax.random.key(seed), 14)
    features = gaussian(keys[0], (STEPS, ROWS_TOTAL, D), 1.0, 6.0, ((1, 32), (2, 8)))
    gain = jnp.clip(1.0 + 0.15 * jax.random.normal(keys[1], (D,), jnp.float32), 0.25, 1.75).astype(jnp.bfloat16)
    w_key = gaussian(keys[2], (D, KVW), D ** -0.5, 0.0625, ((1, 8),))
    w_value = gaussian(keys[3], (D, KVW), D ** -0.5, 0.0625, ((1, 8),))
    pool_a = gaussian(keys[4], (ADAPTERS, D, R), D ** -0.5, 0.0625, ((0, 32), (1, 8)))
    pool_b = gaussian(keys[5], (ADAPTERS, R, KVW), R ** -0.5, 0.75, ((0, 32), (2, 8)))
    placement = draw_placement(jax.random.fold_in(keys[13], 71), 0)
    need_lists = draw_need_lists(jax.random.fold_in(keys[13], 71), 0)
    row_adapter = draw_row_adapter(jax.random.fold_in(keys[13], 71), 0)
    lengths = draw_lengths(jax.random.fold_in(keys[13], 71), 0)
    queries = draw_queries(jax.random.fold_in(keys[13], 71), 0)
    cache_k = draw_cache_k(jax.random.fold_in(keys[13], 71), 0)
    cache_v = gaussian(keys[12], (ROWS_TOTAL, CACHE, KVW), 1.0, 6.0, ((0, 32), (2, 8)))
    return {"features": features, "gain": gain, "w_key": w_key, "w_value": w_value, "pool_a": pool_a, "pool_b": pool_b, "placement": placement, "need_lists": need_lists, "row_adapter": row_adapter, "lengths": lengths, "queries": queries, "cache_k": cache_k, "cache_v": cache_v}


eps = 1e-05
theta = 500000.0

def rotate(key_heads, positions):
    half_size = HD // 2
    frequency = theta ** (-(jnp.arange(half_size, dtype=jnp.float32) * 2.0) / HD)
    angles = positions.astype(jnp.float32)[:, None] * frequency[None, :]
    cosines = jnp.cos(angles)[:, None, :]
    sines = jnp.sin(angles)[:, None, :]
    front_half = key_heads[..., :half_size]
    back_half = key_heads[..., half_size:]
    return jnp.concatenate([front_half * cosines - back_half * sines, back_half * cosines + front_half * sines], axis=-1)

def attend(query_heads, cache_keys, cache_values, lengths, fresh_keys, fresh_values):
    score_scale = 1.0 / math.sqrt(HD)
    highest = lax.Precision.HIGHEST
    cached = jnp.einsum('rkgd,rckd->rkgc', query_heads.astype(jnp.float32), cache_keys.astype(jnp.float32), precision=highest) * score_scale
    fresh_scores = jnp.einsum('rkgd,nrkd->rkgn', query_heads.astype(jnp.float32), fresh_keys.astype(jnp.float32), precision=highest) * score_scale
    live_mask = jnp.arange(cache_keys.shape[1], dtype=jnp.int32)[None, :] < lengths[:, None]
    cached = jnp.where(live_mask[:, None, None, :], cached, -1e+30)
    row_max = jnp.maximum(lax.optimization_barrier(jnp.max(cached, axis=-1, keepdims=True)), lax.optimization_barrier(jnp.max(fresh_scores, axis=-1, keepdims=True)))
    cache_exp = jnp.exp(cached - row_max)
    fresh_exp = jnp.exp(fresh_scores - row_max)
    denominator = lax.optimization_barrier(jnp.sum(cache_exp, axis=-1, keepdims=True)) + lax.optimization_barrier(jnp.sum(fresh_exp, axis=-1, keepdims=True))
    cache_weights = (cache_exp / denominator).astype(jnp.bfloat16)
    fresh_weights = (fresh_exp / denominator).astype(jnp.bfloat16)
    mixed = jnp.einsum('rkgc,rckd->rkgd', cache_weights.astype(jnp.float32), cache_values.astype(jnp.float32), precision=highest)
    return mixed + jnp.einsum('rkgn,nrkd->rkgd', fresh_weights.astype(jnp.float32), fresh_values.astype(jnp.float32), precision=highest)

def replica_block(inputs, gain, w_key, w_value, pool_a, pool_b, placement):
    features, row_adapter, lengths, queries, cache_k, cache_v, replica_id, listed = inputs
    row_count = features.shape[1]
    highest = lax.Precision.HIGHEST
    is_listed = row_adapter < NEED
    list_entry = jnp.minimum(row_adapter, NEED - 1).astype(jnp.int32)
    far_slot = placement[listed[list_entry]].astype(jnp.int32)
    near_slot = (replica_id * POOL_REP + row_adapter - NEED).astype(jnp.int32)
    row_slot = jnp.where(is_listed, far_slot, near_slot).astype(jnp.int32)
    down_rows = pool_a[row_slot].astype(jnp.float32)
    up_rows = pool_b[row_slot].astype(jnp.float32)
    gain_wide = gain.astype(jnp.float32)
    cache_keys = cache_k.reshape(row_count, CACHE, KVH, HD)
    cache_values = cache_v.reshape(row_count, CACHE, KVH, HD)
    key_list = []
    value_list = []
    attention = []
    for which_step in range(STEPS):
        values = features[which_step].astype(jnp.float32)
        scaled = values * lax.rsqrt(lax.optimization_barrier(jnp.mean(values * values, axis=-1, keepdims=True)) + eps) * gain_wide
        normed = scaled.astype(jnp.bfloat16)
        key_base = jnp.dot(normed, w_key, preferred_element_type=jnp.float32)
        value_base = jnp.dot(normed, w_value, preferred_element_type=jnp.float32)
        lowrank = jnp.einsum('rd,rdk->rk', normed.astype(jnp.float32), down_rows, precision=highest)
        coeff = lax.optimization_barrier(lowrank.astype(jnp.bfloat16)).astype(jnp.float32)
        delta = jnp.einsum('rk,rkc->rc', coeff, up_rows, precision=highest)
        value_list.append((value_base + delta).astype(jnp.bfloat16))
        rotated = rotate(key_base.reshape(row_count, KVH, HD), lengths + which_step)
        key_list.append(rotated.reshape(row_count, KVW).astype(jnp.bfloat16))
        fresh_keys = jnp.stack(key_list).reshape(which_step + 1, row_count, KVH, HD)
        fresh_values = jnp.stack(value_list).reshape(which_step + 1, row_count, KVH, HD)
        query_heads = queries[which_step].reshape(row_count, KVH, GROUP, HD)
        mixed = attend(query_heads, cache_keys, cache_values, lengths, fresh_keys, fresh_values)
        attention.append(mixed.reshape(row_count, H * HD).astype(jnp.bfloat16))
    return (jnp.stack(attention), jnp.stack(key_list), jnp.stack(value_list))

def reference(features, gain, w_key, w_value, pool_a, pool_b, placement, need_lists, row_adapter, lengths, queries, cache_k, cache_v):

    def per_replica(inputs):
        return replica_block(inputs, gain, w_key, w_value, pool_a, pool_b, placement)
    blocked = (jnp.moveaxis(features.reshape(STEPS, N_REPLICA, ROWS_REP, D), 1, 0), row_adapter.reshape(N_REPLICA, ROWS_REP), lengths.reshape(N_REPLICA, ROWS_REP), jnp.moveaxis(queries.reshape(STEPS, N_REPLICA, ROWS_REP, H * HD), 1, 0), cache_k.reshape(N_REPLICA, ROWS_REP, CACHE, KVW), cache_v.reshape(N_REPLICA, ROWS_REP, CACHE, KVW), jnp.arange(N_REPLICA, dtype=jnp.int32), need_lists)
    attention, new_keys, new_values = lax.map(per_replica, blocked)

    def unblock(stacked):
        return jnp.moveaxis(stacked, 0, 1).reshape(STEPS, ROWS_TOTAL, stacked.shape[-1])
    return (unblock(attention), unblock(new_keys), unblock(new_values))
```

```python
import functools
import math

import jax
import jax.numpy as jnp
import numpy as np
from jax import lax
from jax.experimental import pallas as pl
from jax.experimental.pallas import tpu as pltpu
from jax.sharding import PartitionSpec as P

HD = 128
GROUP = 8
EPS = 1e-05
THETA = 500000.0
NEG = -1e30
MESH = pl.DeviceIdType.MESH
F32 = jnp.float32
BF16 = jnp.bfloat16
QUARTER = 256
NT = (((1,), (1,)), ((), ()))


def iota(shape, dim):
    return lax.broadcasted_iota(jnp.int32, shape, dim)


def kernel(
    nr,
    nt,
    f_ref,
    gain_ref,
    place_ref,
    need_ref,
    ra_ref,
    len_s,
    len_ref,
    freq_ref,
    q_ref,
    wk_hbm,
    wv_hbm,
    pa_hbm,
    pb_hbm,
    ck_hbm,
    cv_hbm,
    att_ref,
    nk_ref,
    nv_ref,
    wbuf,
    pa,
    pb,
    pbt,
    ck,
    cv,
    stats,
    msg,
    got,
    xall,
    ring,
    part,
    rs_got,
    coeff,
    expand,
    ret_send,
    ret_got,
    scores,
    weights,
    fresh_w,
    acc_kv,
    att_acc,
    load_sem,
    st_send,
    st_recv,
    a2a_send,
    a2a_recv,
    ring_send,
    ring_recv,
    rs_send,
    rs_recv,
    ag_send,
    ag_recv,
    re_send,
    re_recv,
):
    r = lax.axis_index("replica")
    t = lax.axis_index("tp")
    rows2, width = f_ref.shape
    rows = rows2 // 2
    need_count = need_ref.shape[0]
    adapters = place_ref.shape[1]
    pool = adapters // nr
    rank = part.shape[1] * nt
    kpart = rank // nt
    nvis = nr * 4
    ntot = nvis + rows2

    loads = [
        pltpu.make_async_copy(ck_hbm, ck, load_sem.at[0]),
        pltpu.make_async_copy(pa_hbm, pa, load_sem.at[1]),
        pltpu.make_async_copy(wk_hbm, wbuf.at[:, pl.ds(0, HD)], load_sem.at[2]),
        pltpu.make_async_copy(wv_hbm, wbuf.at[:, pl.ds(HD, HD)], load_sem.at[3]),
        pltpu.make_async_copy(pb_hbm, pb, load_sem.at[4]),
        pltpu.make_async_copy(cv_hbm, cv, load_sem.at[5]),
    ]
    for load in loads:
        load.start()

    barrier = pltpu.get_barrier_semaphore()

    @pl.loop(1, nr)
    def _(k):
        pl.semaphore_signal(
            barrier, inc=1, device_id=(lax.rem(r + k, nr), t), device_id_type=MESH
        )

    @pl.loop(1, nt)
    def _(k):
        pl.semaphore_signal(
            barrier, inc=1, device_id=(r, lax.rem(t + k, nt)), device_id_type=MESH
        )

    gain = gain_ref[...].astype(F32)
    f32 = f_ref[...].astype(F32)
    lanes = HD
    chunks = width // lanes
    eye = iota((rows2, lanes), 0) == iota((rows2, lanes), 1)
    square_sum = jnp.sum(f32 * f32, axis=1, keepdims=True)
    square_row = jnp.sum(jnp.where(eye, square_sum, 0.0), axis=0, keepdims=True)
    gain_rows = jnp.concatenate(
        [gain[:, c * lanes : (c + 1) * lanes] for c in range(chunks)], axis=0
    )
    stats[t] = jnp.concatenate(
        [gain_rows, jnp.broadcast_to(square_row, (8, lanes))], axis=0
    )
    own = (f32 * gain).astype(BF16)
    xall[pl.ds(nvis, rows2), :] = own

    ra = ra_ref[...]
    need = need_ref[...]
    mine = jnp.sum(
        jnp.where(iota(need.shape, 1) == r, need, 0).astype(F32), axis=1, keepdims=True
    )
    entry = iota((need_count, rows), 0) == ra
    wanted = jnp.sum(jnp.where(entry, mine, 0.0), axis=0, keepdims=True)
    place = place_ref[...]
    home = place // pool
    local = place - home * pool
    at_me = jnp.where(home == r, local + 1, 0)
    table = jnp.concatenate(
        [
            jnp.broadcast_to(x.astype(F32), (8, adapters))
            for x in (home, local, at_me)
        ],
        axis=0,
    ).astype(BF16)
    which = iota((adapters, rows), 0) == wanted.astype(jnp.int32)
    found = jnp.dot(
        table, jnp.where(which, 1.0, 0.0).astype(BF16), preferred_element_type=F32
    )
    owner = found[0:1].astype(jnp.int32)
    eye_r = iota((rows, rows), 0) == iota((rows, rows), 1)
    ra_f = ra.astype(F32)
    ra_col = jnp.sum(jnp.where(eye_r, ra_f, 0.0), axis=1, keepdims=True)
    twin = (ra_col == ra_f) & (iota((rows, rows), 0) < iota((rows, rows), 1))
    turn = jnp.sum(jnp.where(twin, 1.0, 0.0), axis=0, keepdims=True).astype(jnp.int32)
    is_far = ra < need_count
    code = jnp.where(is_far, owner * 16 + turn * 8, -1000)
    code2 = jnp.concatenate([code, code + 4], axis=1)

    slot_iota = iota((nr * 16, rows2), 0)
    total = None
    for j in range(4):
        pick = jnp.where(slot_iota == code2 + j, 1.0, 0.0).astype(BF16)
        piece = jnp.dot(
            pick, own[:, j * QUARTER : (j + 1) * QUARTER], preferred_element_type=F32
        )
        total = piece if total is None else total + piece
    msg[...] = total.astype(BF16)
    got[pl.ds(pl.multiple_of(r * 16, 16), 16), :] = jnp.zeros((16, QUARTER), BF16)
    ret_got[pl.ds(pl.multiple_of(r * 8, 8), 8), :] = jnp.zeros((8, HD), F32)

    pl.semaphore_wait(barrier, nr - 1 + nt - 1)

    right = (r, lax.rem(t + 1, nt))
    left = (r, lax.rem(t + nt - 1, nt))
    half = nt // 2

    def hop(which_way, h, c):
        if which_way == 0:
            have, there, to = (nt - (h - 1)) % nt, nt - h, right
        else:
            have, there, to = h - 1, h, left
        piece = pl.ds(c * rows, rows)
        src = f_ref.at[piece, :] if have == 0 else ring.at[have, piece, :]
        return pltpu.make_async_remote_copy(
            src_ref=src,
            dst_ref=ring.at[there, piece, :],
            send_sem=ring_send.at[which_way, h - 1, c],
            recv_sem=ring_recv.at[there, c],
            device_id=to,
            device_id_type=MESH,
        )

    def hops(h):
        if h < half:
            return [(0, 0), (1, 0), (0, 1), (1, 1)]
        return [(0, 0), (1, 1)]

    for way, c in hops(1):
        hop(way, 1, c).start()

    @pl.loop(1, nt)
    def _(k):
        pltpu.make_async_remote_copy(
            src_ref=stats.at[t],
            dst_ref=stats.at[t],
            send_sem=st_send,
            recv_sem=st_recv,
            device_id=(r, lax.rem(t + k, nt)),
            device_id_type=MESH,
        ).start()

    @pl.loop(1, nr)
    def _(k):
        to = lax.rem(r + k, nr)
        pltpu.make_async_remote_copy(
            src_ref=msg.at[pl.ds(pl.multiple_of(to * 16, 16), 16), :],
            dst_ref=got.at[pl.ds(pl.multiple_of(r * 16, 16), 16), :],
            send_sem=a2a_send,
            recv_sem=a2a_recv,
            device_id=(to, t),
            device_id_type=MESH,
        ).start()

    def wait_bytes(ref, sem):
        pltpu.make_async_copy(ref, ref, sem).wait()

    asked = jnp.zeros((adapters, nr), jnp.bool_)
    p_iota = iota((adapters, nr), 0)
    for e in range(need_count):
        asked = asked | (p_iota == need[e : e + 1, :])
    visit = jnp.dot(
        table, jnp.where(asked, 1.0, 0.0).astype(BF16), preferred_element_type=F32
    )[16:24]
    spread = jnp.where(iota((nr, nvis), 1) // 4 == iota((nr, nvis), 0), 1.0, 0.0)
    visit_slot = jnp.dot(
        visit.astype(BF16), spread.astype(BF16), preferred_element_type=F32
    )[0:1].astype(jnp.int32) - 1
    own_slot = jnp.where(is_far, -1, ra - need_count)
    slot_row = jnp.concatenate([visit_slot, own_slot, own_slot], axis=1)

    scale = 1.0 / math.sqrt(HD)
    cache_len = ck.shape[1]
    per_row = 2 * GROUP

    def cached_scores(lo, hi):
        @pl.loop(lo, hi, unroll=4)
        def _(i):
            s = (
                lax.dot_general(q_ref[i], ck[i], NT, preferred_element_type=F32) * scale
            )
            live = iota(s.shape, 1) < len_s[i]
            scores[i] = jnp.where(live, s, NEG)

    def ring_stage(h):
        for way, c in hops(h):
            hop(way, h, c).wait_recv()
            if (way, c) in (hops(h + 1) if h < half else []):
                hop(way, h + 1, c).start()

    loads[0].wait()
    cached_scores(0, rows // 2)
    ring_stage(1)

    loads[1].wait()
    wait_bytes(got.at[pl.ds(0, (nr - 1) * 16), :], a2a_recv)
    arrived = got[...]
    for j in range(4):
        gather = iota((nvis, nr * 16), 1) == iota((nvis, nr * 16), 0) * 4 + j
        xall[pl.ds(0, nvis), j * QUARTER : (j + 1) * QUARTER] = jnp.dot(
            jnp.where(gather, 1.0, 0.0).astype(BF16),
            arrived,
            preferred_element_type=F32,
        ).astype(BF16)
    x = xall[...]
    group = 8
    part[...] = jnp.zeros(part.shape, F32)

    @pl.loop(0, pool // group)
    def _(g):
        base = g * group
        block = lax.dot_general(
            pa[pl.ds(pl.multiple_of(base * rank, group * rank), group * rank), :],
            x,
            NT,
            preferred_element_type=F32,
        )
        picked = jnp.zeros((rank, ntot), F32)
        for s in range(group):
            picked += jnp.where(
                slot_row == base + s, block[s * rank : (s + 1) * rank], 0.0
            )
        part[:, :, pl.ds(0, ntot)] += picked.reshape(nt, kpart, ntot)

    @pl.loop(1, nt)
    def _(k):
        to = lax.rem(t + k, nt)
        pltpu.make_async_remote_copy(
            src_ref=part.at[to],
            dst_ref=rs_got.at[t],
            send_sem=rs_send,
            recv_sem=rs_recv,
            device_id=(r, to),
            device_id_type=MESH,
        ).start()

    ring_stage(2)
    cached_scores(rows // 2, rows)

    wait_bytes(stats.at[pl.ds(0, nt - 1)], st_recv)
    square = stats[0, 8:16, :]
    for k in range(1, nt):
        square += stats[k, 8:16, :]
    inverse_row = lax.rsqrt(square[0:1] / (width * nt) + EPS)
    inverse = jnp.sum(jnp.where(eye, inverse_row, 0.0), axis=1, keepdims=True)

    def project(o):
        source = lax.rem(t + o, nt)
        block = f_ref[...] if o == 0 else ring[o]
        block = block.astype(F32) * inverse
        gains = stats[source][0:8]
        normed = jnp.concatenate(
            [
                block[:, c * lanes : (c + 1) * lanes] * gains[c : c + 1]
                for c in range(chunks)
            ],
            axis=1,
        ).astype(BF16)
        w = wbuf[pl.ds(pl.multiple_of(source * width, width), width), :]
        product = jnp.dot(normed, w, preferred_element_type=F32)
        if o == 0:
            acc_kv[...] = product
        else:
            acc_kv[...] += product

    loads[2].wait()
    loads[3].wait()
    project(0)
    for h in range(1, half):
        if h >= 3:
            ring_stage(h)
        project(nt - h)
        project(h)

    wait_bytes(rs_got.at[pl.ds(0, nt - 1)], rs_recv)
    whole = part[t]
    for k in range(nt):
        whole += jnp.where(k == t, 0.0, rs_got[k])
    coeff[t] = whole

    @pl.loop(1, nt)
    def _(k):
        pltpu.make_async_remote_copy(
            src_ref=coeff.at[t],
            dst_ref=coeff.at[t],
            send_sem=ag_send,
            recv_sem=ag_recv,
            device_id=(r, lax.rem(t + k, nt)),
            device_id_type=MESH,
        ).start()

    loads[4].wait()
    pbt[...] = pb[...].T

    if half == 2:
        ring_stage(2)
    elif half >= 4:
        ring_stage(half)
    project(half)

    length_row = len_ref[...].astype(F32)
    positions = jnp.sum(
        jnp.where(eye_r, length_row, 0.0), axis=1, keepdims=True
    )
    positions = jnp.concatenate([positions, positions + 1.0], axis=0)
    angle = positions * freq_ref[...]
    sign = jnp.where(iota((rows2, HD), 1) < HD // 2, -1.0, 1.0)
    key = acc_kv[:, 0:HD]
    turned = key * jnp.cos(angle) + pltpu.roll(key, HD // 2, 1) * jnp.sin(angle) * sign
    new_keys = turned.astype(BF16)
    nk_ref[...] = new_keys

    qrows = 8
    span = qrows * per_row
    for b in range(rows // qrows):
        s = scores[b * qrows : (b + 1) * qrows].reshape(span, cache_len)
        q = q_ref[b * qrows : (b + 1) * qrows].reshape(span, HD)
        fresh = (
            lax.dot_general(q, new_keys, NT, preferred_element_type=F32) * scale
        )
        row_of = iota(fresh.shape, 0) // per_row + b * qrows
        step_of = iota(fresh.shape, 0) % per_row // GROUP
        column = iota(fresh.shape, 1)
        seen = (column == row_of) | ((column == row_of + rows) & (step_of == 1))
        fresh = jnp.where(seen, fresh, NEG)
        top = jnp.maximum(
            jnp.max(s, axis=1, keepdims=True), jnp.max(fresh, axis=1, keepdims=True)
        )
        e_cache = jnp.exp(s - top)
        e_fresh = jnp.exp(fresh - top)
        bottom = jnp.sum(e_cache, axis=1, keepdims=True) + jnp.sum(
            e_fresh, axis=1, keepdims=True
        )
        weights[b * qrows : (b + 1) * qrows] = (
            (e_cache / bottom).astype(BF16).reshape(qrows, per_row, cache_len)
        )
        fresh_w[b * span : (b + 1) * span, :] = (e_fresh / bottom).astype(BF16)

    wait_bytes(coeff.at[pl.ds(0, nt - 1)], ag_recv)
    coeffs = coeff[...].reshape(rank, coeff.shape[2])[:, 0:ntot]
    for s in range(pool):
        expand[s * rank : (s + 1) * rank, :] = jnp.where(
            slot_row == s, coeffs, 0.0
        ).astype(BF16)
    delta = jnp.dot(pbt[...], expand[...], preferred_element_type=F32).T
    ret_send[...] = delta[0:nvis]
    own_delta = delta[nvis:ntot]

    @pl.loop(1, nr)
    def _(k):
        to = lax.rem(r + k, nr)
        pltpu.make_async_remote_copy(
            src_ref=ret_send.at[pl.ds(pl.multiple_of(to // 2 * 8, 8), 8), :],
            dst_ref=ret_got.at[pl.ds(pl.multiple_of(r * 8, 8), 8), :],
            send_sem=re_send,
            recv_sem=re_recv,
            device_id=(to, t),
            device_id_type=MESH,
        ).start()

    loads[5].wait()

    @pl.loop(0, rows, unroll=4)
    def _(i):
        att_acc[i] = jnp.dot(weights[i], cv[i], preferred_element_type=F32)

    code_f = jnp.where(
        is_far, owner * 8 + lax.rem(r, 2) * 4 + turn * 2, -1000
    ).astype(F32)
    code_col = jnp.sum(jnp.where(eye_r, code_f, 0.0), axis=1, keepdims=True)
    code_col = jnp.concatenate([code_col, code_col + 1.0], axis=0).astype(jnp.int32)
    back = jnp.where(iota((rows2, nr * 8), 1) == code_col, 1.0, 0.0).astype(BF16)
    wait_bytes(ret_got.at[pl.ds(0, (nr - 1) * 8), :], re_recv)
    returned = ret_got[...]
    high = returned.astype(BF16)
    low = (returned - high.astype(F32)).astype(BF16)
    far_delta = jnp.dot(back, high, preferred_element_type=F32) + jnp.dot(
        back, low, preferred_element_type=F32
    )
    new_values = (acc_kv[:, HD : 2 * HD] + inverse * (far_delta + own_delta)).astype(
        BF16
    )
    nv_ref[...] = new_values
    mixed = att_acc[...].reshape(rows * per_row, HD) + jnp.dot(
        fresh_w[...], new_values, preferred_element_type=F32
    )
    att_ref[...] = mixed.astype(BF16).reshape(rows, per_row, HD)

    for h in range(1, half + 1):
        for way, c in hops(h):
            hop(way, h, c).wait_send()
    wait_bytes(stats.at[pl.ds(0, nt - 1)], st_send)
    wait_bytes(msg.at[pl.ds(0, (nr - 1) * 16), :], a2a_send)
    wait_bytes(part.at[pl.ds(0, nt - 1)], rs_send)
    wait_bytes(coeff.at[pl.ds(0, nt - 1)], ag_send)
    wait_bytes(ret_got.at[pl.ds(0, (nr - 1) * 8), :], re_send)


def shards(
    features,
    gain,
    w_key,
    w_value,
    pool_a,
    pool_b,
    placement,
    need_lists,
    row_adapter,
    lengths,
    queries,
    cache_k,
    cache_v,
):
    nr, nt = lax.axis_size("replica"), lax.axis_size("tp")
    steps, rows, width = features.shape
    pool, _, rank = pool_a.shape
    cache_len = cache_k.shape[1]
    rows2 = steps * rows
    nvis = nr * 4
    ntot = nvis + rows2
    ntot_pad = -(-ntot // HD) * HD
    per_row = steps * GROUP
    q = queries.reshape(steps, rows, GROUP, HD).transpose(1, 0, 2, 3)
    q = q.reshape(rows, per_row, HD)
    half = HD // 2
    frequency = np.float32(THETA) ** (-(np.arange(half, dtype=np.float32) * 2.0) / HD)
    frequency = np.concatenate([frequency, frequency]).astype(np.float32)[None, :]
    vmem = pl.BlockSpec(memory_space=pltpu.VMEM)
    smem = pl.BlockSpec(memory_space=pltpu.SMEM)
    hbm = pl.BlockSpec(memory_space=pl.ANY)
    dma = pltpu.SemaphoreType.DMA
    att, nk, nv = pl.pallas_call(
        functools.partial(kernel, nr, nt),
        out_shape=(
            jax.ShapeDtypeStruct((rows, per_row, HD), BF16),
            jax.ShapeDtypeStruct((rows2, HD), BF16),
            jax.ShapeDtypeStruct((rows2, HD), BF16),
        ),
        in_specs=[vmem] * 5 + [smem] + [vmem] * 3 + [hbm] * 6,
        out_specs=(vmem, vmem, vmem),
        scratch_shapes=[
            pltpu.VMEM((nt * width, 2 * HD), BF16),
            pltpu.VMEM((pool * rank, width), BF16),
            pltpu.VMEM((pool * rank, HD), BF16),
            pltpu.VMEM((HD, pool * rank), BF16),
            pltpu.VMEM((rows, cache_len, HD), BF16),
            pltpu.VMEM((rows, cache_len, HD), BF16),
            pltpu.VMEM((nt, 16, HD), F32),
            pltpu.VMEM((nr * 16, QUARTER), BF16),
            pltpu.VMEM((nr * 16, QUARTER), BF16),
            pltpu.VMEM((ntot, width), BF16),
            pltpu.VMEM((nt, rows2, width), BF16),
            pltpu.VMEM((nt, rank // nt, ntot_pad), F32),
            pltpu.VMEM((nt, rank // nt, ntot_pad), F32),
            pltpu.VMEM((nt, rank // nt, ntot_pad), F32),
            pltpu.VMEM((pool * rank, ntot), BF16),
            pltpu.VMEM((nvis, HD), F32),
            pltpu.VMEM((nr * 8, HD), F32),
            pltpu.VMEM((rows, per_row, cache_len), F32),
            pltpu.VMEM((rows, per_row, cache_len), BF16),
            pltpu.VMEM((rows * per_row, rows2), BF16),
            pltpu.VMEM((rows2, 2 * HD), F32),
            pltpu.VMEM((rows, per_row, HD), F32),
            dma((6,)),
            dma,
            dma,
            dma,
            dma,
            dma((2, max(nt // 2, 1), 2)),
            dma((nt, 2)),
            dma,
            dma,
            dma,
            dma,
            dma,
            dma,
        ],
        compiler_params=pltpu.CompilerParams(
            collective_id=0, has_side_effects=True, vmem_limit_bytes=48 * 2**20
        ),
        cost_estimate=pl.CostEstimate(
            flops=2 * 64 * 8192 * 256, bytes_accessed=12 * 2**20, transcendentals=0
        ),
    )(
        features.reshape(rows2, width),
        gain.reshape(1, width),
        placement.reshape(1, -1),
        need_lists.T,
        row_adapter.reshape(1, rows),
        lengths,
        lengths.reshape(1, rows),
        jnp.asarray(frequency),
        q,
        w_key,
        w_value,
        pool_a.swapaxes(1, 2).reshape(pool * rank, width),
        pool_b.reshape(pool * rank, HD),
        cache_k,
        cache_v,
    )
    attention = att.reshape(rows, steps, GROUP * HD).transpose(1, 0, 2)
    return attention, nk.reshape(steps, rows, HD), nv.reshape(steps, rows, HD)


def solution(mesh):
    placed = (
        P(None, "replica", "tp"),
        P("tp"),
        P(None, "tp"),
        P(None, "tp"),
        P("replica", "tp", None),
        P("replica", None, "tp"),
        P(),
        P(),
        P("replica"),
        P("replica"),
        P(None, "replica", "tp"),
        P("replica", None, "tp"),
        P("replica", None, "tp"),
    )
    return jax.shard_map(
        shards,
        mesh=mesh,
        in_specs=placed,
        out_specs=(P(None, "replica", "tp"), P(None, "replica", "tp"), P(None, "replica", "tp")),
        check_vma=False,
    )
```

```python
import functools
import math

import jax
import jax.numpy as jnp
import numpy as np
from jax import lax
from jax.experimental import pallas as pl
from jax.experimental.pallas import tpu as pltpu
from jax.sharding import PartitionSpec as P

HD = 128
GROUP = 8
EPS = 1e-05
THETA = 500000.0
NEG = -1e30
MESH = pl.DeviceIdType.MESH
F32 = jnp.float32
BF16 = jnp.bfloat16
QUARTER = 256
NT = (((1,), (1,)), ((), ()))


def iota(shape, dim):
    return lax.broadcasted_iota(jnp.int32, shape, dim)


def kernel(
    nr,
    nt,
    f_hbm,
    gain_hbm,
    place_hbm,
    need_hbm,
    ra_hbm,
    len_s_hbm,
    len_hbm,
    freq_hbm,
    q_hbm,
    wk_hbm,
    wv_hbm,
    pa_hbm,
    pb_hbm,
    ck_hbm,
    cv_hbm,
    att_ref,
    nk_ref,
    nv_ref,
    f_ref,
    gain_ref,
    place_ref,
    need_ref,
    ra_ref,
    len_s,
    len_ref,
    freq_ref,
    q_in,
    q_wide,
    q_ref,
    wbuf,
    pa,
    pb,
    pbt,
    ck,
    cv,
    stats,
    msg,
    got,
    xall,
    ring,
    part,
    rs_got,
    coeff,
    expand,
    ret_send,
    ret_got,
    scores,
    weights,
    fresh_w,
    acc_kv,
    att_acc,
    small_sem,
    load_sem,
    st_send,
    st_recv,
    a2a_send,
    a2a_recv,
    ring_send,
    ring_recv,
    rs_send,
    rs_recv,
    ag_send,
    ag_recv,
    re_send,
    re_recv,
):
    r = lax.axis_index("replica")
    t = lax.axis_index("tp")
    rows2, width = f_ref.shape
    rows = rows2 // 2
    need_count = need_ref.shape[0]
    adapters = place_ref.shape[1]
    pool = adapters // nr
    rank = part.shape[1] * nt
    kpart = rank // nt
    nvis = nr * 4
    ntot = nvis + rows2

    small = [
        pltpu.make_async_copy(a, b, small_sem.at[k])
        for k, (a, b) in enumerate(
            [
                (f_hbm, f_ref),
                (gain_hbm, gain_ref),
                (ra_hbm, ra_ref),
                (need_hbm, need_ref),
                (place_hbm, place_ref),
                (len_s_hbm, len_s),
                (len_hbm, len_ref),
                (freq_hbm, freq_ref),
                (q_hbm, q_in),
            ]
        )
    ]
    loads = [
        pltpu.make_async_copy(ck_hbm, ck, load_sem.at[0]),
        pltpu.make_async_copy(pa_hbm, pa, load_sem.at[1]),
        pltpu.make_async_copy(wk_hbm, wbuf.at[:, pl.ds(0, HD)], load_sem.at[2]),
        pltpu.make_async_copy(wv_hbm, wbuf.at[:, pl.ds(HD, HD)], load_sem.at[3]),
        pltpu.make_async_copy(pb_hbm, pb, load_sem.at[4]),
        pltpu.make_async_copy(cv_hbm, cv, load_sem.at[5]),
    ]
    for load in small + loads:
        load.start()

    barrier = pltpu.get_barrier_semaphore()

    @pl.loop(1, nr)
    def _(k):
        pl.semaphore_signal(
            barrier, inc=1, device_id=(lax.rem(r + k, nr), t), device_id_type=MESH
        )

    @pl.loop(1, nt)
    def _(k):
        pl.semaphore_signal(
            barrier, inc=1, device_id=(r, lax.rem(t + k, nt)), device_id_type=MESH
        )

    small[0].wait()
    small[1].wait()
    gain_rows = gain_ref[...].astype(F32)
    f32 = f_ref[...].astype(F32)
    lanes = HD
    chunks = width // lanes
    eye = iota((rows2, lanes), 0) == iota((rows2, lanes), 1)
    square_sum = jnp.sum(f32 * f32, axis=1, keepdims=True)
    square_row = jnp.sum(jnp.where(eye, square_sum, 0.0), axis=0, keepdims=True)
    stats[t] = jnp.concatenate(
        [gain_rows, jnp.broadcast_to(square_row, (8, lanes))], axis=0
    )
    own = jnp.concatenate(
        [
            f32[:, c * lanes : (c + 1) * lanes] * gain_rows[c : c + 1]
            for c in range(chunks)
        ],
        axis=1,
    ).astype(BF16)
    xall[pl.ds(nvis, rows2), :] = own

    for load in small[2:5]:
        load.wait()
    ra = ra_ref[...]
    need = need_ref[...]
    mine = jnp.sum(
        jnp.where(iota(need.shape, 1) == r, need, 0).astype(F32), axis=1, keepdims=True
    )
    entry = iota((need_count, rows), 0) == ra
    wanted = jnp.sum(jnp.where(entry, mine, 0.0), axis=0, keepdims=True)
    place = place_ref[...]
    home = place // pool
    local = place - home * pool
    at_me = jnp.where(home == r, local + 1, 0)
    table = jnp.concatenate(
        [
            jnp.broadcast_to(x.astype(F32), (8, adapters))
            for x in (home, local, at_me)
        ],
        axis=0,
    ).astype(BF16)
    which = iota((adapters, rows), 0) == wanted.astype(jnp.int32)
    found = jnp.dot(
        table, jnp.where(which, 1.0, 0.0).astype(BF16), preferred_element_type=F32
    )
    owner = found[0:1].astype(jnp.int32)
    eye_r = iota((rows, rows), 0) == iota((rows, rows), 1)
    ra_f = ra.astype(F32)
    ra_col = jnp.sum(jnp.where(eye_r, ra_f, 0.0), axis=1, keepdims=True)
    twin = (ra_col == ra_f) & (iota((rows, rows), 0) < iota((rows, rows), 1))
    turn = jnp.sum(jnp.where(twin, 1.0, 0.0), axis=0, keepdims=True).astype(jnp.int32)
    is_far = ra < need_count
    code = jnp.where(is_far, owner * 16 + turn * 8, -1000)
    code2 = jnp.concatenate([code, code + 4], axis=1)

    slot_iota = iota((nr * 16, rows2), 0)
    total = None
    for j in range(4):
        pick = jnp.where(slot_iota == code2 + j, 1.0, 0.0).astype(BF16)
        piece = jnp.dot(
            pick, own[:, j * QUARTER : (j + 1) * QUARTER], preferred_element_type=F32
        )
        total = piece if total is None else total + piece
    msg[...] = total.astype(BF16)
    got[pl.ds(pl.multiple_of(r * 16, 16), 16), :] = jnp.zeros((16, QUARTER), BF16)
    ret_got[pl.ds(pl.multiple_of(r * 8, 8), 8), :] = jnp.zeros((8, HD), F32)

    pl.semaphore_wait(barrier, nr - 1 + nt - 1)

    right = (r, lax.rem(t + 1, nt))
    left = (r, lax.rem(t + nt - 1, nt))
    half = nt // 2

    def hop(which_way, h, c):
        if which_way == 0:
            have, there, to = (nt - (h - 1)) % nt, nt - h, right
        else:
            have, there, to = h - 1, h, left
        piece = pl.ds(c * rows, rows)
        src = f_ref.at[piece, :] if have == 0 else ring.at[have, piece, :]
        return pltpu.make_async_remote_copy(
            src_ref=src,
            dst_ref=ring.at[there, piece, :],
            send_sem=ring_send.at[which_way, h - 1, c],
            recv_sem=ring_recv.at[there, c],
            device_id=to,
            device_id_type=MESH,
        )

    def hops(h):
        if h < half:
            return [(0, 0), (1, 0), (0, 1), (1, 1)]
        return [(0, 0), (1, 1)]

    for way, c in hops(1):
        hop(way, 1, c).start()

    @pl.loop(1, nt)
    def _(k):
        pltpu.make_async_remote_copy(
            src_ref=stats.at[t],
            dst_ref=stats.at[t],
            send_sem=st_send,
            recv_sem=st_recv,
            device_id=(r, lax.rem(t + k, nt)),
            device_id_type=MESH,
        ).start()

    @pl.loop(1, nr)
    def _(k):
        to = lax.rem(r + k, nr)
        pltpu.make_async_remote_copy(
            src_ref=msg.at[pl.ds(pl.multiple_of(to * 16, 16), 16), :],
            dst_ref=got.at[pl.ds(pl.multiple_of(r * 16, 16), 16), :],
            send_sem=a2a_send,
            recv_sem=a2a_recv,
            device_id=(to, t),
            device_id_type=MESH,
        ).start()

    def wait_bytes(ref, sem):
        pltpu.make_async_copy(ref, ref, sem).wait()

    asked = jnp.zeros((adapters, nr), jnp.bool_)
    p_iota = iota((adapters, nr), 0)
    for e in range(need_count):
        asked = asked | (p_iota == need[e : e + 1, :])
    visit = jnp.dot(
        table, jnp.where(asked, 1.0, 0.0).astype(BF16), preferred_element_type=F32
    )[16:24]
    spread = jnp.where(iota((nr, nvis), 1) // 4 == iota((nr, nvis), 0), 1.0, 0.0)
    visit_slot = jnp.dot(
        visit.astype(BF16), spread.astype(BF16), preferred_element_type=F32
    )[0:1].astype(jnp.int32) - 1
    own_slot = jnp.where(is_far, -1, ra - need_count)
    slot_row = jnp.concatenate([visit_slot, own_slot, own_slot], axis=1)

    scale = 1.0 / math.sqrt(HD)
    cache_len = ck.shape[1]
    per_row = 2 * GROUP

    def cached_scores(lo, hi):
        @pl.loop(lo, hi, unroll=4)
        def _(i):
            s = (
                lax.dot_general(q_ref[i], ck[i], NT, preferred_element_type=F32) * scale
            )
            live = iota(s.shape, 1) < len_s[i]
            scores[i] = jnp.where(live, s, NEG)

    def ring_stage(h, which_chunks=(0, 1)):
        for way, c in hops(h):
            if c not in which_chunks:
                continue
            hop(way, h, c).wait_recv()
            if (way, c) in (hops(h + 1) if h < half else []):
                hop(way, h + 1, c).start()

    for load in small[5:]:
        load.wait()
    for step in range(2):
        for g in range(GROUP):
            q_wide[pl.ds(step * GROUP + g, rows, stride=per_row), :] = q_in[
                step * rows : (step + 1) * rows, g * HD : (g + 1) * HD
            ].astype(F32)
    q_ref[...] = q_wide[...].astype(BF16).reshape(rows, per_row, HD)
    loads[0].wait()
    cached_scores(0, rows // 4)
    ring_stage(1, (0,))
    cached_scores(rows // 4, rows // 2)
    ring_stage(1, (1,))

    loads[1].wait()
    wait_bytes(got.at[pl.ds(0, (nr - 1) * 16), :], a2a_recv)
    arrived = got[...]
    for j in range(4):
        gather = iota((nvis, nr * 16), 1) == iota((nvis, nr * 16), 0) * 4 + j
        xall[pl.ds(0, nvis), j * QUARTER : (j + 1) * QUARTER] = jnp.dot(
            jnp.where(gather, 1.0, 0.0).astype(BF16),
            arrived,
            preferred_element_type=F32,
        ).astype(BF16)
    x = xall[...]
    group = 8
    part[...] = jnp.zeros(part.shape, F32)

    @pl.loop(0, pool // group)
    def _(g):
        base = g * group
        block = lax.dot_general(
            pa[pl.ds(pl.multiple_of(base * rank, group * rank), group * rank), :],
            x,
            NT,
            preferred_element_type=F32,
        )
        picked = jnp.zeros((rank, ntot), F32)
        for s in range(group):
            picked += jnp.where(
                slot_row == base + s, block[s * rank : (s + 1) * rank], 0.0
            )
        part[:, :, pl.ds(0, ntot)] += picked.reshape(nt, kpart, ntot)

    @pl.loop(1, nt)
    def _(k):
        to = lax.rem(t + k, nt)
        pltpu.make_async_remote_copy(
            src_ref=part.at[to],
            dst_ref=rs_got.at[t],
            send_sem=rs_send,
            recv_sem=rs_recv,
            device_id=(r, to),
            device_id_type=MESH,
        ).start()

    if half > 2:
        ring_stage(2)

    wait_bytes(stats.at[pl.ds(0, nt - 1)], st_recv)
    square = stats[0, 8:16, :]
    for k in range(1, nt):
        square += stats[k, 8:16, :]
    inverse_row = lax.rsqrt(square[0:1] / (width * nt) + EPS)
    inverse = jnp.sum(jnp.where(eye, inverse_row, 0.0), axis=1, keepdims=True)

    def project(o):
        source = lax.rem(t + o, nt)
        block = f_ref[...] if o == 0 else ring[o]
        block = block.astype(F32) * inverse
        gains = stats[source][0:8]
        normed = jnp.concatenate(
            [
                block[:, c * lanes : (c + 1) * lanes] * gains[c : c + 1]
                for c in range(chunks)
            ],
            axis=1,
        ).astype(BF16)
        w = wbuf[pl.ds(pl.multiple_of(source * width, width), width), :]
        product = jnp.dot(normed, w, preferred_element_type=F32)
        if o == 0:
            acc_kv[...] = product
        else:
            acc_kv[...] += product

    loads[2].wait()
    loads[3].wait()
    project(0)
    project(nt - 1)
    if half > 1:
        project(1)

    wait_bytes(rs_got.at[pl.ds(0, nt - 1)], rs_recv)
    whole = part[t]
    for k in range(nt):
        whole += jnp.where(k == t, 0.0, rs_got[k])
    coeff[t] = whole

    @pl.loop(1, nt)
    def _(k):
        pltpu.make_async_remote_copy(
            src_ref=coeff.at[t],
            dst_ref=coeff.at[t],
            send_sem=ag_send,
            recv_sem=ag_recv,
            device_id=(r, lax.rem(t + k, nt)),
            device_id_type=MESH,
        ).start()

    for h in range(2, half):
        if h > 2:
            ring_stage(h)
        project(nt - h)
        project(h)
    cached_scores(rows // 2, rows)
    loads[4].wait()
    pbt[...] = pb[...].T

    wait_bytes(coeff.at[pl.ds(0, nt - 1)], ag_recv)
    coeffs = coeff[...].reshape(rank, coeff.shape[2])[:, 0:ntot]
    for s in range(pool):
        expand[s * rank : (s + 1) * rank, :] = jnp.where(
            slot_row == s, coeffs, 0.0
        ).astype(BF16)
    delta = jnp.dot(pbt[...], expand[...], preferred_element_type=F32).T
    ret_send[...] = delta[0:nvis]
    own_delta = delta[nvis:ntot]

    @pl.loop(1, nr)
    def _(k):
        to = lax.rem(r + k, nr)
        pltpu.make_async_remote_copy(
            src_ref=ret_send.at[pl.ds(pl.multiple_of(to // 2 * 8, 8), 8), :],
            dst_ref=ret_got.at[pl.ds(pl.multiple_of(r * 8, 8), 8), :],
            send_sem=re_send,
            recv_sem=re_recv,
            device_id=(to, t),
            device_id_type=MESH,
        ).start()

    ring_stage(half)
    project(half)

    length_row = len_ref[...].astype(F32)
    positions = jnp.sum(
        jnp.where(eye_r, length_row, 0.0), axis=1, keepdims=True
    )
    positions = jnp.concatenate([positions, positions + 1.0], axis=0)
    angle = positions * freq_ref[...]
    sign = jnp.where(iota((rows2, HD), 1) < HD // 2, -1.0, 1.0)
    key = acc_kv[:, 0:HD]
    turned = key * jnp.cos(angle) + pltpu.roll(key, HD // 2, 1) * jnp.sin(angle) * sign
    new_keys = turned.astype(BF16)
    nk_ref[...] = new_keys

    qrows = 8
    span = qrows * per_row
    for b in range(rows // qrows):
        s = scores[b * qrows : (b + 1) * qrows].reshape(span, cache_len)
        q = q_ref[b * qrows : (b + 1) * qrows].reshape(span, HD)
        fresh = (
            lax.dot_general(q, new_keys, NT, preferred_element_type=F32) * scale
        )
        row_of = iota(fresh.shape, 0) // per_row + b * qrows
        step_of = iota(fresh.shape, 0) % per_row // GROUP
        column = iota(fresh.shape, 1)
        seen = (column == row_of) | ((column == row_of + rows) & (step_of == 1))
        fresh = jnp.where(seen, fresh, NEG)
        top = jnp.maximum(
            jnp.max(s, axis=1, keepdims=True), jnp.max(fresh, axis=1, keepdims=True)
        )
        e_cache = jnp.exp(s - top)
        e_fresh = jnp.exp(fresh - top)
        bottom = jnp.sum(e_cache, axis=1, keepdims=True) + jnp.sum(
            e_fresh, axis=1, keepdims=True
        )
        weights[b * qrows : (b + 1) * qrows] = (
            (e_cache / bottom).astype(BF16).reshape(qrows, per_row, cache_len)
        )
        fresh_w[b * span : (b + 1) * span, :] = (e_fresh / bottom).astype(BF16)

    loads[5].wait()

    @pl.loop(0, rows, unroll=4)
    def _(i):
        att_acc[pl.ds(pl.multiple_of(i * per_row, per_row), per_row), :] = jnp.dot(weights[i], cv[i], preferred_element_type=F32)

    code_f = jnp.where(
        is_far, owner * 8 + lax.rem(r, 2) * 4 + turn * 2, -1000
    ).astype(F32)
    code_col = jnp.sum(jnp.where(eye_r, code_f, 0.0), axis=1, keepdims=True)
    code_col = jnp.concatenate([code_col, code_col + 1.0], axis=0).astype(jnp.int32)
    back = jnp.where(iota((rows2, nr * 8), 1) == code_col, 1.0, 0.0).astype(BF16)
    wait_bytes(ret_got.at[pl.ds(0, (nr - 1) * 8), :], re_recv)
    returned = ret_got[...]
    high = returned.astype(BF16)
    low = (returned - high.astype(F32)).astype(BF16)
    far_delta = jnp.dot(back, high, preferred_element_type=F32) + jnp.dot(
        back, low, preferred_element_type=F32
    )
    new_values = (acc_kv[:, HD : 2 * HD] + inverse * (far_delta + own_delta)).astype(
        BF16
    )
    nv_ref[...] = new_values
    att_acc[...] += jnp.dot(fresh_w[...], new_values, preferred_element_type=F32)
    for step in range(2):
        for g in range(GROUP):
            att_ref[step * rows : (step + 1) * rows, g * HD : (g + 1) * HD] = att_acc[
                pl.ds(step * GROUP + g, rows, stride=per_row), :
            ].astype(BF16)

    for h in range(1, half + 1):
        for way, c in hops(h):
            hop(way, h, c).wait_send()
    wait_bytes(stats.at[pl.ds(0, nt - 1)], st_send)
    wait_bytes(msg.at[pl.ds(0, (nr - 1) * 16), :], a2a_send)
    wait_bytes(part.at[pl.ds(0, nt - 1)], rs_send)
    wait_bytes(coeff.at[pl.ds(0, nt - 1)], ag_send)
    wait_bytes(ret_got.at[pl.ds(0, (nr - 1) * 8), :], re_send)


def write_out(a, b, c, a_out, b_out, c_out, sem):
    copies = [
        pltpu.make_async_copy(src, dst, sem.at[k])
        for k, (src, dst) in enumerate([(a, a_out), (b, b_out), (c, c_out)])
    ]
    for copy in copies:
        copy.start()
    for copy in copies:
        copy.wait()


def shards(
    features,
    gain,
    w_key,
    w_value,
    pool_a,
    pool_b,
    placement,
    need_lists,
    row_adapter,
    lengths,
    queries,
    cache_k,
    cache_v,
):
    nr, nt = lax.axis_size("replica"), lax.axis_size("tp")
    steps, rows, width = features.shape
    pool, _, rank = pool_a.shape
    cache_len = cache_k.shape[1]
    rows2 = steps * rows
    nvis = nr * 4
    ntot = nvis + rows2
    ntot_pad = -(-ntot // HD) * HD
    per_row = steps * GROUP
    half = HD // 2
    frequency = np.float32(THETA) ** (-(np.arange(half, dtype=np.float32) * 2.0) / HD)
    frequency = np.concatenate([frequency, frequency]).astype(np.float32)[None, :]
    vmem = pl.BlockSpec(memory_space=pltpu.VMEM)
    hbm = pl.BlockSpec(memory_space=pltpu.HBM)
    dma = pltpu.SemaphoreType.DMA
    att, nk, nv = pl.pallas_call(
        functools.partial(kernel, nr, nt),
        out_shape=(
            jax.ShapeDtypeStruct((rows2, width), BF16),
            jax.ShapeDtypeStruct((rows2, HD), BF16),
            jax.ShapeDtypeStruct((rows2, HD), BF16),
        ),
        in_specs=[hbm] * 15,
        out_specs=(vmem, vmem, vmem),
        scratch_shapes=[
            pltpu.VMEM((rows2, width), BF16),
            pltpu.VMEM((width // HD, HD), BF16),
            pltpu.VMEM((1, placement.shape[0]), jnp.int32),
            pltpu.VMEM(need_lists.shape[::-1], jnp.int32),
            pltpu.VMEM((1, rows), jnp.int32),
            pltpu.SMEM((rows,), jnp.int32),
            pltpu.VMEM((1, rows), jnp.int32),
            pltpu.VMEM((1, HD), F32),
            pltpu.VMEM((rows2, width), BF16),
            pltpu.VMEM((rows * per_row, HD), F32),
            pltpu.VMEM((rows, per_row, HD), BF16),
            pltpu.VMEM((nt * width, 2 * HD), BF16),
            pltpu.VMEM((pool * rank, width), BF16),
            pltpu.VMEM((pool * rank, HD), BF16),
            pltpu.VMEM((HD, pool * rank), BF16),
            pltpu.VMEM((rows, cache_len, HD), BF16),
            pltpu.VMEM((rows, cache_len, HD), BF16),
            pltpu.VMEM((nt, 16, HD), F32),
            pltpu.VMEM((nr * 16, QUARTER), BF16),
            pltpu.VMEM((nr * 16, QUARTER), BF16),
            pltpu.VMEM((ntot, width), BF16),
            pltpu.VMEM((nt, rows2, width), BF16),
            pltpu.VMEM((nt, rank // nt, ntot_pad), F32),
            pltpu.VMEM((nt, rank // nt, ntot_pad), F32),
            pltpu.VMEM((nt, rank // nt, ntot_pad), F32),
            pltpu.VMEM((pool * rank, ntot), BF16),
            pltpu.VMEM((nvis, HD), F32),
            pltpu.VMEM((nr * 8, HD), F32),
            pltpu.VMEM((rows, per_row, cache_len), F32),
            pltpu.VMEM((rows, per_row, cache_len), BF16),
            pltpu.VMEM((rows * per_row, rows2), BF16),
            pltpu.VMEM((rows2, 2 * HD), F32),
            pltpu.VMEM((rows * per_row, HD), F32),
            dma((9,)),
            dma((6,)),
            dma,
            dma,
            dma,
            dma,
            dma((2, max(nt // 2, 1), 2)),
            dma((nt, 2)),
            dma,
            dma,
            dma,
            dma,
            dma,
            dma,
        ],
        compiler_params=pltpu.CompilerParams(
            collective_id=0, has_side_effects=True, vmem_limit_bytes=60 * 2**20
        ),
        cost_estimate=pl.CostEstimate(
            flops=2 * 64 * 8192 * 256, bytes_accessed=12 * 2**20, transcendentals=0
        ),
    )(
        features.reshape(rows2, width),
        gain.reshape(width // HD, HD),
        placement.reshape(1, -1),
        need_lists.T,
        row_adapter.reshape(1, rows),
        lengths,
        lengths.reshape(1, rows),
        jnp.asarray(frequency),
        queries.reshape(rows2, width),
        w_key,
        w_value,
        pool_a.swapaxes(1, 2).reshape(pool * rank, width),
        pool_b.reshape(pool * rank, HD),
        cache_k,
        cache_v,
    )
    shapes = tuple(jax.ShapeDtypeStruct(x.shape, BF16) for x in (att, nk, nv))
    att, nk, nv = pl.pallas_call(
        write_out,
        out_shape=shapes,
        in_specs=[hbm] * 3,
        out_specs=(hbm,) * 3,
        scratch_shapes=[dma((3,))],
    )(att, nk, nv)
    return (
        att.reshape(steps, rows, width),
        nk.reshape(steps, rows, HD),
        nv.reshape(steps, rows, HD),
    )


def solution(mesh):
    placed = (
        P(None, "replica", "tp"),
        P("tp"),
        P(None, "tp"),
        P(None, "tp"),
        P("replica", "tp", None),
        P("replica", None, "tp"),
        P(),
        P(),
        P("replica"),
        P("replica"),
        P(None, "replica", "tp"),
        P("replica", None, "tp"),
        P("replica", None, "tp"),
    )
    return jax.shard_map(
        shards,
        mesh=mesh,
        in_specs=placed,
        out_specs=(P(None, "replica", "tp"), P(None, "replica", "tp"), P(None, "replica", "tp")),
        check_vma=False,
    )
```

```python
import functools
import math

import jax
import jax.numpy as jnp
import numpy as np
from jax import lax
from jax.experimental import pallas as pl
from jax.experimental.pallas import tpu as pltpu
from jax.sharding import PartitionSpec as P

HD = 128
GROUP = 8
EPS = 1e-05
THETA = 500000.0
NEG = -1e30
MESH = pl.DeviceIdType.MESH
F32 = jnp.float32
BF16 = jnp.bfloat16
QUARTER = 256
NT = (((1,), (1,)), ((), ()))


def iota(shape, dim):
    return lax.broadcasted_iota(jnp.int32, shape, dim)


def kernel(
    nr,
    nt,
    f_hbm,
    gain_hbm,
    place_hbm,
    need_hbm,
    ra_hbm,
    len_s_hbm,
    len_hbm,
    freq_hbm,
    q_hbm,
    wk_hbm,
    wv_hbm,
    pa_hbm,
    pb_hbm,
    ck_hbm,
    cv_hbm,
    att_ref,
    nk_ref,
    nv_ref,
    f_ref,
    gain_ref,
    place_ref,
    need_ref,
    ra_ref,
    len_s,
    len_ref,
    freq_ref,
    q_in,
    q_wide,
    q_ref,
    wbuf,
    pa,
    pb,
    pbt,
    ck,
    cv,
    stats,
    msg,
    got,
    xall,
    ring,
    part,
    rs_got,
    coeff,
    expand,
    ret_send,
    ret_got,
    scores,
    weights,
    fresh_w,
    acc_kv,
    att_acc,
    top_ref,
    bottom_ref,
    cos_ref,
    sin_ref,
    small_sem,
    load_sem,
    st_send,
    st_recv,
    a2a_send,
    a2a_recv,
    ring_send,
    ring_recv,
    rs_send,
    rs_recv,
    ag_send,
    ag_recv,
    re_send,
    re_recv,
):
    r = lax.axis_index("replica")
    t = lax.axis_index("tp")
    rows2, width = f_ref.shape
    rows = rows2 // 2
    need_count = need_ref.shape[0]
    adapters = place_ref.shape[1]
    pool = adapters // nr
    rank = part.shape[1] * nt
    kpart = rank // nt
    nvis = nr * 4
    ntot = nvis + rows2

    small = [
        pltpu.make_async_copy(a, b, small_sem.at[k])
        for k, (a, b) in enumerate(
            [
                (f_hbm, f_ref),
                (gain_hbm, gain_ref),
                (ra_hbm, ra_ref),
                (need_hbm, need_ref),
                (place_hbm, place_ref),
                (len_s_hbm, len_s),
                (len_hbm, len_ref),
                (freq_hbm, freq_ref),
                (q_hbm, q_in),
            ]
        )
    ]
    loads = [
        pltpu.make_async_copy(ck_hbm, ck, load_sem.at[0]),
        pltpu.make_async_copy(pa_hbm, pa, load_sem.at[1]),
        pltpu.make_async_copy(wk_hbm, wbuf.at[:, pl.ds(0, HD)], load_sem.at[2]),
        pltpu.make_async_copy(wv_hbm, wbuf.at[:, pl.ds(HD, HD)], load_sem.at[3]),
        pltpu.make_async_copy(pb_hbm, pb, load_sem.at[4]),
        pltpu.make_async_copy(cv_hbm, cv, load_sem.at[5]),
    ]
    for load in small + loads:
        load.start()

    barrier = pltpu.get_barrier_semaphore()

    @pl.loop(1, nr)
    def _(k):
        pl.semaphore_signal(
            barrier, inc=1, device_id=(lax.rem(r + k, nr), t), device_id_type=MESH
        )

    @pl.loop(1, nt)
    def _(k):
        pl.semaphore_signal(
            barrier, inc=1, device_id=(r, lax.rem(t + k, nt)), device_id_type=MESH
        )

    small[0].wait()
    small[1].wait()
    gain_rows = gain_ref[...].astype(F32)
    f32 = f_ref[...].astype(F32)
    lanes = HD
    chunks = width // lanes
    eye = iota((rows2, lanes), 0) == iota((rows2, lanes), 1)
    square_sum = jnp.sum(f32 * f32, axis=1, keepdims=True)
    square_row = jnp.sum(jnp.where(eye, square_sum, 0.0), axis=0, keepdims=True)
    stats[t] = jnp.concatenate(
        [gain_rows, jnp.broadcast_to(square_row, (8, lanes))], axis=0
    )
    own = jnp.concatenate(
        [
            f32[:, c * lanes : (c + 1) * lanes] * gain_rows[c : c + 1]
            for c in range(chunks)
        ],
        axis=1,
    ).astype(BF16)
    xall[pl.ds(nvis, rows2), :] = own

    for load in small[2:5]:
        load.wait()
    ra = ra_ref[...]
    need = need_ref[...]
    mine = jnp.sum(
        jnp.where(iota(need.shape, 1) == r, need, 0).astype(F32), axis=1, keepdims=True
    )
    entry = iota((need_count, rows), 0) == ra
    wanted = jnp.sum(jnp.where(entry, mine, 0.0), axis=0, keepdims=True)
    place = place_ref[...]
    home = place // pool
    local = place - home * pool
    at_me = jnp.where(home == r, local + 1, 0)
    table = jnp.concatenate(
        [
            jnp.broadcast_to(x.astype(F32), (8, adapters))
            for x in (home, local, at_me)
        ],
        axis=0,
    ).astype(BF16)
    which = iota((adapters, rows), 0) == wanted.astype(jnp.int32)
    found = jnp.dot(
        table, jnp.where(which, 1.0, 0.0).astype(BF16), preferred_element_type=F32
    )
    owner = found[0:1].astype(jnp.int32)
    eye_r = iota((rows, rows), 0) == iota((rows, rows), 1)
    ra_f = ra.astype(F32)
    ra_col = jnp.sum(jnp.where(eye_r, ra_f, 0.0), axis=1, keepdims=True)
    twin = (ra_col == ra_f) & (iota((rows, rows), 0) < iota((rows, rows), 1))
    turn = jnp.sum(jnp.where(twin, 1.0, 0.0), axis=0, keepdims=True).astype(jnp.int32)
    is_far = ra < need_count
    code = jnp.where(is_far, owner * 16 + turn * 8, -1000)
    code2 = jnp.concatenate([code, code + 4], axis=1)

    slot_iota = iota((nr * 16, rows2), 0)
    total = None
    for j in range(4):
        pick = jnp.where(slot_iota == code2 + j, 1.0, 0.0).astype(BF16)
        piece = jnp.dot(
            pick, own[:, j * QUARTER : (j + 1) * QUARTER], preferred_element_type=F32
        )
        total = piece if total is None else total + piece
    msg[...] = total.astype(BF16)
    got[pl.ds(pl.multiple_of(r * 16, 16), 16), :] = jnp.zeros((16, QUARTER), BF16)
    ret_got[pl.ds(pl.multiple_of(r * 8, 8), 8), :] = jnp.zeros((8, HD), F32)

    pl.semaphore_wait(barrier, nr - 1 + nt - 1)

    right = (r, lax.rem(t + 1, nt))
    left = (r, lax.rem(t + nt - 1, nt))
    half = nt // 2

    def hop(which_way, h, c):
        if which_way == 0:
            have, there, to = (nt - (h - 1)) % nt, nt - h, right
        else:
            have, there, to = h - 1, h, left
        piece = pl.ds(c * rows, rows)
        src = f_ref.at[piece, :] if have == 0 else ring.at[have, piece, :]
        return pltpu.make_async_remote_copy(
            src_ref=src,
            dst_ref=ring.at[there, piece, :],
            send_sem=ring_send.at[which_way, h - 1, c],
            recv_sem=ring_recv.at[there, c],
            device_id=to,
            device_id_type=MESH,
        )

    def hops(h):
        if h < half:
            return [(0, 0), (1, 0), (0, 1), (1, 1)]
        return [(0, 0), (1, 1)]

    for way, c in hops(1):
        hop(way, 1, c).start()

    @pl.loop(1, nt)
    def _(k):
        pltpu.make_async_remote_copy(
            src_ref=stats.at[t],
            dst_ref=stats.at[t],
            send_sem=st_send,
            recv_sem=st_recv,
            device_id=(r, lax.rem(t + k, nt)),
            device_id_type=MESH,
        ).start()

    @pl.loop(1, nr)
    def _(k):
        to = lax.rem(r + k, nr)
        pltpu.make_async_remote_copy(
            src_ref=msg.at[pl.ds(pl.multiple_of(to * 16, 16), 16), :],
            dst_ref=got.at[pl.ds(pl.multiple_of(r * 16, 16), 16), :],
            send_sem=a2a_send,
            recv_sem=a2a_recv,
            device_id=(to, t),
            device_id_type=MESH,
        ).start()

    def wait_bytes(ref, sem):
        pltpu.make_async_copy(ref, ref, sem).wait()

    asked = jnp.zeros((adapters, nr), jnp.bool_)
    p_iota = iota((adapters, nr), 0)
    for e in range(need_count):
        asked = asked | (p_iota == need[e : e + 1, :])
    visit = jnp.dot(
        table, jnp.where(asked, 1.0, 0.0).astype(BF16), preferred_element_type=F32
    )[16:24]
    spread = jnp.where(iota((nr, nvis), 1) // 4 == iota((nr, nvis), 0), 1.0, 0.0)
    visit_slot = jnp.dot(
        visit.astype(BF16), spread.astype(BF16), preferred_element_type=F32
    )[0:1].astype(jnp.int32) - 1
    own_slot = jnp.where(is_far, -1, ra - need_count)
    slot_row = jnp.concatenate([visit_slot, own_slot, own_slot], axis=1)

    scale = 1.0 / math.sqrt(HD)
    cache_len = ck.shape[1]
    per_row = 2 * GROUP

    def cached_scores(lo, hi):
        @pl.loop(lo, hi, unroll=4)
        def _(i):
            s = (
                lax.dot_general(q_ref[i], ck[i], NT, preferred_element_type=F32) * scale
            )
            live = iota(s.shape, 1) < len_s[i]
            scores[i] = jnp.where(live, s, NEG)

    def ring_stage(h, which_chunks=(0, 1)):
        for way, c in hops(h):
            if c not in which_chunks:
                continue
            hop(way, h, c).wait_recv()
            if (way, c) in (hops(h + 1) if h < half else []):
                hop(way, h + 1, c).start()

    for load in small[5:]:
        load.wait()
    for step in range(2):
        for g in range(GROUP):
            q_wide[pl.ds(step * GROUP + g, rows, stride=per_row), :] = q_in[
                step * rows : (step + 1) * rows, g * HD : (g + 1) * HD
            ].astype(F32)
    q_ref[...] = q_wide[...].astype(BF16).reshape(rows, per_row, HD)
    loads[0].wait()
    cached_scores(0, rows // 4)
    ring_stage(1, (0,))
    cached_scores(rows // 4, rows)
    ring_stage(1, (1,))

    loads[1].wait()
    wait_bytes(got.at[pl.ds(0, (nr - 1) * 16), :], a2a_recv)
    arrived = got[...]
    for j in range(4):
        gather = iota((nvis, nr * 16), 1) == iota((nvis, nr * 16), 0) * 4 + j
        xall[pl.ds(0, nvis), j * QUARTER : (j + 1) * QUARTER] = jnp.dot(
            jnp.where(gather, 1.0, 0.0).astype(BF16),
            arrived,
            preferred_element_type=F32,
        ).astype(BF16)
    x = xall[...]
    group = 8
    part[...] = jnp.zeros(part.shape, F32)

    @pl.loop(0, pool // group)
    def _(g):
        base = g * group
        block = lax.dot_general(
            pa[pl.ds(pl.multiple_of(base * rank, group * rank), group * rank), :],
            x,
            NT,
            preferred_element_type=F32,
        )
        picked = jnp.zeros((rank, ntot), F32)
        for s in range(group):
            picked += jnp.where(
                slot_row == base + s, block[s * rank : (s + 1) * rank], 0.0
            )
        part[:, :, pl.ds(0, ntot)] += picked.reshape(nt, kpart, ntot)

    @pl.loop(1, nt)
    def _(k):
        to = lax.rem(t + k, nt)
        pltpu.make_async_remote_copy(
            src_ref=part.at[to],
            dst_ref=rs_got.at[t],
            send_sem=rs_send,
            recv_sem=rs_recv,
            device_id=(r, to),
            device_id_type=MESH,
        ).start()

    if half > 2:
        ring_stage(2)

    qrows = 8
    span = qrows * per_row
    for b in range(rows // qrows):
        s = scores[b * qrows : (b + 1) * qrows].reshape(span, cache_len)
        top = jnp.max(s, axis=1, keepdims=True)
        e_cache = jnp.exp(s - top)
        top_ref[b * span : (b + 1) * span, :] = top
        bottom_ref[b * span : (b + 1) * span, :] = jnp.sum(
            e_cache, axis=1, keepdims=True
        )
        weights[b * qrows : (b + 1) * qrows] = e_cache.astype(BF16).reshape(
            qrows, per_row, cache_len
        )

    wait_bytes(stats.at[pl.ds(0, nt - 1)], st_recv)
    square = stats[0, 8:16, :]
    for k in range(1, nt):
        square += stats[k, 8:16, :]
    inverse_row = lax.rsqrt(square[0:1] / (width * nt) + EPS)
    inverse = jnp.sum(jnp.where(eye, inverse_row, 0.0), axis=1, keepdims=True)

    def project(o):
        source = lax.rem(t + o, nt)
        block = f_ref[...] if o == 0 else ring[o]
        block = block.astype(F32) * inverse
        gains = stats[source][0:8]
        normed = jnp.concatenate(
            [
                block[:, c * lanes : (c + 1) * lanes] * gains[c : c + 1]
                for c in range(chunks)
            ],
            axis=1,
        ).astype(BF16)
        w = wbuf[pl.ds(pl.multiple_of(source * width, width), width), :]
        product = jnp.dot(normed, w, preferred_element_type=F32)
        if o == 0:
            acc_kv[...] = product
        else:
            acc_kv[...] += product

    loads[2].wait()
    loads[3].wait()
    project(0)
    project(nt - 1)
    if half > 1:
        project(1)

    length_row = len_ref[...].astype(F32)
    positions = jnp.sum(
        jnp.where(eye_r, length_row, 0.0), axis=1, keepdims=True
    )
    positions = jnp.concatenate([positions, positions + 1.0], axis=0)
    angle = positions * freq_ref[...]
    sign = jnp.where(iota((rows2, HD), 1) < HD // 2, -1.0, 1.0)
    cos_ref[...] = jnp.cos(angle)
    sin_ref[...] = jnp.sin(angle) * sign

    wait_bytes(rs_got.at[pl.ds(0, nt - 1)], rs_recv)
    whole = part[t]
    for k in range(nt):
        whole += jnp.where(k == t, 0.0, rs_got[k])
    coeff[t] = whole

    @pl.loop(1, nt)
    def _(k):
        pltpu.make_async_remote_copy(
            src_ref=coeff.at[t],
            dst_ref=coeff.at[t],
            send_sem=ag_send,
            recv_sem=ag_recv,
            device_id=(r, lax.rem(t + k, nt)),
            device_id_type=MESH,
        ).start()

    for h in range(3, half):
        ring_stage(h)
        project(nt - h + 1)
        project(h - 1)

    loads[5].wait()

    @pl.loop(0, rows, unroll=4)
    def _(i):
        att_acc[pl.ds(pl.multiple_of(i * per_row, per_row), per_row), :] = jnp.dot(
            weights[i], cv[i], preferred_element_type=F32
        )

    loads[4].wait()
    pbt[...] = pb[...].T

    wait_bytes(coeff.at[pl.ds(0, nt - 1)], ag_recv)
    coeffs = coeff[...].reshape(rank, coeff.shape[2])[:, 0:ntot]
    for s in range(pool):
        expand[s * rank : (s + 1) * rank, :] = jnp.where(
            slot_row == s, coeffs, 0.0
        ).astype(BF16)
    delta = jnp.dot(pbt[...], expand[...], preferred_element_type=F32).T
    ret_send[...] = delta[0:nvis]
    own_delta = delta[nvis:ntot]

    @pl.loop(1, nr)
    def _(k):
        to = lax.rem(r + k, nr)
        pltpu.make_async_remote_copy(
            src_ref=ret_send.at[pl.ds(pl.multiple_of(to // 2 * 8, 8), 8), :],
            dst_ref=ret_got.at[pl.ds(pl.multiple_of(r * 8, 8), 8), :],
            send_sem=re_send,
            recv_sem=re_recv,
            device_id=(to, t),
            device_id_type=MESH,
        ).start()

    if half > 2:
        project(nt - half + 1)
        project(half - 1)
    ring_stage(half)
    project(half)

    key = acc_kv[:, 0:HD]
    turned = key * cos_ref[...] + pltpu.roll(key, HD // 2, 1) * sin_ref[...]
    new_keys = turned.astype(BF16)
    nk_ref[...] = new_keys

    for b in range(rows // qrows):
        part_rows = slice(b * span, (b + 1) * span)
        q = q_ref[b * qrows : (b + 1) * qrows].reshape(span, HD)
        fresh = (
            lax.dot_general(q, new_keys, NT, preferred_element_type=F32) * scale
        )
        row_of = iota(fresh.shape, 0) // per_row + b * qrows
        step_of = iota(fresh.shape, 0) % per_row // GROUP
        column = iota(fresh.shape, 1)
        seen = (column == row_of) | ((column == row_of + rows) & (step_of == 1))
        fresh = jnp.where(seen, fresh, NEG)
        cache_top = top_ref[part_rows, :]
        top = jnp.maximum(cache_top, jnp.max(fresh, axis=1, keepdims=True))
        shrink = jnp.exp(cache_top - top)
        e_fresh = jnp.exp(fresh - top)
        bottom = bottom_ref[part_rows, :] * shrink + jnp.sum(
            e_fresh, axis=1, keepdims=True
        )
        share = 1.0 / bottom
        fresh_w[part_rows, :] = (e_fresh * share).astype(BF16)
        att_acc[part_rows, :] = att_acc[part_rows, :] * (shrink * share)

    code_f = jnp.where(
        is_far, owner * 8 + lax.rem(r, 2) * 4 + turn * 2, -1000
    ).astype(F32)
    code_col = jnp.sum(jnp.where(eye_r, code_f, 0.0), axis=1, keepdims=True)
    code_col = jnp.concatenate([code_col, code_col + 1.0], axis=0).astype(jnp.int32)
    back = jnp.where(iota((rows2, nr * 8), 1) == code_col, 1.0, 0.0).astype(BF16)
    wait_bytes(ret_got.at[pl.ds(0, (nr - 1) * 8), :], re_recv)
    returned = ret_got[...]
    high = returned.astype(BF16)
    low = (returned - high.astype(F32)).astype(BF16)
    far_delta = jnp.dot(back, high, preferred_element_type=F32) + jnp.dot(
        back, low, preferred_element_type=F32
    )
    new_values = (acc_kv[:, HD : 2 * HD] + inverse * (far_delta + own_delta)).astype(
        BF16
    )
    nv_ref[...] = new_values
    att_acc[...] += jnp.dot(fresh_w[...], new_values, preferred_element_type=F32)
    for step in range(2):
        for g in range(GROUP):
            att_ref[step * rows : (step + 1) * rows, g * HD : (g + 1) * HD] = att_acc[
                pl.ds(step * GROUP + g, rows, stride=per_row), :
            ].astype(BF16)

    for h in range(1, half + 1):
        for way, c in hops(h):
            hop(way, h, c).wait_send()
    wait_bytes(stats.at[pl.ds(0, nt - 1)], st_send)
    wait_bytes(msg.at[pl.ds(0, (nr - 1) * 16), :], a2a_send)
    wait_bytes(part.at[pl.ds(0, nt - 1)], rs_send)
    wait_bytes(coeff.at[pl.ds(0, nt - 1)], ag_send)
    wait_bytes(ret_got.at[pl.ds(0, (nr - 1) * 8), :], re_send)


def write_out(a, b, c, a_out, b_out, c_out, sem):
    copies = [
        pltpu.make_async_copy(src, dst, sem.at[k])
        for k, (src, dst) in enumerate([(a, a_out), (b, b_out), (c, c_out)])
    ]
    for copy in copies:
        copy.start()
    for copy in copies:
        copy.wait()


def shards(
    features,
    gain,
    w_key,
    w_value,
    pool_a,
    pool_b,
    placement,
    need_lists,
    row_adapter,
    lengths,
    queries,
    cache_k,
    cache_v,
):
    nr, nt = lax.axis_size("replica"), lax.axis_size("tp")
    steps, rows, width = features.shape
    pool, _, rank = pool_a.shape
    cache_len = cache_k.shape[1]
    rows2 = steps * rows
    nvis = nr * 4
    ntot = nvis + rows2
    ntot_pad = -(-ntot // HD) * HD
    per_row = steps * GROUP
    half = HD // 2
    frequency = np.float32(THETA) ** (-(np.arange(half, dtype=np.float32) * 2.0) / HD)
    frequency = np.concatenate([frequency, frequency]).astype(np.float32)[None, :]
    vmem = pl.BlockSpec(memory_space=pltpu.VMEM)
    hbm = pl.BlockSpec(memory_space=pltpu.HBM)
    dma = pltpu.SemaphoreType.DMA
    att, nk, nv = pl.pallas_call(
        functools.partial(kernel, nr, nt),
        out_shape=(
            jax.ShapeDtypeStruct((rows2, width), BF16),
            jax.ShapeDtypeStruct((rows2, HD), BF16),
            jax.ShapeDtypeStruct((rows2, HD), BF16),
        ),
        in_specs=[hbm] * 15,
        out_specs=(vmem, vmem, vmem),
        scratch_shapes=[
            pltpu.VMEM((rows2, width), BF16),
            pltpu.VMEM((width // HD, HD), BF16),
            pltpu.VMEM((1, placement.shape[0]), jnp.int32),
            pltpu.VMEM(need_lists.shape[::-1], jnp.int32),
            pltpu.VMEM((1, rows), jnp.int32),
            pltpu.SMEM((rows,), jnp.int32),
            pltpu.VMEM((1, rows), jnp.int32),
            pltpu.VMEM((1, HD), F32),
            pltpu.VMEM((rows2, width), BF16),
            pltpu.VMEM((rows * per_row, HD), F32),
            pltpu.VMEM((rows, per_row, HD), BF16),
            pltpu.VMEM((nt * width, 2 * HD), BF16),
            pltpu.VMEM((pool * rank, width), BF16),
            pltpu.VMEM((pool * rank, HD), BF16),
            pltpu.VMEM((HD, pool * rank), BF16),
            pltpu.VMEM((rows, cache_len, HD), BF16),
            pltpu.VMEM((rows, cache_len, HD), BF16),
            pltpu.VMEM((nt, 16, HD), F32),
            pltpu.VMEM((nr * 16, QUARTER), BF16),
            pltpu.VMEM((nr * 16, QUARTER), BF16),
            pltpu.VMEM((ntot, width), BF16),
            pltpu.VMEM((nt, rows2, width), BF16),
            pltpu.VMEM((nt, rank // nt, ntot_pad), F32),
            pltpu.VMEM((nt, rank // nt, ntot_pad), F32),
            pltpu.VMEM((nt, rank // nt, ntot_pad), F32),
            pltpu.VMEM((pool * rank, ntot), BF16),
            pltpu.VMEM((nvis, HD), F32),
            pltpu.VMEM((nr * 8, HD), F32),
            pltpu.VMEM((rows, per_row, cache_len), F32),
            pltpu.VMEM((rows, per_row, cache_len), BF16),
            pltpu.VMEM((rows * per_row, rows2), BF16),
            pltpu.VMEM((rows2, 2 * HD), F32),
            pltpu.VMEM((rows * per_row, HD), F32),
            pltpu.VMEM((rows * per_row, 1), F32),
            pltpu.VMEM((rows * per_row, 1), F32),
            pltpu.VMEM((rows2, HD), F32),
            pltpu.VMEM((rows2, HD), F32),
            dma((9,)),
            dma((6,)),
            dma,
            dma,
            dma,
            dma,
            dma((2, max(nt // 2, 1), 2)),
            dma((nt, 2)),
            dma,
            dma,
            dma,
            dma,
            dma,
            dma,
        ],
        compiler_params=pltpu.CompilerParams(
            collective_id=0, has_side_effects=True, vmem_limit_bytes=60 * 2**20
        ),
        cost_estimate=pl.CostEstimate(
            flops=2 * 64 * 8192 * 256, bytes_accessed=12 * 2**20, transcendentals=0
        ),
    )(
        features.reshape(rows2, width),
        gain.reshape(width // HD, HD),
        placement.reshape(1, -1),
        need_lists.T,
        row_adapter.reshape(1, rows),
        lengths,
        lengths.reshape(1, rows),
        jnp.asarray(frequency),
        queries.reshape(rows2, width),
        w_key,
        w_value,
        pool_a.swapaxes(1, 2).reshape(pool * rank, width),
        pool_b.reshape(pool * rank, HD),
        cache_k,
        cache_v,
    )
    shapes = tuple(jax.ShapeDtypeStruct(x.shape, BF16) for x in (att, nk, nv))
    att, nk, nv = pl.pallas_call(
        write_out,
        out_shape=shapes,
        in_specs=[vmem] * 3,
        out_specs=(hbm,) * 3,
        scratch_shapes=[dma((3,))],
        compiler_params=pltpu.CompilerParams(vmem_limit_bytes=60 * 2**20),
    )(att, nk, nv)
    return (
        att.reshape(steps, rows, width),
        nk.reshape(steps, rows, HD),
        nv.reshape(steps, rows, HD),
    )


def solution(mesh):
    placed = (
        P(None, "replica", "tp"),
        P("tp"),
        P(None, "tp"),
        P(None, "tp"),
        P("replica", "tp", None),
        P("replica", None, "tp"),
        P(),
        P(),
        P("replica"),
        P("replica"),
        P(None, "replica", "tp"),
        P("replica", None, "tp"),
        P("replica", None, "tp"),
    )
    return jax.shard_map(
        shards,
        mesh=mesh,
        in_specs=placed,
        out_specs=(P(None, "replica", "tp"), P(None, "replica", "tp"), P(None, "replica", "tp")),
        check_vma=False,
    )
```

```python
import functools
import math

import jax
import jax.numpy as jnp
import numpy as np
from jax import lax
from jax.experimental import pallas as pl
from jax.experimental.pallas import tpu as pltpu
from jax.sharding import PartitionSpec as P

HD = 128
GROUP = 8
EPS = 1e-05
THETA = 500000.0
NEG = -1e30
MESH = pl.DeviceIdType.MESH
F32 = jnp.float32
BF16 = jnp.bfloat16
QUARTER = 256
NT = (((1,), (1,)), ((), ()))


def iota(shape, dim):
    return lax.broadcasted_iota(jnp.int32, shape, dim)


def kernel(
    nr,
    nt,
    f_hbm,
    gain_hbm,
    place_hbm,
    need_hbm,
    ra_hbm,
    len_s_hbm,
    len_hbm,
    freq_hbm,
    q_hbm,
    wk_hbm,
    wv_hbm,
    pa_hbm,
    pb_hbm,
    ck_hbm,
    cv_hbm,
    att_ref,
    nk_ref,
    nv_ref,
    f_ref,
    gain_ref,
    place_ref,
    need_ref,
    ra_ref,
    len_s,
    len_ref,
    freq_ref,
    q_in,
    q_wide,
    q_ref,
    wbuf,
    pa,
    pb,
    pbt,
    ck,
    cv,
    stats,
    msg,
    got,
    xall,
    ring,
    part,
    rs_got,
    coeff,
    expand,
    ret_send,
    ret_got,
    scores,
    weights,
    fresh_w,
    acc_kv,
    att_acc,
    top_ref,
    bottom_ref,
    cos_ref,
    sin_ref,
    small_sem,
    load_sem,
    st_send,
    st_recv,
    a2a_send,
    a2a_recv,
    ring_send,
    ring_recv,
    rs_send,
    rs_recv,
    ag_send,
    ag_recv,
    re_send,
    re_recv,
):
    r = lax.axis_index("replica")
    t = lax.axis_index("tp")
    rows2, width = f_ref.shape
    rows = rows2 // 2
    need_count = need_ref.shape[0]
    adapters = place_ref.shape[1]
    pool = adapters // nr
    rank = part.shape[1] * nt
    kpart = rank // nt
    nvis = nr * 4
    ntot = nvis + rows2

    small = [
        pltpu.make_async_copy(a, b, small_sem.at[k])
        for k, (a, b) in enumerate(
            [
                (f_hbm, f_ref),
                (gain_hbm, gain_ref),
                (ra_hbm, ra_ref),
                (need_hbm, need_ref),
                (place_hbm, place_ref),
                (len_s_hbm, len_s),
                (len_hbm, len_ref),
                (freq_hbm, freq_ref),
                (q_hbm, q_in),
            ]
        )
    ]
    loads = [
        pltpu.make_async_copy(ck_hbm, ck, load_sem.at[0]),
        pltpu.make_async_copy(pa_hbm, pa, load_sem.at[1]),
        pltpu.make_async_copy(wk_hbm, wbuf.at[:, pl.ds(0, HD)], load_sem.at[2]),
        pltpu.make_async_copy(wv_hbm, wbuf.at[:, pl.ds(HD, HD)], load_sem.at[3]),
        pltpu.make_async_copy(pb_hbm, pb, load_sem.at[4]),
        pltpu.make_async_copy(cv_hbm, cv, load_sem.at[5]),
    ]

    barrier = pltpu.get_barrier_semaphore()

    @pl.loop(1, nr, unroll=True)
    def _(k):
        pl.semaphore_signal(
            barrier, inc=1, device_id=(lax.rem(r + k, nr), t), device_id_type=MESH
        )

    @pl.loop(1, nt, unroll=True)
    def _(k):
        pl.semaphore_signal(
            barrier, inc=1, device_id=(r, lax.rem(t + k, nt)), device_id_type=MESH
        )

    for load in small + loads:
        load.start()
    pl.semaphore_wait(barrier, nr - 1 + nt - 1)

    right = (r, lax.rem(t + 1, nt))
    left = (r, lax.rem(t + nt - 1, nt))
    half = nt // 2

    def hop(which_way, h, c):
        if which_way == 0:
            have, there, to = (nt - (h - 1)) % nt, nt - h, right
        else:
            have, there, to = h - 1, h, left
        piece = pl.ds(c * rows, rows)
        src = f_hbm.at[piece, :] if have == 0 else ring.at[have, piece, :]
        return pltpu.make_async_remote_copy(
            src_ref=src,
            dst_ref=ring.at[there, piece, :],
            send_sem=ring_send.at[which_way, h - 1, c],
            recv_sem=ring_recv.at[there, c],
            device_id=to,
            device_id_type=MESH,
        )

    def hops(h):
        if h < half:
            return [(0, 0), (1, 0), (0, 1), (1, 1)]
        return [(0, 0), (1, 1)]

    for way, c in hops(1):
        hop(way, 1, c).start()

    small[0].wait()
    small[1].wait()
    gain_rows = gain_ref[...].astype(F32)
    f32 = f_ref[...].astype(F32)
    lanes = HD
    chunks = width // lanes
    eye = iota((rows2, lanes), 0) == iota((rows2, lanes), 1)
    square_sum = jnp.sum(f32 * f32, axis=1, keepdims=True)
    square_row = jnp.sum(jnp.where(eye, square_sum, 0.0), axis=0, keepdims=True)
    stats[t] = jnp.concatenate(
        [gain_rows, jnp.broadcast_to(square_row, (8, lanes))], axis=0
    )
    @pl.loop(1, nt, unroll=True)
    def _(k):
        pltpu.make_async_remote_copy(
            src_ref=stats.at[t],
            dst_ref=stats.at[t],
            send_sem=st_send,
            recv_sem=st_recv,
            device_id=(r, lax.rem(t + k, nt)),
            device_id_type=MESH,
        ).start()

    own = jnp.concatenate(
        [
            f32[:, c * lanes : (c + 1) * lanes] * gain_rows[c : c + 1]
            for c in range(chunks)
        ],
        axis=1,
    ).astype(BF16)
    xall[pl.ds(nvis, rows2), :] = own

    for load in small[2:5]:
        load.wait()
    ra = ra_ref[...]
    need = need_ref[...]
    mine = jnp.sum(
        jnp.where(iota(need.shape, 1) == r, need, 0).astype(F32), axis=1, keepdims=True
    )
    entry = iota((need_count, rows), 0) == ra
    wanted = jnp.sum(jnp.where(entry, mine, 0.0), axis=0, keepdims=True)
    place = place_ref[...]
    home = place // pool
    local = place - home * pool
    at_me = jnp.where(home == r, local + 1, 0)
    table = jnp.concatenate(
        [
            jnp.broadcast_to(x.astype(F32), (8, adapters))
            for x in (home, local, at_me)
        ],
        axis=0,
    ).astype(BF16)
    which = iota((adapters, rows), 0) == wanted.astype(jnp.int32)
    found = jnp.dot(
        table, jnp.where(which, 1.0, 0.0).astype(BF16), preferred_element_type=F32
    )
    owner = found[0:1].astype(jnp.int32)
    eye_r = iota((rows, rows), 0) == iota((rows, rows), 1)
    ra_f = ra.astype(F32)
    ra_col = jnp.sum(jnp.where(eye_r, ra_f, 0.0), axis=1, keepdims=True)
    twin = (ra_col == ra_f) & (iota((rows, rows), 0) < iota((rows, rows), 1))
    turn = jnp.sum(jnp.where(twin, 1.0, 0.0), axis=0, keepdims=True).astype(jnp.int32)
    is_far = ra < need_count
    code = jnp.where(is_far, owner * 16 + turn * 8, -1000)
    code2 = jnp.concatenate([code, code + 4], axis=1)

    slot_iota = iota((nr * 16, rows2), 0)
    total = None
    for j in range(4):
        pick = jnp.where(slot_iota == code2 + j, 1.0, 0.0).astype(BF16)
        piece = jnp.dot(
            pick, own[:, j * QUARTER : (j + 1) * QUARTER], preferred_element_type=F32
        )
        total = piece if total is None else total + piece
    msg[...] = total.astype(BF16)
    got[pl.ds(pl.multiple_of(r * 16, 16), 16), :] = jnp.zeros((16, QUARTER), BF16)
    ret_got[pl.ds(pl.multiple_of(r * 8, 8), 8), :] = jnp.zeros((8, HD), F32)

    @pl.loop(1, nr, unroll=True)
    def _(k):
        to = lax.rem(r + k, nr)
        pltpu.make_async_remote_copy(
            src_ref=msg.at[pl.ds(pl.multiple_of(to * 16, 16), 16), :],
            dst_ref=got.at[pl.ds(pl.multiple_of(r * 16, 16), 16), :],
            send_sem=a2a_send,
            recv_sem=a2a_recv,
            device_id=(to, t),
            device_id_type=MESH,
        ).start()

    def wait_bytes(ref, sem):
        pltpu.make_async_copy(ref, ref, sem).wait()

    asked = jnp.zeros((adapters, nr), jnp.bool_)
    p_iota = iota((adapters, nr), 0)
    for e in range(need_count):
        asked = asked | (p_iota == need[e : e + 1, :])
    visit = jnp.dot(
        table, jnp.where(asked, 1.0, 0.0).astype(BF16), preferred_element_type=F32
    )[16:24]
    spread = jnp.where(iota((nr, nvis), 1) // 4 == iota((nr, nvis), 0), 1.0, 0.0)
    visit_slot = jnp.dot(
        visit.astype(BF16), spread.astype(BF16), preferred_element_type=F32
    )[0:1].astype(jnp.int32) - 1
    own_slot = jnp.where(is_far, -1, ra - need_count)
    slot_row = jnp.concatenate([visit_slot, own_slot, own_slot], axis=1)

    scale = 1.0 / math.sqrt(HD)
    cache_len = ck.shape[1]
    per_row = 2 * GROUP

    def cached_scores(lo, hi):
        @pl.loop(lo, hi, unroll=4)
        def _(i):
            s = (
                lax.dot_general(q_ref[i], ck[i], NT, preferred_element_type=F32) * scale
            )
            live = iota(s.shape, 1) < len_s[i]
            scores[i] = jnp.where(live, s, NEG)

    def ring_stage(h, which_chunks=(0, 1)):
        for way, c in hops(h):
            if c not in which_chunks:
                continue
            hop(way, h, c).wait_recv()
            if (way, c) in (hops(h + 1) if h < half else []):
                hop(way, h + 1, c).start()

    for load in small[5:]:
        load.wait()
    for step in range(2):
        for g in range(GROUP):
            q_wide[pl.ds(step * GROUP + g, rows, stride=per_row), :] = q_in[
                step * rows : (step + 1) * rows, g * HD : (g + 1) * HD
            ].astype(F32)
    q_ref[...] = q_wide[...].astype(BF16).reshape(rows, per_row, HD)
    loads[0].wait()
    cached_scores(0, rows // 4)
    ring_stage(1, (0,))
    cached_scores(rows // 4, rows)
    ring_stage(1, (1,))

    if half > 2:
        ring_stage(2, (0,))
    loads[1].wait()
    wait_bytes(got.at[pl.ds(0, (nr - 1) * 16), :], a2a_recv)
    arrived = got[...]
    for j in range(4):
        gather = iota((nvis, nr * 16), 1) == iota((nvis, nr * 16), 0) * 4 + j
        xall[pl.ds(0, nvis), j * QUARTER : (j + 1) * QUARTER] = jnp.dot(
            jnp.where(gather, 1.0, 0.0).astype(BF16),
            arrived,
            preferred_element_type=F32,
        ).astype(BF16)
    x = xall[...]
    group = 8
    part[...] = jnp.zeros(part.shape, F32)

    def low_rank(g):
        base = g * group
        block = lax.dot_general(
            pa[base * rank : (base + group) * rank, :],
            x,
            NT,
            preferred_element_type=F32,
        )
        picked = jnp.zeros((rank, ntot), F32)
        for s in range(group):
            picked += jnp.where(
                slot_row == base + s, block[s * rank : (s + 1) * rank], 0.0
            )
        part[:, :, pl.ds(0, ntot)] += picked.reshape(nt, kpart, ntot)

    for g in range(pool // group):
        low_rank(g)
        if g == 1 and half > 2:
            ring_stage(2, (1,))

    @pl.loop(1, nt, unroll=True)
    def _(k):
        to = lax.rem(t + k, nt)
        pltpu.make_async_remote_copy(
            src_ref=part.at[to],
            dst_ref=rs_got.at[t],
            send_sem=rs_send,
            recv_sem=rs_recv,
            device_id=(r, to),
            device_id_type=MESH,
        ).start()

    qrows = 8
    span = qrows * per_row
    for b in range(rows // qrows):
        s = scores[b * qrows : (b + 1) * qrows].reshape(span, cache_len)
        top = jnp.max(s, axis=1, keepdims=True)
        e_cache = jnp.exp(s - top)
        top_ref[b * span : (b + 1) * span, :] = top
        bottom_ref[b * span : (b + 1) * span, :] = jnp.sum(
            e_cache, axis=1, keepdims=True
        )
        weights[b * qrows : (b + 1) * qrows] = e_cache.astype(BF16).reshape(
            qrows, per_row, cache_len
        )

    wait_bytes(stats.at[pl.ds(0, nt - 1)], st_recv)
    square = stats[0, 8:16, :]
    for k in range(1, nt):
        square += stats[k, 8:16, :]
    inverse_row = lax.rsqrt(square[0:1] / (width * nt) + EPS)
    inverse = jnp.sum(jnp.where(eye, inverse_row, 0.0), axis=1, keepdims=True)

    def project(o):
        source = lax.rem(t + o, nt)
        block = f_ref[...] if o == 0 else ring[o]
        block = block.astype(F32) * inverse
        gains = stats[source][0:8]
        normed = jnp.concatenate(
            [
                block[:, c * lanes : (c + 1) * lanes] * gains[c : c + 1]
                for c in range(chunks)
            ],
            axis=1,
        ).astype(BF16)
        w = wbuf[pl.ds(pl.multiple_of(source * width, width), width), :]
        product = jnp.dot(normed, w, preferred_element_type=F32)
        if o == 0:
            acc_kv[...] = product
        else:
            acc_kv[...] += product

    loads[2].wait()
    loads[3].wait()
    project(0)
    project(nt - 1)
    if half > 1:
        project(1)

    length_row = len_ref[...].astype(F32)
    positions = jnp.sum(
        jnp.where(eye_r, length_row, 0.0), axis=1, keepdims=True
    )
    positions = jnp.concatenate([positions, positions + 1.0], axis=0)
    angle = positions * freq_ref[...]
    sign = jnp.where(iota((rows2, HD), 1) < HD // 2, -1.0, 1.0)
    cos_ref[...] = jnp.cos(angle)
    sin_ref[...] = jnp.sin(angle) * sign

    wait_bytes(rs_got.at[pl.ds(0, nt - 1)], rs_recv)
    whole = part[t]
    for k in range(nt):
        whole += jnp.where(k == t, 0.0, rs_got[k])
    coeff[t] = whole

    @pl.loop(1, nt, unroll=True)
    def _(k):
        pltpu.make_async_remote_copy(
            src_ref=coeff.at[t],
            dst_ref=coeff.at[t],
            send_sem=ag_send,
            recv_sem=ag_recv,
            device_id=(r, lax.rem(t + k, nt)),
            device_id_type=MESH,
        ).start()

    for h in range(3, half):
        ring_stage(h)
        project(nt - h + 1)
        project(h - 1)

    loads[5].wait()

    @pl.loop(0, rows, unroll=4)
    def _(i):
        att_acc[pl.ds(pl.multiple_of(i * per_row, per_row), per_row), :] = jnp.dot(
            weights[i], cv[i], preferred_element_type=F32
        )

    loads[4].wait()
    pbt[...] = pb[...].T

    wait_bytes(coeff.at[pl.ds(0, nt - 1)], ag_recv)
    coeffs = coeff[...].reshape(rank, coeff.shape[2])[:, 0:ntot]
    for s in range(pool):
        expand[s * rank : (s + 1) * rank, :] = jnp.where(
            slot_row == s, coeffs, 0.0
        ).astype(BF16)
    delta = jnp.dot(pbt[...], expand[...], preferred_element_type=F32).T
    ret_send[...] = delta[0:nvis]
    own_delta = delta[nvis:ntot]

    @pl.loop(1, nr, unroll=True)
    def _(k):
        to = lax.rem(r + k, nr)
        pltpu.make_async_remote_copy(
            src_ref=ret_send.at[pl.ds(pl.multiple_of(to // 2 * 8, 8), 8), :],
            dst_ref=ret_got.at[pl.ds(pl.multiple_of(r * 8, 8), 8), :],
            send_sem=re_send,
            recv_sem=re_recv,
            device_id=(to, t),
            device_id_type=MESH,
        ).start()

    if half > 2:
        project(nt - half + 1)
        project(half - 1)
    ring_stage(half)
    project(half)

    key = acc_kv[:, 0:HD]
    turned = key * cos_ref[...] + pltpu.roll(key, HD // 2, 1) * sin_ref[...]
    new_keys = turned.astype(BF16)
    nk_ref[...] = new_keys

    for b in range(rows // qrows):
        part_rows = slice(b * span, (b + 1) * span)
        q = q_ref[b * qrows : (b + 1) * qrows].reshape(span, HD)
        fresh = (
            lax.dot_general(q, new_keys, NT, preferred_element_type=F32) * scale
        )
        row_of = iota(fresh.shape, 0) // per_row + b * qrows
        step_of = iota(fresh.shape, 0) % per_row // GROUP
        column = iota(fresh.shape, 1)
        seen = (column == row_of) | ((column == row_of + rows) & (step_of == 1))
        fresh = jnp.where(seen, fresh, NEG)
        cache_top = top_ref[part_rows, :]
        top = jnp.maximum(cache_top, jnp.max(fresh, axis=1, keepdims=True))
        shrink = jnp.exp(cache_top - top)
        e_fresh = jnp.exp(fresh - top)
        bottom = bottom_ref[part_rows, :] * shrink + jnp.sum(
            e_fresh, axis=1, keepdims=True
        )
        share = 1.0 / bottom
        fresh_w[part_rows, :] = (e_fresh * share).astype(BF16)
        att_acc[part_rows, :] = att_acc[part_rows, :] * (shrink * share)

    code_f = jnp.where(
        is_far, owner * 8 + lax.rem(r, 2) * 4 + turn * 2, -1000
    ).astype(F32)
    code_col = jnp.sum(jnp.where(eye_r, code_f, 0.0), axis=1, keepdims=True)
    code_col = jnp.concatenate([code_col, code_col + 1.0], axis=0).astype(jnp.int32)
    back = jnp.where(iota((rows2, nr * 8), 1) == code_col, 1.0, 0.0).astype(BF16)
    wait_bytes(ret_got.at[pl.ds(0, (nr - 1) * 8), :], re_recv)
    returned = ret_got[...]
    high = returned.astype(BF16)
    low = (returned - high.astype(F32)).astype(BF16)
    far_delta = jnp.dot(back, high, preferred_element_type=F32) + jnp.dot(
        back, low, preferred_element_type=F32
    )
    new_values = (acc_kv[:, HD : 2 * HD] + inverse * (far_delta + own_delta)).astype(
        BF16
    )
    nv_ref[...] = new_values
    att_acc[...] += jnp.dot(fresh_w[...], new_values, preferred_element_type=F32)
    for step in range(2):
        for g in range(GROUP):
            att_ref[step * rows : (step + 1) * rows, g * HD : (g + 1) * HD] = att_acc[
                pl.ds(step * GROUP + g, rows, stride=per_row), :
            ].astype(BF16)

    for h in range(1, half + 1):
        for way, c in hops(h):
            hop(way, h, c).wait_send()
    wait_bytes(stats.at[pl.ds(0, nt - 1)], st_send)
    wait_bytes(msg.at[pl.ds(0, (nr - 1) * 16), :], a2a_send)
    wait_bytes(part.at[pl.ds(0, nt - 1)], rs_send)
    wait_bytes(coeff.at[pl.ds(0, nt - 1)], ag_send)
    wait_bytes(ret_got.at[pl.ds(0, (nr - 1) * 8), :], re_send)


def write_out(a, b, c, a_out, b_out, c_out, sem):
    copies = [
        pltpu.make_async_copy(src, dst, sem.at[k])
        for k, (src, dst) in enumerate([(a, a_out), (b, b_out), (c, c_out)])
    ]
    for copy in copies:
        copy.start()
    for copy in copies:
        copy.wait()


def shards(
    features,
    gain,
    w_key,
    w_value,
    pool_a,
    pool_b,
    placement,
    need_lists,
    row_adapter,
    lengths,
    queries,
    cache_k,
    cache_v,
):
    nr, nt = lax.axis_size("replica"), lax.axis_size("tp")
    steps, rows, width = features.shape
    pool, _, rank = pool_a.shape
    cache_len = cache_k.shape[1]
    rows2 = steps * rows
    nvis = nr * 4
    ntot = nvis + rows2
    ntot_pad = -(-ntot // HD) * HD
    per_row = steps * GROUP
    half = HD // 2
    frequency = np.float32(THETA) ** (-(np.arange(half, dtype=np.float32) * 2.0) / HD)
    frequency = np.concatenate([frequency, frequency]).astype(np.float32)[None, :]
    vmem = pl.BlockSpec(memory_space=pltpu.VMEM)
    hbm = pl.BlockSpec(memory_space=pltpu.HBM)
    dma = pltpu.SemaphoreType.DMA
    att, nk, nv = pl.pallas_call(
        functools.partial(kernel, nr, nt),
        out_shape=(
            jax.ShapeDtypeStruct((rows2, width), BF16),
            jax.ShapeDtypeStruct((rows2, HD), BF16),
            jax.ShapeDtypeStruct((rows2, HD), BF16),
        ),
        in_specs=[hbm] * 15,
        out_specs=(vmem, vmem, vmem),
        scratch_shapes=[
            pltpu.VMEM((rows2, width), BF16),
            pltpu.VMEM((width // HD, HD), BF16),
            pltpu.VMEM((1, placement.shape[0]), jnp.int32),
            pltpu.VMEM(need_lists.shape[::-1], jnp.int32),
            pltpu.VMEM((1, rows), jnp.int32),
            pltpu.SMEM((rows,), jnp.int32),
            pltpu.VMEM((1, rows), jnp.int32),
            pltpu.VMEM((1, HD), F32),
            pltpu.VMEM((rows2, width), BF16),
            pltpu.VMEM((rows * per_row, HD), F32),
            pltpu.VMEM((rows, per_row, HD), BF16),
            pltpu.VMEM((nt * width, 2 * HD), BF16),
            pltpu.VMEM((pool * rank, width), BF16),
            pltpu.VMEM((pool * rank, HD), BF16),
            pltpu.VMEM((HD, pool * rank), BF16),
            pltpu.VMEM((rows, cache_len, HD), BF16),
            pltpu.VMEM((rows, cache_len, HD), BF16),
            pltpu.VMEM((nt, 16, HD), F32),
            pltpu.VMEM((nr * 16, QUARTER), BF16),
            pltpu.VMEM((nr * 16, QUARTER), BF16),
            pltpu.VMEM((ntot, width), BF16),
            pltpu.VMEM((nt, rows2, width), BF16),
            pltpu.VMEM((nt, rank // nt, ntot_pad), F32),
            pltpu.VMEM((nt, rank // nt, ntot_pad), F32),
            pltpu.VMEM((nt, rank // nt, ntot_pad), F32),
            pltpu.VMEM((pool * rank, ntot), BF16),
            pltpu.VMEM((nvis, HD), F32),
            pltpu.VMEM((nr * 8, HD), F32),
            pltpu.VMEM((rows, per_row, cache_len), F32),
            pltpu.VMEM((rows, per_row, cache_len), BF16),
            pltpu.VMEM((rows * per_row, rows2), BF16),
            pltpu.VMEM((rows2, 2 * HD), F32),
            pltpu.VMEM((rows * per_row, HD), F32),
            pltpu.VMEM((rows * per_row, 1), F32),
            pltpu.VMEM((rows * per_row, 1), F32),
            pltpu.VMEM((rows2, HD), F32),
            pltpu.VMEM((rows2, HD), F32),
            dma((9,)),
            dma((6,)),
            dma,
            dma,
            dma,
            dma,
            dma((2, max(nt // 2, 1), 2)),
            dma((nt, 2)),
            dma,
            dma,
            dma,
            dma,
            dma,
            dma,
        ],
        compiler_params=pltpu.CompilerParams(
            collective_id=0, has_side_effects=True, vmem_limit_bytes=60 * 2**20
        ),
        cost_estimate=pl.CostEstimate(
            flops=2 * 64 * 8192 * 256, bytes_accessed=12 * 2**20, transcendentals=0
        ),
    )(
        features.reshape(rows2, width),
        gain.reshape(width // HD, HD),
        placement.reshape(1, -1),
        need_lists.T,
        row_adapter.reshape(1, rows),
        lengths,
        lengths.reshape(1, rows),
        jnp.asarray(frequency),
        queries.reshape(rows2, width),
        w_key,
        w_value,
        pool_a.swapaxes(1, 2).reshape(pool * rank, width),
        pool_b.reshape(pool * rank, HD),
        cache_k,
        cache_v,
    )
    shapes = tuple(jax.ShapeDtypeStruct(x.shape, BF16) for x in (att, nk, nv))
    att, nk, nv = pl.pallas_call(
        write_out,
        out_shape=shapes,
        in_specs=[vmem] * 3,
        out_specs=(hbm,) * 3,
        scratch_shapes=[dma((3,))],
        compiler_params=pltpu.CompilerParams(vmem_limit_bytes=60 * 2**20),
    )(att, nk, nv)
    return (
        att.reshape(steps, rows, width),
        nk.reshape(steps, rows, HD),
        nv.reshape(steps, rows, HD),
    )


def solution(mesh):
    placed = (
        P(None, "replica", "tp"),
        P("tp"),
        P(None, "tp"),
        P(None, "tp"),
        P("replica", "tp", None),
        P("replica", None, "tp"),
        P(),
        P(),
        P("replica"),
        P("replica"),
        P(None, "replica", "tp"),
        P("replica", None, "tp"),
        P("replica", None, "tp"),
    )
    return jax.shard_map(
        shards,
        mesh=mesh,
        in_specs=placed,
        out_specs=(P(None, "replica", "tp"), P(None, "replica", "tp"), P(None, "replica", "tp")),
        check_vma=False,
    )
```

```python
import functools
import math

import jax
import jax.numpy as jnp
import numpy as np
from jax import lax
from jax.experimental import pallas as pl
from jax.experimental.pallas import tpu as pltpu
from jax.sharding import PartitionSpec as P

HD = 128
GROUP = 8
EPS = 1e-05
THETA = 500000.0
NEG = -1e30
MESH = pl.DeviceIdType.MESH
F32 = jnp.float32
BF16 = jnp.bfloat16
QUARTER = 256
NT = (((1,), (1,)), ((), ()))


def iota(shape, dim):
    return lax.broadcasted_iota(jnp.int32, shape, dim)


def kernel(
    nr,
    nt,
    f_hbm,
    gain_hbm,
    place_hbm,
    need_hbm,
    ra_hbm,
    len_s_hbm,
    len_hbm,
    freq_hbm,
    q_hbm,
    wk_hbm,
    wv_hbm,
    pa_hbm,
    pb_hbm,
    ck_hbm,
    cv_hbm,
    att_ref,
    nk_ref,
    nv_ref,
    gain_ref,
    place_ref,
    need_ref,
    ra_ref,
    len_s,
    len_ref,
    freq_ref,
    q_in,
    q_wide,
    q_ref,
    wbuf,
    pa,
    pb,
    pbt,
    ck,
    cv,
    stats,
    msg,
    got,
    xall,
    ring,
    part,
    rs_got,
    coeff,
    expand,
    ret_send,
    ret_got,
    scores,
    weights,
    fresh_w,
    acc_kv,
    att_acc,
    top_ref,
    bottom_ref,
    cos_ref,
    sin_ref,
    small_sem,
    load_sem,
    st_send,
    st_recv,
    a2a_send,
    a2a_recv,
    ring_send,
    ring_recv,
    rs_send,
    rs_recv,
    ag_send,
    ag_recv,
    re_send,
    re_recv,
):
    r = lax.axis_index("replica")
    t = lax.axis_index("tp")
    rows2, width = f_hbm.shape
    rows = rows2 // 2
    need_count = need_ref.shape[0]
    adapters = place_ref.shape[1]
    pool = adapters // nr
    rank = part.shape[1] * nt
    kpart = rank // nt
    nvis = nr * 4
    ntot = nvis + rows2

    small = [
        pltpu.make_async_copy(a, b, small_sem.at[k])
        for k, (a, b) in enumerate(
            [
                (f_hbm, ring.at[0]),
                (gain_hbm, gain_ref),
                (ra_hbm, ra_ref),
                (need_hbm, need_ref),
                (place_hbm, place_ref),
                (len_s_hbm, len_s),
                (len_hbm, len_ref),
                (freq_hbm, freq_ref),
                (q_hbm, q_in),
            ]
        )
    ]
    loads = [
        pltpu.make_async_copy(ck_hbm, ck, load_sem.at[0]),
        pltpu.make_async_copy(pa_hbm, pa, load_sem.at[1]),
        pltpu.make_async_copy(wk_hbm, wbuf.at[:, pl.ds(0, HD)], load_sem.at[2]),
        pltpu.make_async_copy(wv_hbm, wbuf.at[:, pl.ds(HD, HD)], load_sem.at[3]),
        pltpu.make_async_copy(pb_hbm, pb, load_sem.at[4]),
        pltpu.make_async_copy(cv_hbm, cv, load_sem.at[5]),
    ]

    barrier = pltpu.get_barrier_semaphore()

    @pl.loop(1, nr)
    def _(k):
        pl.semaphore_signal(
            barrier, inc=1, device_id=(lax.rem(r + k, nr), t), device_id_type=MESH
        )

    @pl.loop(1, nt)
    def _(k):
        pl.semaphore_signal(
            barrier, inc=1, device_id=(r, lax.rem(t + k, nt)), device_id_type=MESH
        )

    for load in small + loads:
        load.start()

    small[0].wait()
    small[1].wait()
    gain_rows = gain_ref[...].astype(F32)
    f32 = ring[0].astype(F32)
    lanes = HD
    chunks = width // lanes
    eye = iota((rows2, lanes), 0) == iota((rows2, lanes), 1)
    square_sum = jnp.sum(f32 * f32, axis=1, keepdims=True)
    square_row = jnp.sum(jnp.where(eye, square_sum, 0.0), axis=0, keepdims=True)
    stats[t] = jnp.concatenate(
        [gain_rows, jnp.broadcast_to(square_row, (8, lanes))], axis=0
    )
    own = jnp.concatenate(
        [
            f32[:, c * lanes : (c + 1) * lanes] * gain_rows[c : c + 1]
            for c in range(chunks)
        ],
        axis=1,
    ).astype(BF16)
    xall[pl.ds(nvis, rows2), :] = own

    for load in small[2:5]:
        load.wait()
    ra = ra_ref[...]
    need = need_ref[...]
    mine = jnp.sum(
        jnp.where(iota(need.shape, 1) == r, need, 0).astype(F32), axis=1, keepdims=True
    )
    entry = iota((need_count, rows), 0) == ra
    wanted = jnp.sum(jnp.where(entry, mine, 0.0), axis=0, keepdims=True)
    place = place_ref[...]
    home = place // pool
    local = place - home * pool
    table = jnp.concatenate(
        [
            jnp.broadcast_to(x.astype(F32), (8, adapters))
            for x in (home, local)
        ],
        axis=0,
    ).astype(BF16)
    which = iota((adapters, rows), 0) == wanted.astype(jnp.int32)
    found = jnp.dot(
        table, jnp.where(which, 1.0, 0.0).astype(BF16), preferred_element_type=F32
    )
    owner = found[0:1].astype(jnp.int32)
    eye_r = iota((rows, rows), 0) == iota((rows, rows), 1)
    ra_f = ra.astype(F32)
    ra_col = jnp.sum(jnp.where(eye_r, ra_f, 0.0), axis=1, keepdims=True)
    twin = (ra_col == ra_f) & (iota((rows, rows), 0) < iota((rows, rows), 1))
    turn = jnp.sum(jnp.where(twin, 1.0, 0.0), axis=0, keepdims=True).astype(jnp.int32)
    is_far = ra < need_count
    code = jnp.where(is_far, owner * 16 + turn * 8, -1000)
    code2 = jnp.concatenate([code, code + 4], axis=1)

    slot_iota = iota((nr * 16, rows2), 0)
    total = None
    for j in range(4):
        pick = jnp.where(slot_iota == code2 + j, 1.0, 0.0).astype(BF16)
        piece = jnp.dot(
            pick, own[:, j * QUARTER : (j + 1) * QUARTER], preferred_element_type=F32
        )
        total = piece if total is None else total + piece
    msg[...] = total.astype(BF16)
    got[pl.ds(pl.multiple_of(r * 16, 16), 16), :] = jnp.zeros((16, QUARTER), BF16)
    ret_got[pl.ds(pl.multiple_of(r * 8, 8), 8), :] = jnp.zeros((8, HD), F32)

    pl.semaphore_wait(barrier, nr - 1 + nt - 1)

    right = (r, lax.rem(t + 1, nt))
    left = (r, lax.rem(t + nt - 1, nt))
    half = nt // 2

    def hop(which_way, h, c):
        if which_way == 0:
            have, there, to = (nt - (h - 1)) % nt, nt - h, right
        else:
            have, there, to = h - 1, h, left
        piece = pl.ds(c * rows, rows)
        return pltpu.make_async_remote_copy(
            src_ref=ring.at[have, piece, :],
            dst_ref=ring.at[there, piece, :],
            send_sem=ring_send.at[which_way, h - 1, c],
            recv_sem=ring_recv.at[there, c],
            device_id=to,
            device_id_type=MESH,
        )

    def hops(h):
        if h < half:
            return [(0, 0), (1, 0), (0, 1), (1, 1)]
        return [(0, 0), (1, 1)]

    for way, c in hops(1):
        hop(way, 1, c).start()

    @pl.loop(1, nt)
    def _(k):
        pltpu.make_async_remote_copy(
            src_ref=stats.at[t],
            dst_ref=stats.at[t],
            send_sem=st_send,
            recv_sem=st_recv,
            device_id=(r, lax.rem(t + k, nt)),
            device_id_type=MESH,
        ).start()

    @pl.loop(1, nr)
    def _(k):
        to = lax.rem(r + k, nr)
        pltpu.make_async_remote_copy(
            src_ref=msg.at[pl.ds(pl.multiple_of(to * 16, 16), 16), :],
            dst_ref=got.at[pl.ds(pl.multiple_of(r * 16, 16), 16), :],
            send_sem=a2a_send,
            recv_sem=a2a_recv,
            device_id=(to, t),
            device_id_type=MESH,
        ).start()

    def wait_bytes(ref, sem):
        pltpu.make_async_copy(ref, ref, sem).wait()

    packs = max(1, min(HD // nr, need_count))
    while need_count % packs:
        packs -= 1
    tall = need_count // packs
    packed = jnp.concatenate(
        [need[k * tall : (k + 1) * tall, :] for k in range(packs)], axis=1
    )
    span_p = 256

    def visitors(k, total):
        base = pl.multiple_of(k * span_p, span_p)
        p_iota = iota((span_p, packs * nr), 0) + base
        asked = p_iota == packed[0:1, :]
        for e in range(1, tall):
            asked = asked | (p_iota == packed[e : e + 1, :])
        there = place_ref[:, pl.ds(base, span_p)]
        there_home = there // pool
        slot1 = jnp.where(there_home == r, there - there_home * pool + 1, 0)
        slot1 = jnp.broadcast_to(slot1.astype(F32), (8, span_p)).astype(BF16)
        return total + jnp.dot(
            slot1, jnp.where(asked, 1.0, 0.0).astype(BF16), preferred_element_type=F32
        )

    visit = lax.fori_loop(
        0, adapters // span_p, visitors, jnp.zeros((8, packs * nr), F32)
    )
    wide = (packs * nr, nvis)
    spread = jnp.where(iota(wide, 1) // 4 == iota(wide, 0) % nr, 1.0, 0.0)
    visit_slot = jnp.dot(
        visit.astype(BF16), spread.astype(BF16), preferred_element_type=F32
    )[0:1].astype(jnp.int32) - 1
    own_slot = jnp.where(is_far, -1, ra - need_count)
    slot_row = jnp.concatenate([visit_slot, own_slot, own_slot], axis=1)

    scale = 1.0 / math.sqrt(HD)
    cache_len = ck.shape[1]
    per_row = 2 * GROUP

    def cached_scores(lo, hi):
        @pl.loop(lo, hi, unroll=2)
        def _(i):
            s = (
                lax.dot_general(q_ref[i], ck[i], NT, preferred_element_type=F32) * scale
            )
            live = iota(s.shape, 1) < len_s[i]
            scores[i] = jnp.where(live, s, NEG)

    def ring_stage(h, which_chunks=(0, 1)):
        for way, c in hops(h):
            if c not in which_chunks:
                continue
            hop(way, h, c).wait_recv()
            if (way, c) in (hops(h + 1) if h < half else []):
                hop(way, h + 1, c).start()

    for load in small[5:]:
        load.wait()
    for step in range(2):
        for g in range(GROUP):
            q_wide[pl.ds(step * GROUP + g, rows, stride=per_row), :] = q_in[
                step * rows : (step + 1) * rows, g * HD : (g + 1) * HD
            ].astype(F32)
    q_ref[...] = q_wide[...].astype(BF16).reshape(rows, per_row, HD)
    loads[0].wait()
    cached_scores(0, rows // 4)
    ring_stage(1, (0,))
    cached_scores(rows // 4, rows)
    ring_stage(1, (1,))

    if half > 2:
        ring_stage(2, (0,))
    loads[1].wait()
    wait_bytes(got.at[pl.ds(0, (nr - 1) * 16), :], a2a_recv)
    arrived = got[...]
    for j in range(4):
        gather = iota((nvis, nr * 16), 1) == iota((nvis, nr * 16), 0) * 4 + j
        xall[pl.ds(0, nvis), j * QUARTER : (j + 1) * QUARTER] = jnp.dot(
            jnp.where(gather, 1.0, 0.0).astype(BF16),
            arrived,
            preferred_element_type=F32,
        ).astype(BF16)
    x = xall[...]
    group = 4
    part[...] = jnp.zeros(part.shape, F32)

    @pl.loop(0, pool // group)
    def _(g):
        base = g * group
        block = lax.dot_general(
            pa[pl.ds(pl.multiple_of(base * rank, group * rank), group * rank), :],
            x,
            NT,
            preferred_element_type=F32,
        )
        picked = jnp.zeros((rank, ntot), F32)
        for s in range(group):
            picked += jnp.where(
                slot_row == base + s, block[s * rank : (s + 1) * rank], 0.0
            )
        part[:, :, pl.ds(0, ntot)] += picked.reshape(nt, kpart, ntot)

    @pl.loop(1, nt)
    def _(k):
        to = lax.rem(t + k, nt)
        pltpu.make_async_remote_copy(
            src_ref=part.at[to],
            dst_ref=rs_got.at[t],
            send_sem=rs_send,
            recv_sem=rs_recv,
            device_id=(r, to),
            device_id_type=MESH,
        ).start()

    if half > 2:
        ring_stage(2, (1,))

    qrows = 8
    span = qrows * per_row
    @pl.loop(0, rows // qrows)
    def _(b):
        group_rows = pl.ds(b * qrows, qrows)
        lines = pl.ds(pl.multiple_of(b * span, span), span)
        s = scores[group_rows].reshape(span, cache_len)
        top = jnp.max(s, axis=1, keepdims=True)
        e_cache = jnp.exp(s - top)
        top_ref[lines, :] = top
        bottom_ref[lines, :] = jnp.sum(e_cache, axis=1, keepdims=True)
        weights[group_rows] = e_cache.astype(BF16).reshape(qrows, per_row, cache_len)

    wait_bytes(stats.at[pl.ds(0, nt - 1)], st_recv)
    square = stats[0, 8:16, :]
    for k in range(1, nt):
        square += stats[k, 8:16, :]
    inverse_row = lax.rsqrt(square[0:1] / (width * nt) + EPS)
    inverse = jnp.sum(jnp.where(eye, inverse_row, 0.0), axis=1, keepdims=True)

    acc_kv[...] = jnp.zeros(acc_kv.shape, F32)

    def project(o):
        source = lax.rem(t + o, nt)
        block = ring[o].astype(F32) * inverse
        gains = stats[source, 0:8, :]
        normed = jnp.concatenate(
            [
                block[:, c * lanes : (c + 1) * lanes] * gains[c : c + 1]
                for c in range(chunks)
            ],
            axis=1,
        ).astype(BF16)
        w = wbuf[pl.ds(pl.multiple_of(source * width, width), width), :]
        acc_kv[...] += jnp.dot(normed, w, preferred_element_type=F32)

    def project_all(first, count, stride):
        @pl.loop(0, count)
        def _(k):
            project(lax.rem(first + k * stride, nt))

    loads[2].wait()
    loads[3].wait()
    project_all(nt - 1, 3, 1)

    length_row = len_ref[...].astype(F32)
    positions = jnp.sum(
        jnp.where(eye_r, length_row, 0.0), axis=1, keepdims=True
    )
    positions = jnp.concatenate([positions, positions + 1.0], axis=0)
    angle = positions * freq_ref[...]
    sign = jnp.where(iota((rows2, HD), 1) < HD // 2, -1.0, 1.0)
    cos_ref[...] = angle
    sin_ref[...] = sign

    @pl.loop(0, rows2 // 8)
    def _(k):
        lines = pl.ds(pl.multiple_of(k * 8, 8), 8)
        some = cos_ref[lines, :]
        cos_ref[lines, :] = jnp.cos(some)
        sin_ref[lines, :] = jnp.sin(some) * sin_ref[lines, :]

    wait_bytes(rs_got.at[pl.ds(0, nt - 1)], rs_recv)
    whole = part[t]
    for k in range(nt):
        whole += jnp.where(k == t, 0.0, rs_got[k])
    coeff[t] = whole

    @pl.loop(1, nt)
    def _(k):
        pltpu.make_async_remote_copy(
            src_ref=coeff.at[t],
            dst_ref=coeff.at[t],
            send_sem=ag_send,
            recv_sem=ag_recv,
            device_id=(r, lax.rem(t + k, nt)),
            device_id_type=MESH,
        ).start()

    for h in range(3, half):
        ring_stage(h)
        project_all(nt - h + 1, 2, 2 * (h - 1))

    loads[5].wait()

    @pl.loop(0, rows, unroll=2)
    def _(i):
        att_acc[pl.ds(pl.multiple_of(i * per_row, per_row), per_row), :] = jnp.dot(
            weights[i], cv[i], preferred_element_type=F32
        )

    loads[4].wait()

    @pl.loop(0, pool * rank // HD)
    def _(k):
        lines = pl.ds(pl.multiple_of(k * HD, HD), HD)
        pbt[:, lines] = pb[lines, :].T

    wait_bytes(coeff.at[pl.ds(0, nt - 1)], ag_recv)
    coeffs = coeff[...].reshape(rank, coeff.shape[2])[:, 0:ntot]
    @pl.loop(0, pool)
    def _(s):
        expand[pl.ds(pl.multiple_of(s * rank, rank), rank), :] = jnp.where(
            slot_row == s, coeffs, 0.0
        ).astype(BF16)

    delta = jnp.dot(pbt[...], expand[...], preferred_element_type=F32).T
    ret_send[...] = delta[0:nvis]
    own_delta = delta[nvis:ntot]

    @pl.loop(1, nr)
    def _(k):
        to = lax.rem(r + k, nr)
        pltpu.make_async_remote_copy(
            src_ref=ret_send.at[pl.ds(pl.multiple_of(to // 2 * 8, 8), 8), :],
            dst_ref=ret_got.at[pl.ds(pl.multiple_of(r * 8, 8), 8), :],
            send_sem=re_send,
            recv_sem=re_recv,
            device_id=(to, t),
            device_id_type=MESH,
        ).start()

    ring_stage(half)
    project_all(half - 1, 3, 1)

    key = acc_kv[:, 0:HD]
    turned = key * cos_ref[...] + pltpu.roll(key, HD // 2, 1) * sin_ref[...]
    new_keys = turned.astype(BF16)
    nk_ref[...] = new_keys

    @pl.loop(0, rows // qrows)
    def _(b):
        part_rows = pl.ds(pl.multiple_of(b * span, span), span)
        q = q_ref[pl.ds(b * qrows, qrows)].reshape(span, HD)
        fresh = (
            lax.dot_general(q, new_keys, NT, preferred_element_type=F32) * scale
        )
        row_of = iota(fresh.shape, 0) // per_row + b * qrows
        step_of = iota(fresh.shape, 0) % per_row // GROUP
        column = iota(fresh.shape, 1)
        seen = (column == row_of) | ((column == row_of + rows) & (step_of == 1))
        fresh = jnp.where(seen, fresh, NEG)
        cache_top = top_ref[part_rows, :]
        top = jnp.maximum(cache_top, jnp.max(fresh, axis=1, keepdims=True))
        shrink = jnp.exp(cache_top - top)
        e_fresh = jnp.exp(fresh - top)
        bottom = bottom_ref[part_rows, :] * shrink + jnp.sum(
            e_fresh, axis=1, keepdims=True
        )
        share = 1.0 / bottom
        fresh_w[part_rows, :] = (e_fresh * share).astype(BF16)
        att_acc[part_rows, :] = att_acc[part_rows, :] * (shrink * share)

    code_f = jnp.where(
        is_far, owner * 8 + lax.rem(r, 2) * 4 + turn * 2, -1000
    ).astype(F32)
    code_col = jnp.sum(jnp.where(eye_r, code_f, 0.0), axis=1, keepdims=True)
    code_col = jnp.concatenate([code_col, code_col + 1.0], axis=0).astype(jnp.int32)
    back = jnp.where(iota((rows2, nr * 8), 1) == code_col, 1.0, 0.0).astype(BF16)
    wait_bytes(ret_got.at[pl.ds(0, (nr - 1) * 8), :], re_recv)
    returned = ret_got[...]
    high = returned.astype(BF16)
    low = (returned - high.astype(F32)).astype(BF16)
    far_delta = jnp.dot(back, high, preferred_element_type=F32) + jnp.dot(
        back, low, preferred_element_type=F32
    )
    new_values = (acc_kv[:, HD : 2 * HD] + inverse * (far_delta + own_delta)).astype(
        BF16
    )
    nv_ref[...] = new_values
    att_acc[...] += jnp.dot(fresh_w[...], new_values, preferred_element_type=F32)
    for step in range(2):
        for g in range(GROUP):
            att_ref[step * rows : (step + 1) * rows, g * HD : (g + 1) * HD] = att_acc[
                pl.ds(step * GROUP + g, rows, stride=per_row), :
            ].astype(BF16)

    for h in range(1, half + 1):
        for way, c in hops(h):
            hop(way, h, c).wait_send()
    wait_bytes(stats.at[pl.ds(0, nt - 1)], st_send)
    wait_bytes(msg.at[pl.ds(0, (nr - 1) * 16), :], a2a_send)
    wait_bytes(part.at[pl.ds(0, nt - 1)], rs_send)
    wait_bytes(coeff.at[pl.ds(0, nt - 1)], ag_send)
    wait_bytes(ret_got.at[pl.ds(0, (nr - 1) * 8), :], re_send)


def write_out(a, b, c, a_out, b_out, c_out, sem):
    copies = [
        pltpu.make_async_copy(src, dst, sem.at[k])
        for k, (src, dst) in enumerate([(a, a_out), (b, b_out), (c, c_out)])
    ]
    for copy in copies:
        copy.start()
    for copy in copies:
        copy.wait()


def shards(
    features,
    gain,
    w_key,
    w_value,
    pool_a,
    pool_b,
    placement,
    need_lists,
    row_adapter,
    lengths,
    queries,
    cache_k,
    cache_v,
):
    nr, nt = lax.axis_size("replica"), lax.axis_size("tp")
    steps, rows, width = features.shape
    pool, _, rank = pool_a.shape
    cache_len = cache_k.shape[1]
    rows2 = steps * rows
    nvis = nr * 4
    ntot = nvis + rows2
    ntot_pad = -(-ntot // HD) * HD
    per_row = steps * GROUP
    half = HD // 2
    frequency = np.float32(THETA) ** (-(np.arange(half, dtype=np.float32) * 2.0) / HD)
    frequency = np.concatenate([frequency, frequency]).astype(np.float32)[None, :]
    vmem = pl.BlockSpec(memory_space=pltpu.VMEM)
    hbm = pl.BlockSpec(memory_space=pltpu.HBM)
    dma = pltpu.SemaphoreType.DMA
    att, nk, nv = pl.pallas_call(
        functools.partial(kernel, nr, nt),
        out_shape=(
            jax.ShapeDtypeStruct((rows2, width), BF16),
            jax.ShapeDtypeStruct((rows2, HD), BF16),
            jax.ShapeDtypeStruct((rows2, HD), BF16),
        ),
        in_specs=[hbm] * 15,
        out_specs=(vmem, vmem, vmem),
        scratch_shapes=[
            pltpu.VMEM((width // HD, HD), BF16),
            pltpu.VMEM((1, placement.shape[0]), jnp.int32),
            pltpu.VMEM(need_lists.shape[::-1], jnp.int32),
            pltpu.VMEM((1, rows), jnp.int32),
            pltpu.SMEM((rows,), jnp.int32),
            pltpu.VMEM((1, rows), jnp.int32),
            pltpu.VMEM((1, HD), F32),
            pltpu.VMEM((rows2, width), BF16),
            pltpu.VMEM((rows * per_row, HD), F32),
            pltpu.VMEM((rows, per_row, HD), BF16),
            pltpu.VMEM((nt * width, 2 * HD), BF16),
            pltpu.VMEM((pool * rank, width), BF16),
            pltpu.VMEM((pool * rank, HD), BF16),
            pltpu.VMEM((HD, pool * rank), BF16),
            pltpu.VMEM((rows, cache_len, HD), BF16),
            pltpu.VMEM((rows, cache_len, HD), BF16),
            pltpu.VMEM((nt, 16, HD), F32),
            pltpu.VMEM((nr * 16, QUARTER), BF16),
            pltpu.VMEM((nr * 16, QUARTER), BF16),
            pltpu.VMEM((ntot, width), BF16),
            pltpu.VMEM((nt, rows2, width), BF16),
            pltpu.VMEM((nt, rank // nt, ntot_pad), F32),
            pltpu.VMEM((nt, rank // nt, ntot_pad), F32),
            pltpu.VMEM((nt, rank // nt, ntot_pad), F32),
            pltpu.VMEM((pool * rank, ntot), BF16),
            pltpu.VMEM((nvis, HD), F32),
            pltpu.VMEM((nr * 8, HD), F32),
            pltpu.VMEM((rows, per_row, cache_len), F32),
            pltpu.VMEM((rows, per_row, cache_len), BF16),
            pltpu.VMEM((rows * per_row, rows2), BF16),
            pltpu.VMEM((rows2, 2 * HD), F32),
            pltpu.VMEM((rows * per_row, HD), F32),
            pltpu.VMEM((rows * per_row, 1), F32),
            pltpu.VMEM((rows * per_row, 1), F32),
            pltpu.VMEM((rows2, HD), F32),
            pltpu.VMEM((rows2, HD), F32),
            dma((9,)),
            dma((6,)),
            dma,
            dma,
            dma,
            dma,
            dma((2, max(nt // 2, 1), 2)),
            dma((nt, 2)),
            dma,
            dma,
            dma,
            dma,
            dma,
            dma,
        ],
        compiler_params=pltpu.CompilerParams(
            collective_id=0, has_side_effects=True, vmem_limit_bytes=60 * 2**20
        ),
        cost_estimate=pl.CostEstimate(
            flops=2 * 64 * 8192 * 256, bytes_accessed=12 * 2**20, transcendentals=0
        ),
    )(
        features.reshape(rows2, width),
        gain.reshape(width // HD, HD),
        placement.reshape(1, -1),
        need_lists.T,
        row_adapter.reshape(1, rows),
        lengths,
        lengths.reshape(1, rows),
        jnp.asarray(frequency),
        queries.reshape(rows2, width),
        w_key,
        w_value,
        pool_a.swapaxes(1, 2).reshape(pool * rank, width),
        pool_b.reshape(pool * rank, HD),
        cache_k,
        cache_v,
    )
    shapes = tuple(jax.ShapeDtypeStruct(x.shape, BF16) for x in (att, nk, nv))
    att, nk, nv = pl.pallas_call(
        write_out,
        out_shape=shapes,
        in_specs=[vmem] * 3,
        out_specs=(hbm,) * 3,
        scratch_shapes=[dma((3,))],
        compiler_params=pltpu.CompilerParams(vmem_limit_bytes=60 * 2**20),
    )(att, nk, nv)
    return (
        att.reshape(steps, rows, width),
        nk.reshape(steps, rows, HD),
        nv.reshape(steps, rows, HD),
    )


def solution(mesh):
    placed = (
        P(None, "replica", "tp"),
        P("tp"),
        P(None, "tp"),
        P(None, "tp"),
        P("replica", "tp", None),
        P("replica", None, "tp"),
        P(),
        P(),
        P("replica"),
        P("replica"),
        P(None, "replica", "tp"),
        P("replica", None, "tp"),
        P("replica", None, "tp"),
    )
    return jax.shard_map(
        shards,
        mesh=mesh,
        in_specs=placed,
        out_specs=(P(None, "replica", "tp"), P(None, "replica", "tp"), P(None, "replica", "tp")),
        check_vma=False,
    )
```

```python
import functools
import math

import jax
import jax.numpy as jnp
import numpy as np
from jax import lax
from jax.experimental import pallas as pl
from jax.experimental.pallas import tpu as pltpu
from jax.sharding import PartitionSpec as P

HD = 128
GROUP = 8
EPS = 1e-05
THETA = 500000.0
NEG = -1e30
MESH = pl.DeviceIdType.MESH
F32 = jnp.float32
BF16 = jnp.bfloat16
SENT = 32
NT = (((1,), (1,)), ((), ()))


def iota(shape, dim):
    return lax.broadcasted_iota(jnp.int32, shape, dim)


def kernel(
    nr,
    nt,
    f_hbm,
    gain_hbm,
    place_hbm,
    need_hbm,
    ra_hbm,
    len_s_hbm,
    len_hbm,
    freq_hbm,
    q_hbm,
    wk_hbm,
    wv_hbm,
    pa_hbm,
    pb_hbm,
    ck_hbm,
    cv_hbm,
    att_ref,
    nk_ref,
    nv_ref,
    f_ref,
    gain_ref,
    place_ref,
    need_ref,
    ra_ref,
    len_s,
    len_ref,
    freq_ref,
    q_in,
    q_wide,
    q_ref,
    wbuf,
    pa,
    pb,
    pbt,
    ck,
    cv,
    stats,
    msg,
    wide_rows,
    got,
    xall,
    ring,
    part,
    rs_got,
    coeff,
    expand,
    ret_send,
    ret_got,
    scores,
    weights,
    fresh_w,
    acc_kv,
    att_acc,
    top_ref,
    bottom_ref,
    cos_ref,
    sin_ref,
    small_sem,
    load_sem,
    st_send,
    st_recv,
    a2a_send,
    a2a_recv,
    ring_send,
    ring_recv,
    rs_send,
    rs_recv,
    ag_send,
    ag_recv,
    re_send,
    re_recv,
):
    r = lax.axis_index("replica")
    t = lax.axis_index("tp")
    rows2, width = f_ref.shape
    rows = rows2 // 2
    need_count = need_ref.shape[0]
    adapters = place_ref.shape[1]
    pool = adapters // nr
    rank = part.shape[1] * nt
    kpart = rank // nt
    nvis = nr * 4
    ntot = nvis + rows2

    small = [
        pltpu.make_async_copy(a, b, small_sem.at[k])
        for k, (a, b) in enumerate(
            [
                (ra_hbm, ra_ref),
                (need_hbm, need_ref),
                (place_hbm, place_ref),
                (gain_hbm, gain_ref),
                (f_hbm, f_ref),
                (len_s_hbm, len_s),
                (len_hbm, len_ref),
                (freq_hbm, freq_ref),
                (q_hbm, q_in),
            ]
        )
    ]
    loads = [
        pltpu.make_async_copy(ck_hbm, ck, load_sem.at[0]),
        pltpu.make_async_copy(pa_hbm, pa, load_sem.at[1]),
        pltpu.make_async_copy(wk_hbm, wbuf.at[:, pl.ds(0, HD)], load_sem.at[2]),
        pltpu.make_async_copy(wv_hbm, wbuf.at[:, pl.ds(HD, HD)], load_sem.at[3]),
        pltpu.make_async_copy(pb_hbm, pb, load_sem.at[4]),
        pltpu.make_async_copy(cv_hbm, cv, load_sem.at[5]),
    ]
    for load in small:
        load.start()

    barrier = pltpu.get_barrier_semaphore()

    @pl.loop(1, nr)
    def _(k):
        pl.semaphore_signal(
            barrier, inc=1, device_id=(lax.rem(r + k, nr), t), device_id_type=MESH
        )

    @pl.loop(1, nt)
    def _(k):
        pl.semaphore_signal(
            barrier, inc=1, device_id=(r, lax.rem(t + k, nt)), device_id_type=MESH
        )

    for load in loads:
        load.start()

    for load in small[:3]:
        load.wait()
    ra = ra_ref[...]
    need = need_ref[...]
    mine = jnp.sum(
        jnp.where(iota(need.shape, 1) == r, need, 0).astype(F32), axis=1, keepdims=True
    )
    entry = iota((need_count, rows), 0) == ra
    wanted = jnp.sum(jnp.where(entry, mine, 0.0), axis=0, keepdims=True)
    place = place_ref[...]
    home = place // pool
    local = place - home * pool
    at_me = jnp.where(home == r, local + 1, 0)
    table = jnp.concatenate(
        [
            jnp.broadcast_to(x.astype(F32), (8, adapters))
            for x in (home, local, at_me)
        ],
        axis=0,
    ).astype(BF16)
    which = iota((adapters, rows), 0) == wanted.astype(jnp.int32)
    found = jnp.dot(
        table, jnp.where(which, 1.0, 0.0).astype(BF16), preferred_element_type=F32
    )
    owner = found[0:1].astype(jnp.int32)
    eye_r = iota((rows, rows), 0) == iota((rows, rows), 1)
    ra_f = ra.astype(F32)
    ra_col = jnp.sum(jnp.where(eye_r, ra_f, 0.0), axis=1, keepdims=True)
    twin = (ra_col == ra_f) & (iota((rows, rows), 0) < iota((rows, rows), 1))
    turn = jnp.sum(jnp.where(twin, 1.0, 0.0), axis=0, keepdims=True).astype(jnp.int32)
    is_far = ra < need_count
    code = jnp.where(is_far, owner * 4 + turn * 2, -1000)
    code2 = jnp.concatenate([code, code + 1], axis=1)
    pick = jnp.where(iota((nvis, rows2), 0) == code2, 1.0, 0.0).astype(BF16)

    small[3].wait()
    small[4].wait()
    gain_rows = gain_ref[...].astype(F32)
    f32 = f_ref[...].astype(F32)
    lanes = HD
    chunks = width // lanes
    eye = iota((rows2, lanes), 0) == iota((rows2, lanes), 1)
    square_sum = jnp.sum(f32 * f32, axis=1, keepdims=True)
    square_row = jnp.sum(jnp.where(eye, square_sum, 0.0), axis=0, keepdims=True)
    stats[t] = jnp.concatenate(
        [gain_rows, jnp.broadcast_to(square_row, (8, lanes))], axis=0
    )
    own = jnp.concatenate(
        [
            f32[:, c * lanes : (c + 1) * lanes] * gain_rows[c : c + 1]
            for c in range(chunks)
        ],
        axis=1,
    ).astype(BF16)
    xall[pl.ds(nvis, rows2), :] = own

    picked_rows = jnp.dot(pick, own, preferred_element_type=F32)
    for j in range(chunks):
        wide_rows[pl.ds(j, nvis, stride=chunks), :] = picked_rows[
            :, j * lanes : (j + 1) * lanes
        ]
    msg[...] = wide_rows[...].astype(BF16)
    got[pl.ds(pl.multiple_of(r * SENT, SENT), SENT), :] = jnp.zeros((SENT, HD), BF16)
    ret_got[pl.ds(pl.multiple_of(r * 8, 8), 8), :] = jnp.zeros((8, HD), F32)

    pl.semaphore_wait(barrier, nr - 1 + nt - 1)

    right = (r, lax.rem(t + 1, nt))
    left = (r, lax.rem(t + nt - 1, nt))
    half = nt // 2

    def hop(which_way, h, c):
        if which_way == 0:
            have, there, to = (nt - (h - 1)) % nt, nt - h, right
        else:
            have, there, to = h - 1, h, left
        piece = pl.ds(c * rows, rows)
        src = f_ref.at[piece, :] if have == 0 else ring.at[have, piece, :]
        return pltpu.make_async_remote_copy(
            src_ref=src,
            dst_ref=ring.at[there, piece, :],
            send_sem=ring_send.at[which_way, h - 1, c],
            recv_sem=ring_recv.at[there, c],
            device_id=to,
            device_id_type=MESH,
        )

    def hops(h):
        if h < half:
            return [(0, 0), (1, 0), (0, 1), (1, 1)]
        return [(0, 0), (1, 1)]

    @pl.loop(1, nr)
    def _(k):
        to = lax.rem(r + k, nr)
        pltpu.make_async_remote_copy(
            src_ref=msg.at[pl.ds(pl.multiple_of(to * SENT, SENT), SENT), :],
            dst_ref=got.at[pl.ds(pl.multiple_of(r * SENT, SENT), SENT), :],
            send_sem=a2a_send,
            recv_sem=a2a_recv,
            device_id=(to, t),
            device_id_type=MESH,
        ).start()

    for way, c in hops(1):
        hop(way, 1, c).start()

    @pl.loop(1, nt)
    def _(k):
        pltpu.make_async_remote_copy(
            src_ref=stats.at[t],
            dst_ref=stats.at[t],
            send_sem=st_send,
            recv_sem=st_recv,
            device_id=(r, lax.rem(t + k, nt)),
            device_id_type=MESH,
        ).start()

    def wait_bytes(ref, sem):
        pltpu.make_async_copy(ref, ref, sem).wait()

    asked = jnp.zeros((adapters, nr), jnp.bool_)
    p_iota = iota((adapters, nr), 0)
    for e in range(need_count):
        asked = asked | (p_iota == need[e : e + 1, :])
    visit = jnp.dot(
        table, jnp.where(asked, 1.0, 0.0).astype(BF16), preferred_element_type=F32
    )[16:24]
    spread = jnp.where(iota((nr, nvis), 1) // 4 == iota((nr, nvis), 0), 1.0, 0.0)
    visit_slot = jnp.dot(
        visit.astype(BF16), spread.astype(BF16), preferred_element_type=F32
    )[0:1].astype(jnp.int32) - 1
    own_slot = jnp.where(is_far, -1, ra - need_count)
    slot_row = jnp.concatenate([visit_slot, own_slot, own_slot], axis=1)

    scale = 1.0 / math.sqrt(HD)
    cache_len = ck.shape[1]
    per_row = 2 * GROUP

    def cached_scores(lo, hi):
        @pl.loop(lo, hi, unroll=4)
        def _(i):
            s = (
                lax.dot_general(q_ref[i], ck[i], NT, preferred_element_type=F32) * scale
            )
            live = iota(s.shape, 1) < len_s[i]
            scores[i] = jnp.where(live, s, NEG)

    def ring_stage(h, which_chunks=(0, 1)):
        for way, c in hops(h):
            if c not in which_chunks:
                continue
            hop(way, h, c).wait_recv()
            if (way, c) in (hops(h + 1) if h < half else []):
                hop(way, h + 1, c).start()

    for load in small[5:]:
        load.wait()
    for step in range(2):
        for g in range(GROUP):
            q_wide[pl.ds(step * GROUP + g, rows, stride=per_row), :] = q_in[
                step * rows : (step + 1) * rows, g * HD : (g + 1) * HD
            ].astype(F32)
    q_ref[...] = q_wide[...].astype(BF16).reshape(rows, per_row, HD)
    loads[0].wait()
    cached_scores(0, rows // 4)
    ring_stage(1, (0,))
    cached_scores(rows // 4, rows // 2)
    ring_stage(1, (1,))

    loads[1].wait()
    wait_bytes(got.at[pl.ds(0, (nr - 1) * SENT), :], a2a_recv)
    wide_rows[...] = got[...].astype(F32)
    for j in range(chunks):
        xall[pl.ds(0, nvis), j * lanes : (j + 1) * lanes] = wide_rows[
            pl.ds(j, nvis, stride=chunks), :
        ].astype(BF16)
    x = xall[...]
    group = 8
    part[...] = jnp.zeros(part.shape, F32)

    @pl.loop(0, pool // group)
    def _(g):
        base = g * group
        block = lax.dot_general(
            pa[pl.ds(pl.multiple_of(base * rank, group * rank), group * rank), :],
            x,
            NT,
            preferred_element_type=F32,
        )
        picked = jnp.zeros((rank, ntot), F32)
        for s in range(group):
            picked += jnp.where(
                slot_row == base + s, block[s * rank : (s + 1) * rank], 0.0
            )
        part[:, :, pl.ds(0, ntot)] += picked.reshape(nt, kpart, ntot)

    @pl.loop(1, nt)
    def _(k):
        to = lax.rem(t + k, nt)
        pltpu.make_async_remote_copy(
            src_ref=part.at[to],
            dst_ref=rs_got.at[t],
            send_sem=rs_send,
            recv_sem=rs_recv,
            device_id=(r, to),
            device_id_type=MESH,
        ).start()

    cached_scores(rows // 2, rows)

    qrows = 8
    span = qrows * per_row
    for b in range(rows // qrows):
        s = scores[b * qrows : (b + 1) * qrows].reshape(span, cache_len)
        top = jnp.max(s, axis=1, keepdims=True)
        e_cache = jnp.exp(s - top)
        top_ref[b * span : (b + 1) * span, :] = top
        bottom_ref[b * span : (b + 1) * span, :] = jnp.sum(
            e_cache, axis=1, keepdims=True
        )
        weights[b * qrows : (b + 1) * qrows] = e_cache.astype(BF16).reshape(
            qrows, per_row, cache_len
        )

    wait_bytes(rs_got.at[pl.ds(0, nt - 1)], rs_recv)
    whole = part[t]
    for k in range(nt):
        whole += jnp.where(k == t, 0.0, rs_got[k])
    coeff[t] = whole

    @pl.loop(1, nt)
    def _(k):
        pltpu.make_async_remote_copy(
            src_ref=coeff.at[t],
            dst_ref=coeff.at[t],
            send_sem=ag_send,
            recv_sem=ag_recv,
            device_id=(r, lax.rem(t + k, nt)),
            device_id_type=MESH,
        ).start()

    if half > 2:
        ring_stage(2)

    wait_bytes(stats.at[pl.ds(0, nt - 1)], st_recv)
    square = stats[0, 8:16, :]
    for k in range(1, nt):
        square += stats[k, 8:16, :]
    inverse_row = lax.rsqrt(square[0:1] / (width * nt) + EPS)
    inverse = jnp.sum(jnp.where(eye, inverse_row, 0.0), axis=1, keepdims=True)

    def project(o):
        source = lax.rem(t + o, nt)
        block = f_ref[...] if o == 0 else ring[o]
        block = block.astype(F32) * inverse
        gains = stats[source][0:8]
        normed = jnp.concatenate(
            [
                block[:, c * lanes : (c + 1) * lanes] * gains[c : c + 1]
                for c in range(chunks)
            ],
            axis=1,
        ).astype(BF16)
        w = wbuf[pl.ds(pl.multiple_of(source * width, width), width), :]
        product = jnp.dot(normed, w, preferred_element_type=F32)
        if o == 0:
            acc_kv[...] = product
        else:
            acc_kv[...] += product

    loads[2].wait()
    loads[3].wait()
    project(0)
    project(nt - 1)
    if half > 1:
        project(1)

    length_row = len_ref[...].astype(F32)
    positions = jnp.sum(
        jnp.where(eye_r, length_row, 0.0), axis=1, keepdims=True
    )
    positions = jnp.concatenate([positions, positions + 1.0], axis=0)
    angle = positions * freq_ref[...]
    sign = jnp.where(iota((rows2, HD), 1) < HD // 2, -1.0, 1.0)
    cos_ref[...] = jnp.cos(angle)
    sin_ref[...] = jnp.sin(angle) * sign

    loads[4].wait()
    pbt[...] = pb[...].T

    wait_bytes(coeff.at[pl.ds(0, nt - 1)], ag_recv)
    coeffs = coeff[...].reshape(rank, coeff.shape[2])[:, 0:ntot]
    for s in range(pool):
        expand[s * rank : (s + 1) * rank, :] = jnp.where(
            slot_row == s, coeffs, 0.0
        ).astype(BF16)
    delta = jnp.dot(pbt[...], expand[...], preferred_element_type=F32).T
    ret_send[...] = delta[0:nvis]
    own_delta = delta[nvis:ntot]

    @pl.loop(1, nr)
    def _(k):
        to = lax.rem(r + k, nr)
        pltpu.make_async_remote_copy(
            src_ref=ret_send.at[pl.ds(pl.multiple_of(to // 2 * 8, 8), 8), :],
            dst_ref=ret_got.at[pl.ds(pl.multiple_of(r * 8, 8), 8), :],
            send_sem=re_send,
            recv_sem=re_recv,
            device_id=(to, t),
            device_id_type=MESH,
        ).start()

    for h in range(3, half):
        ring_stage(h)
        project(nt - h + 1)
        project(h - 1)

    loads[5].wait()

    @pl.loop(0, rows, unroll=4)
    def _(i):
        att_acc[pl.ds(pl.multiple_of(i * per_row, per_row), per_row), :] = jnp.dot(
            weights[i], cv[i], preferred_element_type=F32
        )

    if half > 2:
        project(nt - half + 1)
        project(half - 1)
    ring_stage(half)
    project(half)

    key = acc_kv[:, 0:HD]
    turned = key * cos_ref[...] + pltpu.roll(key, HD // 2, 1) * sin_ref[...]
    new_keys = turned.astype(BF16)
    nk_ref[...] = new_keys

    for b in range(rows // qrows):
        part_rows = slice(b * span, (b + 1) * span)
        q = q_ref[b * qrows : (b + 1) * qrows].reshape(span, HD)
        fresh = (
            lax.dot_general(q, new_keys, NT, preferred_element_type=F32) * scale
        )
        row_of = iota(fresh.shape, 0) // per_row + b * qrows
        step_of = iota(fresh.shape, 0) % per_row // GROUP
        column = iota(fresh.shape, 1)
        seen = (column == row_of) | ((column == row_of + rows) & (step_of == 1))
        fresh = jnp.where(seen, fresh, NEG)
        cache_top = top_ref[part_rows, :]
        top = jnp.maximum(cache_top, jnp.max(fresh, axis=1, keepdims=True))
        shrink = jnp.exp(cache_top - top)
        e_fresh = jnp.exp(fresh - top)
        bottom = bottom_ref[part_rows, :] * shrink + jnp.sum(
            e_fresh, axis=1, keepdims=True
        )
        share = 1.0 / bottom
        fresh_w[part_rows, :] = (e_fresh * share).astype(BF16)
        att_acc[part_rows, :] = att_acc[part_rows, :] * (shrink * share)

    code_f = jnp.where(
        is_far, owner * 8 + lax.rem(r, 2) * 4 + turn * 2, -1000
    ).astype(F32)
    code_col = jnp.sum(jnp.where(eye_r, code_f, 0.0), axis=1, keepdims=True)
    code_col = jnp.concatenate([code_col, code_col + 1.0], axis=0).astype(jnp.int32)
    back = jnp.where(iota((rows2, nr * 8), 1) == code_col, 1.0, 0.0).astype(BF16)
    wait_bytes(ret_got.at[pl.ds(0, (nr - 1) * 8), :], re_recv)
    returned = ret_got[...]
    high = returned.astype(BF16)
    low = (returned - high.astype(F32)).astype(BF16)
    far_delta = jnp.dot(back, high, preferred_element_type=F32) + jnp.dot(
        back, low, preferred_element_type=F32
    )
    new_values = (acc_kv[:, HD : 2 * HD] + inverse * (far_delta + own_delta)).astype(
        BF16
    )
    nv_ref[...] = new_values
    att_acc[...] += jnp.dot(fresh_w[...], new_values, preferred_element_type=F32)
    for step in range(2):
        for g in range(GROUP):
            att_ref[step * rows : (step + 1) * rows, g * HD : (g + 1) * HD] = att_acc[
                pl.ds(step * GROUP + g, rows, stride=per_row), :
            ].astype(BF16)

    for h in range(1, half + 1):
        for way, c in hops(h):
            hop(way, h, c).wait_send()
    wait_bytes(stats.at[pl.ds(0, nt - 1)], st_send)
    wait_bytes(msg.at[pl.ds(0, (nr - 1) * SENT), :], a2a_send)
    wait_bytes(part.at[pl.ds(0, nt - 1)], rs_send)
    wait_bytes(coeff.at[pl.ds(0, nt - 1)], ag_send)
    wait_bytes(ret_got.at[pl.ds(0, (nr - 1) * 8), :], re_send)


def write_out(a, b, c, a_out, b_out, c_out, sem):
    copies = [
        pltpu.make_async_copy(src, dst, sem.at[k])
        for k, (src, dst) in enumerate([(a, a_out), (b, b_out), (c, c_out)])
    ]
    for copy in copies:
        copy.start()
    for copy in copies:
        copy.wait()


def shards(
    features,
    gain,
    w_key,
    w_value,
    pool_a,
    pool_b,
    placement,
    need_lists,
    row_adapter,
    lengths,
    queries,
    cache_k,
    cache_v,
):
    nr, nt = lax.axis_size("replica"), lax.axis_size("tp")
    steps, rows, width = features.shape
    pool, _, rank = pool_a.shape
    cache_len = cache_k.shape[1]
    rows2 = steps * rows
    nvis = nr * 4
    ntot = nvis + rows2
    ntot_pad = -(-ntot // HD) * HD
    per_row = steps * GROUP
    half = HD // 2
    frequency = np.float32(THETA) ** (-(np.arange(half, dtype=np.float32) * 2.0) / HD)
    frequency = np.concatenate([frequency, frequency]).astype(np.float32)[None, :]
    vmem = pl.BlockSpec(memory_space=pltpu.VMEM)
    hbm = pl.BlockSpec(memory_space=pltpu.HBM)
    dma = pltpu.SemaphoreType.DMA
    att, nk, nv = pl.pallas_call(
        functools.partial(kernel, nr, nt),
        out_shape=(
            jax.ShapeDtypeStruct((rows2, width), BF16),
            jax.ShapeDtypeStruct((rows2, HD), BF16),
            jax.ShapeDtypeStruct((rows2, HD), BF16),
        ),
        in_specs=[hbm] * 15,
        out_specs=(vmem, vmem, vmem),
        scratch_shapes=[
            pltpu.VMEM((rows2, width), BF16),
            pltpu.VMEM((width // HD, HD), BF16),
            pltpu.VMEM((1, placement.shape[0]), jnp.int32),
            pltpu.VMEM(need_lists.shape[::-1], jnp.int32),
            pltpu.VMEM((1, rows), jnp.int32),
            pltpu.SMEM((rows,), jnp.int32),
            pltpu.VMEM((1, rows), jnp.int32),
            pltpu.VMEM((1, HD), F32),
            pltpu.VMEM((rows2, width), BF16),
            pltpu.VMEM((rows * per_row, HD), F32),
            pltpu.VMEM((rows, per_row, HD), BF16),
            pltpu.VMEM((nt * width, 2 * HD), BF16),
            pltpu.VMEM((pool * rank, width), BF16),
            pltpu.VMEM((pool * rank, HD), BF16),
            pltpu.VMEM((HD, pool * rank), BF16),
            pltpu.VMEM((rows, cache_len, HD), BF16),
            pltpu.VMEM((rows, cache_len, HD), BF16),
            pltpu.VMEM((nt, 16, HD), F32),
            pltpu.VMEM((nr * SENT, HD), BF16),
            pltpu.VMEM((nr * SENT, HD), F32),
            pltpu.VMEM((nr * SENT, HD), BF16),
            pltpu.VMEM((ntot, width), BF16),
            pltpu.VMEM((nt, rows2, width), BF16),
            pltpu.VMEM((nt, rank // nt, ntot_pad), F32),
            pltpu.VMEM((nt, rank // nt, ntot_pad), F32),
            pltpu.VMEM((nt, rank // nt, ntot_pad), F32),
            pltpu.VMEM((pool * rank, ntot), BF16),
            pltpu.VMEM((nvis, HD), F32),
            pltpu.VMEM((nr * 8, HD), F32),
            pltpu.VMEM((rows, per_row, cache_len), F32),
            pltpu.VMEM((rows, per_row, cache_len), BF16),
            pltpu.VMEM((rows * per_row, rows2), BF16),
            pltpu.VMEM((rows2, 2 * HD), F32),
            pltpu.VMEM((rows * per_row, HD), F32),
            pltpu.VMEM((rows * per_row, 1), F32),
            pltpu.VMEM((rows * per_row, 1), F32),
            pltpu.VMEM((rows2, HD), F32),
            pltpu.VMEM((rows2, HD), F32),
            dma((9,)),
            dma((6,)),
            dma,
            dma,
            dma,
            dma,
            dma((2, max(nt // 2, 1), 2)),
            dma((nt, 2)),
            dma,
            dma,
            dma,
            dma,
            dma,
            dma,
        ],
        compiler_params=pltpu.CompilerParams(
            collective_id=0, has_side_effects=True, vmem_limit_bytes=60 * 2**20
        ),
        cost_estimate=pl.CostEstimate(
            flops=2 * 64 * 8192 * 256, bytes_accessed=12 * 2**20, transcendentals=0
        ),
    )(
        features.reshape(rows2, width),
        gain.reshape(width // HD, HD),
        placement.reshape(1, -1),
        need_lists.T,
        row_adapter.reshape(1, rows),
        lengths,
        lengths.reshape(1, rows),
        jnp.asarray(frequency),
        queries.reshape(rows2, width),
        w_key,
        w_value,
        pool_a.swapaxes(1, 2).reshape(pool * rank, width),
        pool_b.reshape(pool * rank, HD),
        cache_k,
        cache_v,
    )
    shapes = tuple(jax.ShapeDtypeStruct(x.shape, BF16) for x in (att, nk, nv))
    att, nk, nv = pl.pallas_call(
        write_out,
        out_shape=shapes,
        in_specs=[vmem] * 3,
        out_specs=(hbm,) * 3,
        scratch_shapes=[dma((3,))],
        compiler_params=pltpu.CompilerParams(vmem_limit_bytes=60 * 2**20),
    )(att, nk, nv)
    return (
        att.reshape(steps, rows, width),
        nk.reshape(steps, rows, HD),
        nv.reshape(steps, rows, HD),
    )


def solution(mesh):
    placed = (
        P(None, "replica", "tp"),
        P("tp"),
        P(None, "tp"),
        P(None, "tp"),
        P("replica", "tp", None),
        P("replica", None, "tp"),
        P(),
        P(),
        P("replica"),
        P("replica"),
        P(None, "replica", "tp"),
        P("replica", None, "tp"),
        P("replica", None, "tp"),
    )
    return jax.shard_map(
        shards,
        mesh=mesh,
        in_specs=placed,
        out_specs=(P(None, "replica", "tp"), P(None, "replica", "tp"), P(None, "replica", "tp")),
        check_vma=False,
    )
```

```python
import functools
import math

import jax
import jax.numpy as jnp
import numpy as np
from jax import lax
from jax.experimental import pallas as pl
from jax.experimental.pallas import tpu as pltpu
from jax.sharding import PartitionSpec as P

HD = 128
GROUP = 8
EPS = 1e-05
THETA = 500000.0
NEG = -1e30
MESH = pl.DeviceIdType.MESH
F32 = jnp.float32
BF16 = jnp.bfloat16
SENT = 32
NT = (((1,), (1,)), ((), ()))


def iota(shape, dim):
    return lax.broadcasted_iota(jnp.int32, shape, dim)


def kernel(
    nr,
    nt,
    f_hbm,
    gain_hbm,
    place_hbm,
    need_hbm,
    ra_hbm,
    len_s_hbm,
    len_hbm,
    freq_hbm,
    q_hbm,
    wk_hbm,
    wv_hbm,
    pa_hbm,
    pb_hbm,
    ck_hbm,
    cv_hbm,
    att_ref,
    nk_ref,
    nv_ref,
    f_ref,
    gain_ref,
    place_ref,
    need_ref,
    ra_ref,
    len_s,
    len_ref,
    freq_ref,
    q_in,
    q_wide,
    q_ref,
    wbuf,
    pa,
    pb,
    pbt,
    ck,
    cv,
    stats,
    msg,
    wide_rows,
    got,
    xall,
    ring,
    part,
    rs_got,
    coeff,
    expand,
    ret_send,
    ret_got,
    scores,
    weights,
    fresh_w,
    acc_kv,
    att_acc,
    top_ref,
    bottom_ref,
    cos_ref,
    sin_ref,
    small_sem,
    load_sem,
    st_send,
    st_recv,
    a2a_send,
    a2a_recv,
    ring_send,
    ring_recv,
    rs_send,
    rs_recv,
    ag_send,
    ag_recv,
    re_send,
    re_recv,
):
    r = lax.axis_index("replica")
    t = lax.axis_index("tp")
    rows2, width = f_ref.shape
    rows = rows2 // 2
    need_count = need_ref.shape[0]
    adapters = place_ref.shape[1]
    pool = adapters // nr
    rank = part.shape[1] * nt
    kpart = rank // nt
    nvis = nr * 4
    ntot = nvis + rows2

    small = [
        pltpu.make_async_copy(a, b, small_sem.at[k])
        for k, (a, b) in enumerate(
            [
                (ra_hbm, ra_ref),
                (need_hbm, need_ref),
                (place_hbm, place_ref),
                (gain_hbm, gain_ref),
                (f_hbm, f_ref),
                (len_s_hbm, len_s),
                (len_hbm, len_ref),
                (freq_hbm, freq_ref),
                (q_hbm, q_in),
            ]
        )
    ]
    loads = [
        pltpu.make_async_copy(ck_hbm, ck, load_sem.at[0]),
        pltpu.make_async_copy(pa_hbm, pa, load_sem.at[1]),
        pltpu.make_async_copy(wk_hbm, wbuf.at[:, pl.ds(0, HD)], load_sem.at[2]),
        pltpu.make_async_copy(wv_hbm, wbuf.at[:, pl.ds(HD, HD)], load_sem.at[3]),
        pltpu.make_async_copy(pb_hbm, pb, load_sem.at[4]),
        pltpu.make_async_copy(cv_hbm, cv, load_sem.at[5]),
    ]
    for load in small:
        load.start()

    barrier = pltpu.get_barrier_semaphore()

    @pl.loop(1, nr)
    def _(k):
        pl.semaphore_signal(
            barrier, inc=1, device_id=(lax.rem(r + k, nr), t), device_id_type=MESH
        )

    @pl.loop(1, nt)
    def _(k):
        pl.semaphore_signal(
            barrier, inc=1, device_id=(r, lax.rem(t + k, nt)), device_id_type=MESH
        )

    for load in loads:
        load.start()

    for load in small[:3]:
        load.wait()
    ra = ra_ref[...]
    need = need_ref[...]
    mine = jnp.sum(
        jnp.where(iota(need.shape, 1) == r, need, 0).astype(F32), axis=1, keepdims=True
    )
    entry = iota((need_count, rows), 0) == ra
    wanted = jnp.sum(jnp.where(entry, mine, 0.0), axis=0, keepdims=True)
    place = place_ref[...]
    home = place // pool
    local = place - home * pool
    at_me = jnp.where(home == r, local + 1, 0)
    table = jnp.concatenate(
        [
            jnp.broadcast_to(x.astype(F32), (8, adapters))
            for x in (home, local, at_me)
        ],
        axis=0,
    ).astype(BF16)
    which = iota((adapters, rows), 0) == wanted.astype(jnp.int32)
    found = jnp.dot(
        table, jnp.where(which, 1.0, 0.0).astype(BF16), preferred_element_type=F32
    )
    owner = found[0:1].astype(jnp.int32)
    eye_r = iota((rows, rows), 0) == iota((rows, rows), 1)
    ra_f = ra.astype(F32)
    ra_col = jnp.sum(jnp.where(eye_r, ra_f, 0.0), axis=1, keepdims=True)
    twin = (ra_col == ra_f) & (iota((rows, rows), 0) < iota((rows, rows), 1))
    turn = jnp.sum(jnp.where(twin, 1.0, 0.0), axis=0, keepdims=True).astype(jnp.int32)
    is_far = ra < need_count
    code = jnp.where(is_far, owner * 4 + turn * 2, -1000)
    code2 = jnp.concatenate([code, code + 1], axis=1)
    pick = jnp.where(iota((nvis, rows2), 0) == code2, 1.0, 0.0).astype(BF16)

    small[3].wait()
    small[4].wait()
    pl.semaphore_wait(barrier, nr - 1 + nt - 1)
    right = (r, lax.rem(t + 1, nt))
    left = (r, lax.rem(t + nt - 1, nt))
    half = nt // 2

    def hop(which_way, h, c):
        if which_way == 0:
            have, there, to = (nt - (h - 1)) % nt, nt - h, right
        else:
            have, there, to = h - 1, h, left
        piece = pl.ds(c * rows, rows)
        src = f_ref.at[piece, :] if have == 0 else ring.at[have, piece, :]
        return pltpu.make_async_remote_copy(
            src_ref=src,
            dst_ref=ring.at[there, piece, :],
            send_sem=ring_send.at[which_way, h - 1, c],
            recv_sem=ring_recv.at[there, c],
            device_id=to,
            device_id_type=MESH,
        )

    def hops(h):
        if h < half:
            return [(0, 0), (1, 0), (0, 1), (1, 1)]
        return [(0, 0), (1, 1)]

    for way, c in hops(1):
        hop(way, 1, c).start()

    gain_rows = gain_ref[...].astype(F32)
    f32 = f_ref[...].astype(F32)
    lanes = HD
    chunks = width // lanes
    eye = iota((rows2, lanes), 0) == iota((rows2, lanes), 1)
    square_sum = jnp.sum(f32 * f32, axis=1, keepdims=True)
    square_row = jnp.sum(jnp.where(eye, square_sum, 0.0), axis=0, keepdims=True)
    stats[t] = jnp.concatenate(
        [gain_rows, jnp.broadcast_to(square_row, (8, lanes))], axis=0
    )
    own = jnp.concatenate(
        [
            f32[:, c * lanes : (c + 1) * lanes] * gain_rows[c : c + 1]
            for c in range(chunks)
        ],
        axis=1,
    ).astype(BF16)
    xall[pl.ds(nvis, rows2), :] = own

    picked_rows = jnp.dot(pick, own, preferred_element_type=F32)
    for j in range(chunks):
        wide_rows[pl.ds(j, nvis, stride=chunks), :] = picked_rows[
            :, j * lanes : (j + 1) * lanes
        ]
    msg[...] = wide_rows[...].astype(BF16)
    got[pl.ds(pl.multiple_of(r * SENT, SENT), SENT), :] = jnp.zeros((SENT, HD), BF16)
    ret_got[pl.ds(pl.multiple_of(r * 8, 8), 8), :] = jnp.zeros((8, HD), F32)

    @pl.loop(1, nr)
    def _(k):
        to = lax.rem(r + k, nr)
        pltpu.make_async_remote_copy(
            src_ref=msg.at[pl.ds(pl.multiple_of(to * SENT, SENT), SENT), :],
            dst_ref=got.at[pl.ds(pl.multiple_of(r * SENT, SENT), SENT), :],
            send_sem=a2a_send,
            recv_sem=a2a_recv,
            device_id=(to, t),
            device_id_type=MESH,
        ).start()

    @pl.loop(1, nt)
    def _(k):
        pltpu.make_async_remote_copy(
            src_ref=stats.at[t],
            dst_ref=stats.at[t],
            send_sem=st_send,
            recv_sem=st_recv,
            device_id=(r, lax.rem(t + k, nt)),
            device_id_type=MESH,
        ).start()

    def wait_bytes(ref, sem):
        pltpu.make_async_copy(ref, ref, sem).wait()

    asked = jnp.zeros((adapters, nr), jnp.bool_)
    p_iota = iota((adapters, nr), 0)
    for e in range(need_count):
        asked = asked | (p_iota == need[e : e + 1, :])
    visit = jnp.dot(
        table, jnp.where(asked, 1.0, 0.0).astype(BF16), preferred_element_type=F32
    )[16:24]
    spread = jnp.where(iota((nr, nvis), 1) // 4 == iota((nr, nvis), 0), 1.0, 0.0)
    visit_slot = jnp.dot(
        visit.astype(BF16), spread.astype(BF16), preferred_element_type=F32
    )[0:1].astype(jnp.int32) - 1
    own_slot = jnp.where(is_far, -1, ra - need_count)
    slot_row = jnp.concatenate([visit_slot, own_slot, own_slot], axis=1)

    scale = 1.0 / math.sqrt(HD)
    cache_len = ck.shape[1]
    per_row = 2 * GROUP

    def cached_scores(lo, hi):
        @pl.loop(lo, hi, unroll=4)
        def _(i):
            s = (
                lax.dot_general(q_ref[i], ck[i], NT, preferred_element_type=F32) * scale
            )
            live = iota(s.shape, 1) < len_s[i]
            scores[i] = jnp.where(live, s, NEG)

    def ring_stage(h, which_chunks=(0, 1)):
        for way, c in hops(h):
            if c not in which_chunks:
                continue
            hop(way, h, c).wait_recv()
            if (way, c) in (hops(h + 1) if h < half else []):
                hop(way, h + 1, c).start()

    for load in small[5:]:
        load.wait()
    for step in range(2):
        for g in range(GROUP):
            q_wide[pl.ds(step * GROUP + g, rows, stride=per_row), :] = q_in[
                step * rows : (step + 1) * rows, g * HD : (g + 1) * HD
            ].astype(F32)
    q_ref[...] = q_wide[...].astype(BF16).reshape(rows, per_row, HD)
    loads[0].wait()
    cached_scores(0, rows // 4)
    ring_stage(1, (0,))
    cached_scores(rows // 4, rows // 2)
    ring_stage(1, (1,))

    loads[1].wait()
    wait_bytes(got.at[pl.ds(0, (nr - 1) * SENT), :], a2a_recv)
    wide_rows[...] = got[...].astype(F32)
    for j in range(chunks):
        xall[pl.ds(0, nvis), j * lanes : (j + 1) * lanes] = wide_rows[
            pl.ds(j, nvis, stride=chunks), :
        ].astype(BF16)
    x = xall[...]
    group = 8
    part[...] = jnp.zeros(part.shape, F32)

    @pl.loop(0, pool // group)
    def _(g):
        base = g * group
        block = lax.dot_general(
            pa[pl.ds(pl.multiple_of(base * rank, group * rank), group * rank), :],
            x,
            NT,
            preferred_element_type=F32,
        )
        picked = jnp.zeros((rank, ntot), F32)
        for s in range(group):
            picked += jnp.where(
                slot_row == base + s, block[s * rank : (s + 1) * rank], 0.0
            )
        part[:, :, pl.ds(0, ntot)] += picked.reshape(nt, kpart, ntot)

    @pl.loop(1, nt)
    def _(k):
        to = lax.rem(t + k, nt)
        pltpu.make_async_remote_copy(
            src_ref=part.at[to],
            dst_ref=rs_got.at[t],
            send_sem=rs_send,
            recv_sem=rs_recv,
            device_id=(r, to),
            device_id_type=MESH,
        ).start()

    if half > 2:
        ring_stage(2, (0,))
    cached_scores(rows // 2, rows)

    qrows = 8
    span = qrows * per_row
    for b in range(rows // qrows):
        s = scores[b * qrows : (b + 1) * qrows].reshape(span, cache_len)
        top = jnp.max(s, axis=1, keepdims=True)
        e_cache = jnp.exp(s - top)
        top_ref[b * span : (b + 1) * span, :] = top
        bottom_ref[b * span : (b + 1) * span, :] = jnp.sum(
            e_cache, axis=1, keepdims=True
        )
        weights[b * qrows : (b + 1) * qrows] = e_cache.astype(BF16).reshape(
            qrows, per_row, cache_len
        )

    if half > 2:
        ring_stage(2, (1,))

    wait_bytes(rs_got.at[pl.ds(0, nt - 1)], rs_recv)
    whole = part[t]
    for k in range(nt):
        whole += jnp.where(k == t, 0.0, rs_got[k])
    coeff[t] = whole

    @pl.loop(1, nt)
    def _(k):
        pltpu.make_async_remote_copy(
            src_ref=coeff.at[t],
            dst_ref=coeff.at[t],
            send_sem=ag_send,
            recv_sem=ag_recv,
            device_id=(r, lax.rem(t + k, nt)),
            device_id_type=MESH,
        ).start()

    wait_bytes(stats.at[pl.ds(0, nt - 1)], st_recv)
    square = stats[0, 8:16, :]
    for k in range(1, nt):
        square += stats[k, 8:16, :]
    inverse_row = lax.rsqrt(square[0:1] / (width * nt) + EPS)
    inverse = jnp.sum(jnp.where(eye, inverse_row, 0.0), axis=1, keepdims=True)

    def project(o):
        source = lax.rem(t + o, nt)
        block = f_ref[...] if o == 0 else ring[o]
        block = block.astype(F32) * inverse
        gains = stats[source][0:8]
        normed = jnp.concatenate(
            [
                block[:, c * lanes : (c + 1) * lanes] * gains[c : c + 1]
                for c in range(chunks)
            ],
            axis=1,
        ).astype(BF16)
        w = wbuf[pl.ds(pl.multiple_of(source * width, width), width), :]
        product = jnp.dot(normed, w, preferred_element_type=F32)
        if o == 0:
            acc_kv[...] = product
        else:
            acc_kv[...] += product

    loads[2].wait()
    loads[3].wait()
    project(0)
    project(nt - 1)
    if half > 1:
        project(1)

    length_row = len_ref[...].astype(F32)
    positions = jnp.sum(
        jnp.where(eye_r, length_row, 0.0), axis=1, keepdims=True
    )
    positions = jnp.concatenate([positions, positions + 1.0], axis=0)
    angle = positions * freq_ref[...]
    sign = jnp.where(iota((rows2, HD), 1) < HD // 2, -1.0, 1.0)
    cos_ref[...] = jnp.cos(angle)
    sin_ref[...] = jnp.sin(angle) * sign

    loads[4].wait()
    pbt[...] = pb[...].T

    for h in range(3, half):
        ring_stage(h)
        project(nt - h + 1)
        project(h - 1)

    wait_bytes(coeff.at[pl.ds(0, nt - 1)], ag_recv)
    coeffs = coeff[...].reshape(rank, coeff.shape[2])[:, 0:ntot]
    for s in range(pool):
        expand[s * rank : (s + 1) * rank, :] = jnp.where(
            slot_row == s, coeffs, 0.0
        ).astype(BF16)
    delta = jnp.dot(pbt[...], expand[...], preferred_element_type=F32).T
    ret_send[...] = delta[0:nvis]
    own_delta = delta[nvis:ntot]

    @pl.loop(1, nr)
    def _(k):
        to = lax.rem(r + k, nr)
        pltpu.make_async_remote_copy(
            src_ref=ret_send.at[pl.ds(pl.multiple_of(to // 2 * 8, 8), 8), :],
            dst_ref=ret_got.at[pl.ds(pl.multiple_of(r * 8, 8), 8), :],
            send_sem=re_send,
            recv_sem=re_recv,
            device_id=(to, t),
            device_id_type=MESH,
        ).start()

    loads[5].wait()

    @pl.loop(0, rows, unroll=4)
    def _(i):
        att_acc[pl.ds(pl.multiple_of(i * per_row, per_row), per_row), :] = jnp.dot(
            weights[i], cv[i], preferred_element_type=F32
        )

    if half > 2:
        project(nt - half + 1)
        project(half - 1)
    ring_stage(half)
    project(half)

    key = acc_kv[:, 0:HD]
    turned = key * cos_ref[...] + pltpu.roll(key, HD // 2, 1) * sin_ref[...]
    new_keys = turned.astype(BF16)
    nk_ref[...] = new_keys

    for b in range(rows // qrows):
        part_rows = slice(b * span, (b + 1) * span)
        q = q_ref[b * qrows : (b + 1) * qrows].reshape(span, HD)
        fresh = (
            lax.dot_general(q, new_keys, NT, preferred_element_type=F32) * scale
        )
        row_of = iota(fresh.shape, 0) // per_row + b * qrows
        step_of = iota(fresh.shape, 0) % per_row // GROUP
        column = iota(fresh.shape, 1)
        seen = (column == row_of) | ((column == row_of + rows) & (step_of == 1))
        fresh = jnp.where(seen, fresh, NEG)
        cache_top = top_ref[part_rows, :]
        top = jnp.maximum(cache_top, jnp.max(fresh, axis=1, keepdims=True))
        shrink = jnp.exp(cache_top - top)
        e_fresh = jnp.exp(fresh - top)
        bottom = bottom_ref[part_rows, :] * shrink + jnp.sum(
            e_fresh, axis=1, keepdims=True
        )
        share = 1.0 / bottom
        fresh_w[part_rows, :] = (e_fresh * share).astype(BF16)
        att_acc[part_rows, :] = att_acc[part_rows, :] * (shrink * share)

    code_f = jnp.where(
        is_far, owner * 8 + lax.rem(r, 2) * 4 + turn * 2, -1000
    ).astype(F32)
    code_col = jnp.sum(jnp.where(eye_r, code_f, 0.0), axis=1, keepdims=True)
    code_col = jnp.concatenate([code_col, code_col + 1.0], axis=0).astype(jnp.int32)
    back = jnp.where(iota((rows2, nr * 8), 1) == code_col, 1.0, 0.0).astype(BF16)
    wait_bytes(ret_got.at[pl.ds(0, (nr - 1) * 8), :], re_recv)
    returned = ret_got[...]
    high = returned.astype(BF16)
    low = (returned - high.astype(F32)).astype(BF16)
    far_delta = jnp.dot(back, high, preferred_element_type=F32) + jnp.dot(
        back, low, preferred_element_type=F32
    )
    new_values = (acc_kv[:, HD : 2 * HD] + inverse * (far_delta + own_delta)).astype(
        BF16
    )
    nv_ref[...] = new_values
    att_acc[...] += jnp.dot(fresh_w[...], new_values, preferred_element_type=F32)
    for step in range(2):
        for g in range(GROUP):
            att_ref[step * rows : (step + 1) * rows, g * HD : (g + 1) * HD] = att_acc[
                pl.ds(step * GROUP + g, rows, stride=per_row), :
            ].astype(BF16)

    for h in range(1, half + 1):
        for way, c in hops(h):
            hop(way, h, c).wait_send()
    wait_bytes(stats.at[pl.ds(0, nt - 1)], st_send)
    wait_bytes(msg.at[pl.ds(0, (nr - 1) * SENT), :], a2a_send)
    wait_bytes(part.at[pl.ds(0, nt - 1)], rs_send)
    wait_bytes(coeff.at[pl.ds(0, nt - 1)], ag_send)
    wait_bytes(ret_got.at[pl.ds(0, (nr - 1) * 8), :], re_send)


def write_out(a, b, c, a_out, b_out, c_out, sem):
    copies = [
        pltpu.make_async_copy(src, dst, sem.at[k])
        for k, (src, dst) in enumerate([(a, a_out), (b, b_out), (c, c_out)])
    ]
    for copy in copies:
        copy.start()
    for copy in copies:
        copy.wait()


def shards(
    features,
    gain,
    w_key,
    w_value,
    pool_a,
    pool_b,
    placement,
    need_lists,
    row_adapter,
    lengths,
    queries,
    cache_k,
    cache_v,
):
    nr, nt = lax.axis_size("replica"), lax.axis_size("tp")
    steps, rows, width = features.shape
    pool, _, rank = pool_a.shape
    cache_len = cache_k.shape[1]
    rows2 = steps * rows
    nvis = nr * 4
    ntot = nvis + rows2
    ntot_pad = -(-ntot // HD) * HD
    per_row = steps * GROUP
    half = HD // 2
    frequency = np.float32(THETA) ** (-(np.arange(half, dtype=np.float32) * 2.0) / HD)
    frequency = np.concatenate([frequency, frequency]).astype(np.float32)[None, :]
    vmem = pl.BlockSpec(memory_space=pltpu.VMEM)
    hbm = pl.BlockSpec(memory_space=pltpu.HBM)
    dma = pltpu.SemaphoreType.DMA
    att, nk, nv = pl.pallas_call(
        functools.partial(kernel, nr, nt),
        out_shape=(
            jax.ShapeDtypeStruct((rows2, width), BF16),
            jax.ShapeDtypeStruct((rows2, HD), BF16),
            jax.ShapeDtypeStruct((rows2, HD), BF16),
        ),
        in_specs=[hbm] * 15,
        out_specs=(vmem, vmem, vmem),
        scratch_shapes=[
            pltpu.VMEM((rows2, width), BF16),
            pltpu.VMEM((width // HD, HD), BF16),
            pltpu.VMEM((1, placement.shape[0]), jnp.int32),
            pltpu.VMEM(need_lists.shape[::-1], jnp.int32),
            pltpu.VMEM((1, rows), jnp.int32),
            pltpu.SMEM((rows,), jnp.int32),
            pltpu.VMEM((1, rows), jnp.int32),
            pltpu.VMEM((1, HD), F32),
            pltpu.VMEM((rows2, width), BF16),
            pltpu.VMEM((rows * per_row, HD), F32),
            pltpu.VMEM((rows, per_row, HD), BF16),
            pltpu.VMEM((nt * width, 2 * HD), BF16),
            pltpu.VMEM((pool * rank, width), BF16),
            pltpu.VMEM((pool * rank, HD), BF16),
            pltpu.VMEM((HD, pool * rank), BF16),
            pltpu.VMEM((rows, cache_len, HD), BF16),
            pltpu.VMEM((rows, cache_len, HD), BF16),
            pltpu.VMEM((nt, 16, HD), F32),
            pltpu.VMEM((nr * SENT, HD), BF16),
            pltpu.VMEM((nr * SENT, HD), F32),
            pltpu.VMEM((nr * SENT, HD), BF16),
            pltpu.VMEM((ntot, width), BF16),
            pltpu.VMEM((nt, rows2, width), BF16),
            pltpu.VMEM((nt, rank // nt, ntot_pad), F32),
            pltpu.VMEM((nt, rank // nt, ntot_pad), F32),
            pltpu.VMEM((nt, rank // nt, ntot_pad), F32),
            pltpu.VMEM((pool * rank, ntot), BF16),
            pltpu.VMEM((nvis, HD), F32),
            pltpu.VMEM((nr * 8, HD), F32),
            pltpu.VMEM((rows, per_row, cache_len), F32),
            pltpu.VMEM((rows, per_row, cache_len), BF16),
            pltpu.VMEM((rows * per_row, rows2), BF16),
            pltpu.VMEM((rows2, 2 * HD), F32),
            pltpu.VMEM((rows * per_row, HD), F32),
            pltpu.VMEM((rows * per_row, 1), F32),
            pltpu.VMEM((rows * per_row, 1), F32),
            pltpu.VMEM((rows2, HD), F32),
            pltpu.VMEM((rows2, HD), F32),
            dma((9,)),
            dma((6,)),
            dma,
            dma,
            dma,
            dma,
            dma((2, max(nt // 2, 1), 2)),
            dma((nt, 2)),
            dma,
            dma,
            dma,
            dma,
            dma,
            dma,
        ],
        compiler_params=pltpu.CompilerParams(
            collective_id=0, has_side_effects=True, vmem_limit_bytes=60 * 2**20
        ),
        cost_estimate=pl.CostEstimate(
            flops=2 * 64 * 8192 * 256, bytes_accessed=12 * 2**20, transcendentals=0
        ),
    )(
        features.reshape(rows2, width),
        gain.reshape(width // HD, HD),
        placement.reshape(1, -1),
        need_lists.T,
        row_adapter.reshape(1, rows),
        lengths,
        lengths.reshape(1, rows),
        jnp.asarray(frequency),
        queries.reshape(rows2, width),
        w_key,
        w_value,
        pool_a.swapaxes(1, 2).reshape(pool * rank, width),
        pool_b.reshape(pool * rank, HD),
        cache_k,
        cache_v,
    )
    shapes = tuple(jax.ShapeDtypeStruct(x.shape, BF16) for x in (att, nk, nv))
    att, nk, nv = pl.pallas_call(
        write_out,
        out_shape=shapes,
        in_specs=[vmem] * 3,
        out_specs=(hbm,) * 3,
        scratch_shapes=[dma((3,))],
        compiler_params=pltpu.CompilerParams(vmem_limit_bytes=60 * 2**20),
    )(att, nk, nv)
    return (
        att.reshape(steps, rows, width),
        nk.reshape(steps, rows, HD),
        nv.reshape(steps, rows, HD),
    )


def solution(mesh):
    placed = (
        P(None, "replica", "tp"),
        P("tp"),
        P(None, "tp"),
        P(None, "tp"),
        P("replica", "tp", None),
        P("replica", None, "tp"),
        P(),
        P(),
        P("replica"),
        P("replica"),
        P(None, "replica", "tp"),
        P("replica", None, "tp"),
        P("replica", None, "tp"),
    )
    return jax.shard_map(
        shards,
        mesh=mesh,
        in_specs=placed,
        out_specs=(P(None, "replica", "tp"), P(None, "replica", "tp"), P(None, "replica", "tp")),
        check_vma=False,
    )
```

```python
import functools
import math

import jax
import jax.numpy as jnp
import numpy as np
from jax import lax
from jax.experimental import pallas as pl
from jax.experimental.pallas import tpu as pltpu
from jax.sharding import PartitionSpec as P

HD = 128
GROUP = 8
EPS = 1e-05
THETA = 500000.0
NEG = -1e30
MESH = pl.DeviceIdType.MESH
F32 = jnp.float32
BF16 = jnp.bfloat16
SENT = 32
NT = (((1,), (1,)), ((), ()))


def iota(shape, dim):
    return lax.broadcasted_iota(jnp.int32, shape, dim)


def kernel(
    nr,
    nt,
    f_hbm,
    gain_hbm,
    place_hbm,
    need_hbm,
    ra_hbm,
    len_s_hbm,
    len_hbm,
    freq_hbm,
    q_hbm,
    wk_hbm,
    wv_hbm,
    pa_hbm,
    pb_hbm,
    ck_hbm,
    cv_hbm,
    att_ref,
    nk_ref,
    nv_ref,
    f_ref,
    gain_ref,
    place_ref,
    need_ref,
    ra_ref,
    len_s,
    len_ref,
    freq_ref,
    q_in,
    q_wide,
    q_ref,
    wbuf,
    pa,
    pb,
    pbt,
    ck,
    cv,
    stats,
    msg,
    wide_rows,
    got,
    xall,
    ring,
    part,
    rs_got,
    coeff,
    expand,
    ret_send,
    ret_got,
    scores,
    weights,
    fresh_w,
    acc_kv,
    att_acc,
    top_ref,
    bottom_ref,
    cos_ref,
    sin_ref,
    small_sem,
    load_sem,
    st_send,
    st_recv,
    a2a_send,
    a2a_recv,
    ring_send,
    ring_recv,
    rs_send,
    rs_recv,
    ag_send,
    ag_recv,
    re_send,
    re_recv,
):
    r = lax.axis_index("replica")
    t = lax.axis_index("tp")
    rows2, width = f_ref.shape
    rows = rows2 // 2
    need_count = need_ref.shape[0]
    adapters = place_ref.shape[1]
    pool = adapters // nr
    rank = part.shape[1] * nt
    kpart = rank // nt
    nvis = nr * 4
    ntot = nvis + rows2
    ntot_pad = part.shape[2]

    small = [
        pltpu.make_async_copy(a, b, small_sem.at[k])
        for k, (a, b) in enumerate(
            [
                (ra_hbm, ra_ref),
                (need_hbm, need_ref),
                (place_hbm, place_ref),
                (gain_hbm, gain_ref),
                (f_hbm, f_ref),
                (len_s_hbm, len_s),
                (len_hbm, len_ref),
                (freq_hbm, freq_ref),
                (q_hbm, q_in),
            ]
        )
    ]
    loads = [
        pltpu.make_async_copy(ck_hbm, ck, load_sem.at[0]),
        pltpu.make_async_copy(pa_hbm, pa, load_sem.at[1]),
        pltpu.make_async_copy(wk_hbm, wbuf.at[:, pl.ds(0, HD)], load_sem.at[2]),
        pltpu.make_async_copy(wv_hbm, wbuf.at[:, pl.ds(HD, HD)], load_sem.at[3]),
        pltpu.make_async_copy(pb_hbm, pb, load_sem.at[4]),
        pltpu.make_async_copy(cv_hbm, cv, load_sem.at[5]),
    ]
    for load in small:
        load.start()

    barrier = pltpu.get_barrier_semaphore()

    @pl.loop(1, nr)
    def _(k):
        pl.semaphore_signal(
            barrier, inc=1, device_id=(lax.rem(r + k, nr), t), device_id_type=MESH
        )

    @pl.loop(1, nt)
    def _(k):
        pl.semaphore_signal(
            barrier, inc=1, device_id=(r, lax.rem(t + k, nt)), device_id_type=MESH
        )

    for load in loads:
        load.start()

    for load in small[:3]:
        load.wait()
    ra = ra_ref[...]
    need = need_ref[...]
    mine = jnp.sum(
        jnp.where(iota(need.shape, 1) == r, need, 0).astype(F32), axis=1, keepdims=True
    )
    entry = iota((need_count, rows), 0) == ra
    wanted = jnp.sum(jnp.where(entry, mine, 0.0), axis=0, keepdims=True)
    place = place_ref[...]
    home = place // pool
    local = place - home * pool
    at_me = jnp.where(home == r, local + 1, 0)
    table = jnp.concatenate(
        [
            jnp.broadcast_to(x.astype(F32), (8, adapters))
            for x in (home, local, at_me)
        ],
        axis=0,
    ).astype(BF16)
    which = iota((adapters, rows), 0) == wanted.astype(jnp.int32)
    found = jnp.dot(
        table, jnp.where(which, 1.0, 0.0).astype(BF16), preferred_element_type=F32
    )
    owner = found[0:1].astype(jnp.int32)
    eye_r = iota((rows, rows), 0) == iota((rows, rows), 1)
    ra_f = ra.astype(F32)
    ra_col = jnp.sum(jnp.where(eye_r, ra_f, 0.0), axis=1, keepdims=True)
    twin = (ra_col == ra_f) & (iota((rows, rows), 0) < iota((rows, rows), 1))
    turn = jnp.sum(jnp.where(twin, 1.0, 0.0), axis=0, keepdims=True).astype(jnp.int32)
    is_far = ra < need_count
    code = jnp.where(is_far, owner * 4 + turn * 2, -1000)
    code2 = jnp.concatenate([code, code + 1], axis=1)
    pick = jnp.where(iota((nvis, rows2), 0) == code2, 1.0, 0.0).astype(BF16)

    small[3].wait()
    small[4].wait()
    pl.semaphore_wait(barrier, nr - 1 + nt - 1)
    right = (r, lax.rem(t + 1, nt))
    left = (r, lax.rem(t + nt - 1, nt))
    half = nt // 2

    def hop(which_way, h, c):
        if which_way == 0:
            have, there, to = (nt - (h - 1)) % nt, nt - h, right
        else:
            have, there, to = h - 1, h, left
        piece = pl.ds(c * rows, rows)
        src = f_ref.at[piece, :] if have == 0 else ring.at[have, piece, :]
        return pltpu.make_async_remote_copy(
            src_ref=src,
            dst_ref=ring.at[there, piece, :],
            send_sem=ring_send.at[which_way, h - 1, c],
            recv_sem=ring_recv.at[there, c],
            device_id=to,
            device_id_type=MESH,
        )

    def hops(h):
        if h < half:
            return [(0, 0), (1, 0), (0, 1), (1, 1)]
        return [(0, 0), (1, 1)]

    for way, c in hops(1):
        hop(way, 1, c).start()

    gain_rows = gain_ref[...].astype(F32)
    f32 = f_ref[...].astype(F32)
    lanes = HD
    chunks = width // lanes
    eye = iota((rows2, lanes), 0) == iota((rows2, lanes), 1)
    square_sum = jnp.sum(f32 * f32, axis=1, keepdims=True)
    square_row = jnp.sum(jnp.where(eye, square_sum, 0.0), axis=0, keepdims=True)
    stats[t] = jnp.concatenate(
        [gain_rows, jnp.broadcast_to(square_row, (8, lanes))], axis=0
    )
    own = jnp.concatenate(
        [
            f32[:, c * lanes : (c + 1) * lanes] * gain_rows[c : c + 1]
            for c in range(chunks)
        ],
        axis=1,
    ).astype(BF16)
    xall[pl.ds(nvis, rows2), :] = own

    picked_rows = jnp.dot(pick, own, preferred_element_type=F32)
    for j in range(chunks):
        wide_rows[pl.ds(j, nvis, stride=chunks), :] = picked_rows[
            :, j * lanes : (j + 1) * lanes
        ]
    msg[...] = wide_rows[...].astype(BF16)
    got[pl.ds(pl.multiple_of(r * SENT, SENT), SENT), :] = jnp.zeros((SENT, HD), BF16)
    ret_got[pl.ds(pl.multiple_of(r * 8, 8), 8), :] = jnp.zeros((8, HD), F32)

    @pl.loop(1, nr)
    def _(k):
        to = lax.rem(r + k, nr)
        pltpu.make_async_remote_copy(
            src_ref=msg.at[pl.ds(pl.multiple_of(to * SENT, SENT), SENT), :],
            dst_ref=got.at[pl.ds(pl.multiple_of(r * SENT, SENT), SENT), :],
            send_sem=a2a_send,
            recv_sem=a2a_recv,
            device_id=(to, t),
            device_id_type=MESH,
        ).start()

    @pl.loop(1, nt)
    def _(k):
        pltpu.make_async_remote_copy(
            src_ref=stats.at[t],
            dst_ref=stats.at[t],
            send_sem=st_send,
            recv_sem=st_recv,
            device_id=(r, lax.rem(t + k, nt)),
            device_id_type=MESH,
        ).start()

    def wait_bytes(ref, sem):
        pltpu.make_async_copy(ref, ref, sem).wait()

    packs = max(1, min(HD // nr, need_count))
    while need_count % packs:
        packs -= 1
    tall = need_count // packs
    packed = jnp.concatenate(
        [need[k * tall : (k + 1) * tall, :] for k in range(packs)], axis=1
    )
    p_iota = iota((adapters, packs * nr), 0)
    asked = p_iota == packed[0:1, :]
    for e in range(1, tall):
        asked = asked | (p_iota == packed[e : e + 1, :])
    visit = jnp.dot(
        table, jnp.where(asked, 1.0, 0.0).astype(BF16), preferred_element_type=F32
    )[16:24]
    wide = (packs * nr, nvis)
    spread = jnp.where(iota(wide, 1) // 4 == iota(wide, 0) % nr, 1.0, 0.0)
    visit_slot = jnp.dot(
        visit.astype(BF16), spread.astype(BF16), preferred_element_type=F32
    )[0:1].astype(jnp.int32) - 1
    own_slot = jnp.where(is_far, -1, ra - need_count)
    slot_row = jnp.concatenate([visit_slot, own_slot, own_slot], axis=1)

    scale = 1.0 / math.sqrt(HD)
    cache_len = ck.shape[1]
    per_row = 2 * GROUP

    def cached_scores(lo, hi):
        @pl.loop(lo, hi, unroll=8)
        def _(i):
            s = (
                lax.dot_general(q_ref[i], ck[i], NT, preferred_element_type=F32) * scale
            )
            live = iota(s.shape, 1) < len_s[i]
            scores[i] = jnp.where(live, s, NEG)

    def ring_stage(h, which_chunks=(0, 1)):
        for way, c in hops(h):
            if c not in which_chunks:
                continue
            hop(way, h, c).wait_recv()
            if (way, c) in (hops(h + 1) if h < half else []):
                hop(way, h + 1, c).start()

    for load in small[5:]:
        load.wait()
    for step in range(2):
        for g in range(GROUP):
            q_wide[pl.ds(step * GROUP + g, rows, stride=per_row), :] = q_in[
                step * rows : (step + 1) * rows, g * HD : (g + 1) * HD
            ].astype(F32)
    q_ref[...] = q_wide[...].astype(BF16).reshape(rows, per_row, HD)
    loads[0].wait()
    cached_scores(0, rows // 4)
    ring_stage(1, (0,))
    cached_scores(rows // 4, rows // 2)
    ring_stage(1, (1,))

    loads[1].wait()
    wait_bytes(got.at[pl.ds(0, (nr - 1) * SENT), :], a2a_recv)
    wide_rows[...] = got[...].astype(F32)
    for j in range(chunks):
        xall[pl.ds(0, nvis), j * lanes : (j + 1) * lanes] = wide_rows[
            pl.ds(j, nvis, stride=chunks), :
        ].astype(BF16)
    x = xall[...]
    group = 8
    picked = jnp.zeros((rank, ntot), F32)
    for base in range(0, pool, group):
        block = lax.dot_general(
            pa[base * rank : (base + group) * rank, :],
            x,
            NT,
            preferred_element_type=F32,
        )
        for s in range(group):
            picked += jnp.where(
                slot_row == base + s, block[s * rank : (s + 1) * rank], 0.0
            )
    if ntot_pad > ntot:
        picked = jnp.concatenate(
            [picked, jnp.zeros((rank, ntot_pad - ntot), F32)], axis=1
        )
    part[...] = picked.reshape(nt, kpart, ntot_pad)

    @pl.loop(1, nt)
    def _(k):
        to = lax.rem(t + k, nt)
        pltpu.make_async_remote_copy(
            src_ref=part.at[to],
            dst_ref=rs_got.at[t],
            send_sem=rs_send,
            recv_sem=rs_recv,
            device_id=(r, to),
            device_id_type=MESH,
        ).start()

    if half > 2:
        ring_stage(2, (0,))
    cached_scores(rows // 2, rows)

    qrows = 8
    span = qrows * per_row
    for b in range(rows // qrows):
        s = scores[b * qrows : (b + 1) * qrows].reshape(span, cache_len)
        top = jnp.max(s, axis=1, keepdims=True)
        e_cache = jnp.exp(s - top)
        top_ref[b * span : (b + 1) * span, :] = top
        bottom_ref[b * span : (b + 1) * span, :] = jnp.sum(
            e_cache, axis=1, keepdims=True
        )
        weights[b * qrows : (b + 1) * qrows] = e_cache.astype(BF16).reshape(
            qrows, per_row, cache_len
        )

    if half > 2:
        ring_stage(2, (1,))

    wait_bytes(rs_got.at[pl.ds(0, nt - 1)], rs_recv)
    whole = part[t]
    for k in range(nt):
        whole += jnp.where(k == t, 0.0, rs_got[k])
    coeff[t] = whole

    @pl.loop(1, nt)
    def _(k):
        pltpu.make_async_remote_copy(
            src_ref=coeff.at[t],
            dst_ref=coeff.at[t],
            send_sem=ag_send,
            recv_sem=ag_recv,
            device_id=(r, lax.rem(t + k, nt)),
            device_id_type=MESH,
        ).start()

    wait_bytes(stats.at[pl.ds(0, nt - 1)], st_recv)
    square = stats[0, 8:16, :]
    for k in range(1, nt):
        square += stats[k, 8:16, :]
    inverse_row = lax.rsqrt(square[0:1] / (width * nt) + EPS)
    inverse = jnp.sum(jnp.where(eye, inverse_row, 0.0), axis=1, keepdims=True)

    def project(o):
        source = lax.rem(t + o, nt)
        block = f_ref[...] if o == 0 else ring[o]
        block = block.astype(F32) * inverse
        gains = stats[source][0:8]
        normed = jnp.concatenate(
            [
                block[:, c * lanes : (c + 1) * lanes] * gains[c : c + 1]
                for c in range(chunks)
            ],
            axis=1,
        ).astype(BF16)
        w = wbuf[pl.ds(pl.multiple_of(source * width, width), width), :]
        return jnp.dot(normed, w, preferred_element_type=F32)

    loads[2].wait()
    loads[3].wait()
    first = project(0) + project(nt - 1)
    if half > 1:
        first += project(1)
    acc_kv[...] = first

    length_row = len_ref[...].astype(F32)
    positions = jnp.sum(
        jnp.where(eye_r, length_row, 0.0), axis=1, keepdims=True
    )
    positions = jnp.concatenate([positions, positions + 1.0], axis=0)
    angle = positions * freq_ref[...]
    sign = jnp.where(iota((rows2, HD), 1) < HD // 2, -1.0, 1.0)
    cos_ref[...] = jnp.cos(angle)
    sin_ref[...] = jnp.sin(angle) * sign

    loads[4].wait()
    pbt[...] = pb[...].T

    for h in range(3, half):
        ring_stage(h)
        acc_kv[...] += project(nt - h + 1) + project(h - 1)

    wait_bytes(coeff.at[pl.ds(0, nt - 1)], ag_recv)
    coeffs = coeff[...].reshape(rank, coeff.shape[2])[:, 0:ntot]
    for s in range(pool):
        expand[s * rank : (s + 1) * rank, :] = jnp.where(
            slot_row == s, coeffs, 0.0
        ).astype(BF16)
    delta = jnp.dot(pbt[...], expand[...], preferred_element_type=F32).T
    ret_send[...] = delta[0:nvis]
    own_delta = delta[nvis:ntot]

    @pl.loop(1, nr)
    def _(k):
        to = lax.rem(r + k, nr)
        pltpu.make_async_remote_copy(
            src_ref=ret_send.at[pl.ds(pl.multiple_of(to // 2 * 8, 8), 8), :],
            dst_ref=ret_got.at[pl.ds(pl.multiple_of(r * 8, 8), 8), :],
            send_sem=re_send,
            recv_sem=re_recv,
            device_id=(to, t),
            device_id_type=MESH,
        ).start()

    loads[5].wait()

    @pl.loop(0, rows, unroll=8)
    def _(i):
        att_acc[pl.ds(pl.multiple_of(i * per_row, per_row), per_row), :] = jnp.dot(
            weights[i], cv[i], preferred_element_type=F32
        )

    if half > 2:
        acc_kv[...] += project(nt - half + 1) + project(half - 1)
    ring_stage(half)
    acc_kv[...] += project(half)

    key = acc_kv[:, 0:HD]
    turned = key * cos_ref[...] + pltpu.roll(key, HD // 2, 1) * sin_ref[...]
    new_keys = turned.astype(BF16)
    nk_ref[...] = new_keys

    for b in range(rows // qrows):
        part_rows = slice(b * span, (b + 1) * span)
        q = q_ref[b * qrows : (b + 1) * qrows].reshape(span, HD)
        fresh = (
            lax.dot_general(q, new_keys, NT, preferred_element_type=F32) * scale
        )
        row_of = iota(fresh.shape, 0) // per_row + b * qrows
        step_of = iota(fresh.shape, 0) % per_row // GROUP
        column = iota(fresh.shape, 1)
        seen = (column == row_of) | ((column == row_of + rows) & (step_of == 1))
        fresh = jnp.where(seen, fresh, NEG)
        cache_top = top_ref[part_rows, :]
        top = jnp.maximum(cache_top, jnp.max(fresh, axis=1, keepdims=True))
        shrink = jnp.exp(cache_top - top)
        e_fresh = jnp.exp(fresh - top)
        bottom = bottom_ref[part_rows, :] * shrink + jnp.sum(
            e_fresh, axis=1, keepdims=True
        )
        share = 1.0 / bottom
        fresh_w[part_rows, :] = (e_fresh * share).astype(BF16)
        att_acc[part_rows, :] = att_acc[part_rows, :] * (shrink * share)

    code_f = jnp.where(
        is_far, owner * 8 + lax.rem(r, 2) * 4 + turn * 2, -1000
    ).astype(F32)
    code_col = jnp.sum(jnp.where(eye_r, code_f, 0.0), axis=1, keepdims=True)
    code_col = jnp.concatenate([code_col, code_col + 1.0], axis=0).astype(jnp.int32)
    back = jnp.where(iota((rows2, nr * 8), 1) == code_col, 1.0, 0.0).astype(BF16)
    wait_bytes(ret_got.at[pl.ds(0, (nr - 1) * 8), :], re_recv)
    returned = ret_got[...]
    high = returned.astype(BF16)
    low = (returned - high.astype(F32)).astype(BF16)
    far_delta = jnp.dot(back, high, preferred_element_type=F32) + jnp.dot(
        back, low, preferred_element_type=F32
    )
    new_values = (acc_kv[:, HD : 2 * HD] + inverse * (far_delta + own_delta)).astype(
        BF16
    )
    nv_ref[...] = new_values
    att_acc[...] += jnp.dot(fresh_w[...], new_values, preferred_element_type=F32)
    for step in range(2):
        for g in range(GROUP):
            att_ref[step * rows : (step + 1) * rows, g * HD : (g + 1) * HD] = att_acc[
                pl.ds(step * GROUP + g, rows, stride=per_row), :
            ].astype(BF16)

    for h in range(1, half + 1):
        for way, c in hops(h):
            hop(way, h, c).wait_send()
    wait_bytes(stats.at[pl.ds(0, nt - 1)], st_send)
    wait_bytes(msg.at[pl.ds(0, (nr - 1) * SENT), :], a2a_send)
    wait_bytes(part.at[pl.ds(0, nt - 1)], rs_send)
    wait_bytes(coeff.at[pl.ds(0, nt - 1)], ag_send)
    wait_bytes(ret_got.at[pl.ds(0, (nr - 1) * 8), :], re_send)


def write_out(a, b, c, a_out, b_out, c_out, sem):
    copies = [
        pltpu.make_async_copy(src, dst, sem.at[k])
        for k, (src, dst) in enumerate([(a, a_out), (b, b_out), (c, c_out)])
    ]
    for copy in copies:
        copy.start()
    for copy in copies:
        copy.wait()


def shards(
    features,
    gain,
    w_key,
    w_value,
    pool_a,
    pool_b,
    placement,
    need_lists,
    row_adapter,
    lengths,
    queries,
    cache_k,
    cache_v,
):
    nr, nt = lax.axis_size("replica"), lax.axis_size("tp")
    steps, rows, width = features.shape
    pool, _, rank = pool_a.shape
    cache_len = cache_k.shape[1]
    rows2 = steps * rows
    nvis = nr * 4
    ntot = nvis + rows2
    ntot_pad = -(-ntot // HD) * HD
    per_row = steps * GROUP
    half = HD // 2
    frequency = np.float32(THETA) ** (-(np.arange(half, dtype=np.float32) * 2.0) / HD)
    frequency = np.concatenate([frequency, frequency]).astype(np.float32)[None, :]
    vmem = pl.BlockSpec(memory_space=pltpu.VMEM)
    hbm = pl.BlockSpec(memory_space=pltpu.HBM)
    dma = pltpu.SemaphoreType.DMA
    att, nk, nv = pl.pallas_call(
        functools.partial(kernel, nr, nt),
        out_shape=(
            jax.ShapeDtypeStruct((rows2, width), BF16),
            jax.ShapeDtypeStruct((rows2, HD), BF16),
            jax.ShapeDtypeStruct((rows2, HD), BF16),
        ),
        in_specs=[hbm] * 15,
        out_specs=(vmem, vmem, vmem),
        scratch_shapes=[
            pltpu.VMEM((rows2, width), BF16),
            pltpu.VMEM((width // HD, HD), BF16),
            pltpu.VMEM((1, placement.shape[0]), jnp.int32),
            pltpu.VMEM(need_lists.shape[::-1], jnp.int32),
            pltpu.VMEM((1, rows), jnp.int32),
            pltpu.SMEM((rows,), jnp.int32),
            pltpu.VMEM((1, rows), jnp.int32),
            pltpu.VMEM((1, HD), F32),
            pltpu.VMEM((rows2, width), BF16),
            pltpu.VMEM((rows * per_row, HD), F32),
            pltpu.VMEM((rows, per_row, HD), BF16),
            pltpu.VMEM((nt * width, 2 * HD), BF16),
            pltpu.VMEM((pool * rank, width), BF16),
            pltpu.VMEM((pool * rank, HD), BF16),
            pltpu.VMEM((HD, pool * rank), BF16),
            pltpu.VMEM((rows, cache_len, HD), BF16),
            pltpu.VMEM((rows, cache_len, HD), BF16),
            pltpu.VMEM((nt, 16, HD), F32),
            pltpu.VMEM((nr * SENT, HD), BF16),
            pltpu.VMEM((nr * SENT, HD), F32),
            pltpu.VMEM((nr * SENT, HD), BF16),
            pltpu.VMEM((ntot, width), BF16),
            pltpu.VMEM((nt, rows2, width), BF16),
            pltpu.VMEM((nt, rank // nt, ntot_pad), F32),
            pltpu.VMEM((nt, rank // nt, ntot_pad), F32),
            pltpu.VMEM((nt, rank // nt, ntot_pad), F32),
            pltpu.VMEM((pool * rank, ntot), BF16),
            pltpu.VMEM((nvis, HD), F32),
            pltpu.VMEM((nr * 8, HD), F32),
            pltpu.VMEM((rows, per_row, cache_len), F32),
            pltpu.VMEM((rows, per_row, cache_len), BF16),
            pltpu.VMEM((rows * per_row, rows2), BF16),
            pltpu.VMEM((rows2, 2 * HD), F32),
            pltpu.VMEM((rows * per_row, HD), F32),
            pltpu.VMEM((rows * per_row, 1), F32),
            pltpu.VMEM((rows * per_row, 1), F32),
            pltpu.VMEM((rows2, HD), F32),
            pltpu.VMEM((rows2, HD), F32),
            dma((9,)),
            dma((6,)),
            dma,
            dma,
            dma,
            dma,
            dma((2, max(nt // 2, 1), 2)),
            dma((nt, 2)),
            dma,
            dma,
            dma,
            dma,
            dma,
            dma,
        ],
        compiler_params=pltpu.CompilerParams(
            collective_id=0, has_side_effects=True, vmem_limit_bytes=60 * 2**20
        ),
        cost_estimate=pl.CostEstimate(
            flops=2 * 64 * 8192 * 256, bytes_accessed=12 * 2**20, transcendentals=0
        ),
    )(
        features.reshape(rows2, width),
        gain.reshape(width // HD, HD),
        placement.reshape(1, -1),
        need_lists.T,
        row_adapter.reshape(1, rows),
        lengths,
        lengths.reshape(1, rows),
        jnp.asarray(frequency),
        queries.reshape(rows2, width),
        w_key,
        w_value,
        pool_a.swapaxes(1, 2).reshape(pool * rank, width),
        pool_b.reshape(pool * rank, HD),
        cache_k,
        cache_v,
    )
    shapes = tuple(jax.ShapeDtypeStruct(x.shape, BF16) for x in (att, nk, nv))
    att, nk, nv = pl.pallas_call(
        write_out,
        out_shape=shapes,
        in_specs=[vmem] * 3,
        out_specs=(hbm,) * 3,
        scratch_shapes=[dma((3,))],
        compiler_params=pltpu.CompilerParams(vmem_limit_bytes=60 * 2**20),
    )(att, nk, nv)
    return (
        att.reshape(steps, rows, width),
        nk.reshape(steps, rows, HD),
        nv.reshape(steps, rows, HD),
    )


def solution(mesh):
    placed = (
        P(None, "replica", "tp"),
        P("tp"),
        P(None, "tp"),
        P(None, "tp"),
        P("replica", "tp", None),
        P("replica", None, "tp"),
        P(),
        P(),
        P("replica"),
        P("replica"),
        P(None, "replica", "tp"),
        P("replica", None, "tp"),
        P("replica", None, "tp"),
    )
    return jax.shard_map(
        shards,
        mesh=mesh,
        in_specs=placed,
        out_specs=(P(None, "replica", "tp"), P(None, "replica", "tp"), P(None, "replica", "tp")),
        check_vma=False,
    )
```

```python
import functools
import math

import jax
import jax.numpy as jnp
import numpy as np
from jax import lax
from jax.experimental import pallas as pl
from jax.experimental.pallas import tpu as pltpu
from jax.sharding import PartitionSpec as P

HD = 128
GROUP = 8
EPS = 1e-05
THETA = 500000.0
NEG = -1e30
MESH = pl.DeviceIdType.MESH
F32 = jnp.float32
BF16 = jnp.bfloat16
SENT = 32
NT = (((1,), (1,)), ((), ()))


def iota(shape, dim):
    return lax.broadcasted_iota(jnp.int32, shape, dim)


def kernel(
    nr,
    nt,
    f_hbm,
    gain_hbm,
    place_hbm,
    need_hbm,
    ra_hbm,
    len_s_hbm,
    len_hbm,
    freq_hbm,
    q_hbm,
    wk_hbm,
    wv_hbm,
    pa_hbm,
    pb_hbm,
    ck_hbm,
    cv_hbm,
    att_ref,
    nk_ref,
    nv_ref,
    f_ref,
    gain_ref,
    place_ref,
    need_ref,
    ra_ref,
    len_s,
    len_ref,
    freq_ref,
    q_in,
    q_wide,
    q_ref,
    wbuf,
    pa,
    pb,
    pbt,
    ck,
    cv,
    stats,
    msg,
    wide_rows,
    got,
    xall,
    ring,
    visit_part,
    own_part,
    expand,
    ret_send,
    ret_got,
    scores,
    weights,
    fresh_w,
    acc_kv,
    att_acc,
    top_ref,
    bottom_ref,
    cos_ref,
    sin_ref,
    small_sem,
    load_sem,
    st_send,
    st_recv,
    a2a_send,
    a2a_recv,
    ring_send,
    ring_recv,
    rs_send,
    rs_recv,
    ag_send,
    ag_recv,
    re_send,
    re_recv,
):
    r = lax.axis_index("replica")
    t = lax.axis_index("tp")
    rows2, width = f_ref.shape
    rows = rows2 // 2
    need_count = need_ref.shape[0]
    adapters = place_ref.shape[1]
    pool = adapters // nr
    rank = visit_part.shape[1]
    nvis = nr * 4
    ntot = nvis + rows2

    small = [
        pltpu.make_async_copy(a, b, small_sem.at[k])
        for k, (a, b) in enumerate(
            [
                (ra_hbm, ra_ref),
                (need_hbm, need_ref),
                (place_hbm, place_ref),
                (gain_hbm, gain_ref),
                (f_hbm, f_ref),
                (len_s_hbm, len_s),
                (len_hbm, len_ref),
                (freq_hbm, freq_ref),
                (q_hbm, q_in),
            ]
        )
    ]
    loads = [
        pltpu.make_async_copy(ck_hbm, ck, load_sem.at[0]),
        pltpu.make_async_copy(pa_hbm, pa, load_sem.at[1]),
        pltpu.make_async_copy(wk_hbm, wbuf.at[:, pl.ds(0, HD)], load_sem.at[2]),
        pltpu.make_async_copy(wv_hbm, wbuf.at[:, pl.ds(HD, HD)], load_sem.at[3]),
        pltpu.make_async_copy(pb_hbm, pb, load_sem.at[4]),
        pltpu.make_async_copy(cv_hbm, cv, load_sem.at[5]),
    ]
    for load in small:
        load.start()

    barrier = pltpu.get_barrier_semaphore()

    @pl.loop(1, nr)
    def _(k):
        pl.semaphore_signal(
            barrier, inc=1, device_id=(lax.rem(r + k, nr), t), device_id_type=MESH
        )

    @pl.loop(1, nt)
    def _(k):
        pl.semaphore_signal(
            barrier, inc=1, device_id=(r, lax.rem(t + k, nt)), device_id_type=MESH
        )

    for load in loads:
        load.start()

    for load in small[:3]:
        load.wait()
    ra = ra_ref[...]
    need = need_ref[...]
    mine = jnp.sum(
        jnp.where(iota(need.shape, 1) == r, need, 0).astype(F32), axis=1, keepdims=True
    )
    entry = iota((need_count, rows), 0) == ra
    wanted = jnp.sum(jnp.where(entry, mine, 0.0), axis=0, keepdims=True)
    place = place_ref[...]
    home = place // pool
    local = place - home * pool
    at_me = jnp.where(home == r, local + 1, 0)
    table = jnp.concatenate(
        [
            jnp.broadcast_to(x.astype(F32), (8, adapters))
            for x in (home, local, at_me)
        ],
        axis=0,
    ).astype(BF16)
    which = iota((adapters, rows), 0) == wanted.astype(jnp.int32)
    found = jnp.dot(
        table, jnp.where(which, 1.0, 0.0).astype(BF16), preferred_element_type=F32
    )
    owner = found[0:1].astype(jnp.int32)
    eye_r = iota((rows, rows), 0) == iota((rows, rows), 1)
    ra_f = ra.astype(F32)
    ra_col = jnp.sum(jnp.where(eye_r, ra_f, 0.0), axis=1, keepdims=True)
    twin = (ra_col == ra_f) & (iota((rows, rows), 0) < iota((rows, rows), 1))
    turn = jnp.sum(jnp.where(twin, 1.0, 0.0), axis=0, keepdims=True).astype(jnp.int32)
    is_far = ra < need_count
    code = jnp.where(is_far, owner * 4 + turn * 2, -1000)
    code2 = jnp.concatenate([code, code + 1], axis=1)
    pick = jnp.where(iota((nvis, rows2), 0) == code2, 1.0, 0.0).astype(BF16)

    small[3].wait()
    small[4].wait()
    pl.semaphore_wait(barrier, nr - 1 + nt - 1)
    right = (r, lax.rem(t + 1, nt))
    left = (r, lax.rem(t + nt - 1, nt))
    half = nt // 2

    def hop(which_way, h, c):
        if which_way == 0:
            have, there, to = (nt - (h - 1)) % nt, nt - h, right
        else:
            have, there, to = h - 1, h, left
        piece = pl.ds(c * rows, rows)
        src = f_ref.at[piece, :] if have == 0 else ring.at[have, piece, :]
        return pltpu.make_async_remote_copy(
            src_ref=src,
            dst_ref=ring.at[there, piece, :],
            send_sem=ring_send.at[which_way, h - 1, c],
            recv_sem=ring_recv.at[there, c],
            device_id=to,
            device_id_type=MESH,
        )

    def hops(h):
        if h < half:
            return [(0, 0), (1, 0), (0, 1), (1, 1)]
        return [(0, 0), (1, 1)]

    for way, c in hops(1):
        hop(way, 1, c).start()

    gain_rows = gain_ref[...].astype(F32)
    f32 = f_ref[...].astype(F32)
    lanes = HD
    chunks = width // lanes
    eye = iota((rows2, lanes), 0) == iota((rows2, lanes), 1)
    square_sum = jnp.sum(f32 * f32, axis=1, keepdims=True)
    square_row = jnp.sum(jnp.where(eye, square_sum, 0.0), axis=0, keepdims=True)
    stats[t] = jnp.concatenate(
        [gain_rows, jnp.broadcast_to(square_row, (8, lanes))], axis=0
    )
    own = jnp.concatenate(
        [
            f32[:, c * lanes : (c + 1) * lanes] * gain_rows[c : c + 1]
            for c in range(chunks)
        ],
        axis=1,
    ).astype(BF16)
    xall[pl.ds(nvis, rows2), :] = own

    picked_rows = jnp.dot(pick, own, preferred_element_type=F32)
    for j in range(chunks):
        wide_rows[pl.ds(j, nvis, stride=chunks), :] = picked_rows[
            :, j * lanes : (j + 1) * lanes
        ]
    msg[...] = wide_rows[...].astype(BF16)
    got[pl.ds(pl.multiple_of(r * SENT, SENT), SENT), :] = jnp.zeros((SENT, HD), BF16)
    ret_got[pl.ds(pl.multiple_of(r * 8, 8), 8), :] = jnp.zeros((8, HD), F32)

    @pl.loop(1, nr)
    def _(k):
        to = lax.rem(r + k, nr)
        pltpu.make_async_remote_copy(
            src_ref=msg.at[pl.ds(pl.multiple_of(to * SENT, SENT), SENT), :],
            dst_ref=got.at[pl.ds(pl.multiple_of(r * SENT, SENT), SENT), :],
            send_sem=a2a_send,
            recv_sem=a2a_recv,
            device_id=(to, t),
            device_id_type=MESH,
        ).start()

    @pl.loop(1, nt)
    def _(k):
        pltpu.make_async_remote_copy(
            src_ref=stats.at[t],
            dst_ref=stats.at[t],
            send_sem=st_send,
            recv_sem=st_recv,
            device_id=(r, lax.rem(t + k, nt)),
            device_id_type=MESH,
        ).start()

    def wait_bytes(ref, sem):
        pltpu.make_async_copy(ref, ref, sem).wait()

    packs = max(1, min(HD // nr, need_count))
    while need_count % packs:
        packs -= 1
    tall = need_count // packs
    packed = jnp.concatenate(
        [need[k * tall : (k + 1) * tall, :] for k in range(packs)], axis=1
    )
    p_iota = iota((adapters, packs * nr), 0)
    asked = p_iota == packed[0:1, :]
    for e in range(1, tall):
        asked = asked | (p_iota == packed[e : e + 1, :])
    visit = jnp.dot(
        table, jnp.where(asked, 1.0, 0.0).astype(BF16), preferred_element_type=F32
    )[16:24]
    wide = (packs * nr, nvis)
    spread = jnp.where(iota(wide, 1) // 4 == iota(wide, 0) % nr, 1.0, 0.0)
    visit_slot = jnp.dot(
        visit.astype(BF16), spread.astype(BF16), preferred_element_type=F32
    )[0:1].astype(jnp.int32) - 1
    own_slot = jnp.where(is_far, -1, ra - need_count)
    own_slot = jnp.concatenate([own_slot, own_slot], axis=1)
    slot_row = jnp.concatenate([visit_slot, own_slot], axis=1)

    scale = 1.0 / math.sqrt(HD)
    cache_len = ck.shape[1]
    per_row = 2 * GROUP

    def cached_scores(lo, hi):
        @pl.loop(lo, hi, unroll=8)
        def _(i):
            s = (
                lax.dot_general(q_ref[i], ck[i], NT, preferred_element_type=F32) * scale
            )
            live = iota(s.shape, 1) < len_s[i]
            scores[i] = jnp.where(live, s, NEG)

    def ring_stage(h, which_chunks=(0, 1)):
        for way, c in hops(h):
            if c not in which_chunks:
                continue
            hop(way, h, c).wait_recv()
            if (way, c) in (hops(h + 1) if h < half else []):
                hop(way, h + 1, c).start()

    for load in small[5:]:
        load.wait()
    for step in range(2):
        for g in range(GROUP):
            q_wide[pl.ds(step * GROUP + g, rows, stride=per_row), :] = q_in[
                step * rows : (step + 1) * rows, g * HD : (g + 1) * HD
            ].astype(F32)
    q_ref[...] = q_wide[...].astype(BF16).reshape(rows, per_row, HD)
    loads[0].wait()
    cached_scores(0, rows // 4)
    ring_stage(1, (0,))
    cached_scores(rows // 4, rows // 2)
    ring_stage(1, (1,))

    loads[4].wait()
    pbt[...] = pb[...].T
    loads[1].wait()
    wait_bytes(got.at[pl.ds(0, (nr - 1) * SENT), :], a2a_recv)
    wide_rows[...] = got[...].astype(F32)
    for j in range(chunks):
        xall[pl.ds(0, nvis), j * lanes : (j + 1) * lanes] = wide_rows[
            pl.ds(j, nvis, stride=chunks), :
        ].astype(BF16)
    x = xall[...]
    group = 8
    picked = jnp.zeros((rank, ntot), F32)
    for base in range(0, pool, group):
        block = lax.dot_general(
            pa[base * rank : (base + group) * rank, :],
            x,
            NT,
            preferred_element_type=F32,
        )
        for s in range(group):
            picked += jnp.where(
                slot_row == base + s, block[s * rank : (s + 1) * rank], 0.0
            )
    visit_part[t] = picked[:, 0:nvis].astype(BF16)
    own_part[t] = picked[:, nvis:ntot].astype(BF16)

    def hand_round(ref, send_sem, recv_sem):
        @pl.loop(1, nt)
        def _(k):
            pltpu.make_async_remote_copy(
                src_ref=ref.at[t],
                dst_ref=ref.at[t],
                send_sem=send_sem,
                recv_sem=recv_sem,
                device_id=(r, lax.rem(t + k, nt)),
                device_id_type=MESH,
            ).start()

    hand_round(visit_part, rs_send, rs_recv)
    hand_round(own_part, ag_send, ag_recv)

    if half > 2:
        ring_stage(2, (0,))
    cached_scores(rows // 2, rows)

    qrows = 8
    span = qrows * per_row
    for b in range(rows // qrows):
        s = scores[b * qrows : (b + 1) * qrows].reshape(span, cache_len)
        top = jnp.max(s, axis=1, keepdims=True)
        e_cache = jnp.exp(s - top)
        top_ref[b * span : (b + 1) * span, :] = top
        bottom_ref[b * span : (b + 1) * span, :] = jnp.sum(
            e_cache, axis=1, keepdims=True
        )
        weights[b * qrows : (b + 1) * qrows] = e_cache.astype(BF16).reshape(
            qrows, per_row, cache_len
        )

    if half > 2:
        ring_stage(2, (1,))

    def low_rank_terms(part, slots):
        total = part[0].astype(F32)
        for k in range(1, nt):
            total += part[k].astype(F32)
        coeffs = total.astype(BF16).astype(F32)
        count = slots.shape[1]
        for s in range(pool):
            expand[s * rank : (s + 1) * rank, 0:count] = jnp.where(
                slots == s, coeffs, 0.0
            ).astype(BF16)
        return jnp.dot(
            pbt[...], expand[:, 0:count], preferred_element_type=F32
        ).T

    wait_bytes(visit_part.at[pl.ds(0, nt - 1)], rs_recv)
    ret_send[...] = low_rank_terms(visit_part, visit_slot)

    @pl.loop(1, nr)
    def _(k):
        to = lax.rem(r + k, nr)
        pltpu.make_async_remote_copy(
            src_ref=ret_send.at[pl.ds(pl.multiple_of(to // 2 * 8, 8), 8), :],
            dst_ref=ret_got.at[pl.ds(pl.multiple_of(r * 8, 8), 8), :],
            send_sem=re_send,
            recv_sem=re_recv,
            device_id=(to, t),
            device_id_type=MESH,
        ).start()

    wait_bytes(stats.at[pl.ds(0, nt - 1)], st_recv)
    square = stats[0, 8:16, :]
    for k in range(1, nt):
        square += stats[k, 8:16, :]
    inverse_row = lax.rsqrt(square[0:1] / (width * nt) + EPS)
    inverse = jnp.sum(jnp.where(eye, inverse_row, 0.0), axis=1, keepdims=True)

    def project(o):
        source = lax.rem(t + o, nt)
        block = f_ref[...] if o == 0 else ring[o]
        block = block.astype(F32) * inverse
        gains = stats[source][0:8]
        normed = jnp.concatenate(
            [
                block[:, c * lanes : (c + 1) * lanes] * gains[c : c + 1]
                for c in range(chunks)
            ],
            axis=1,
        ).astype(BF16)
        w = wbuf[pl.ds(pl.multiple_of(source * width, width), width), :]
        return jnp.dot(normed, w, preferred_element_type=F32)

    loads[2].wait()
    loads[3].wait()
    first = project(0) + project(nt - 1)
    if half > 1:
        first += project(1)
    acc_kv[...] = first

    length_row = len_ref[...].astype(F32)
    positions = jnp.sum(
        jnp.where(eye_r, length_row, 0.0), axis=1, keepdims=True
    )
    positions = jnp.concatenate([positions, positions + 1.0], axis=0)
    angle = positions * freq_ref[...]
    sign = jnp.where(iota((rows2, HD), 1) < HD // 2, -1.0, 1.0)
    cos_ref[...] = jnp.cos(angle)
    sin_ref[...] = jnp.sin(angle) * sign

    for h in range(3, half):
        ring_stage(h)
        acc_kv[...] += project(nt - h + 1) + project(h - 1)

    loads[5].wait()

    @pl.loop(0, rows, unroll=8)
    def _(i):
        att_acc[pl.ds(pl.multiple_of(i * per_row, per_row), per_row), :] = jnp.dot(
            weights[i], cv[i], preferred_element_type=F32
        )

    if half > 2:
        acc_kv[...] += project(nt - half + 1) + project(half - 1)
    ring_stage(half)
    acc_kv[...] += project(half)

    key = acc_kv[:, 0:HD]
    turned = key * cos_ref[...] + pltpu.roll(key, HD // 2, 1) * sin_ref[...]
    new_keys = turned.astype(BF16)
    nk_ref[...] = new_keys

    for b in range(rows // qrows):
        part_rows = slice(b * span, (b + 1) * span)
        q = q_ref[b * qrows : (b + 1) * qrows].reshape(span, HD)
        fresh = (
            lax.dot_general(q, new_keys, NT, preferred_element_type=F32) * scale
        )
        row_of = iota(fresh.shape, 0) // per_row + b * qrows
        step_of = iota(fresh.shape, 0) % per_row // GROUP
        column = iota(fresh.shape, 1)
        seen = (column == row_of) | ((column == row_of + rows) & (step_of == 1))
        fresh = jnp.where(seen, fresh, NEG)
        cache_top = top_ref[part_rows, :]
        top = jnp.maximum(cache_top, jnp.max(fresh, axis=1, keepdims=True))
        shrink = jnp.exp(cache_top - top)
        e_fresh = jnp.exp(fresh - top)
        bottom = bottom_ref[part_rows, :] * shrink + jnp.sum(
            e_fresh, axis=1, keepdims=True
        )
        share = 1.0 / bottom
        fresh_w[part_rows, :] = (e_fresh * share).astype(BF16)
        att_acc[part_rows, :] = att_acc[part_rows, :] * (shrink * share)

    wait_bytes(own_part.at[pl.ds(0, nt - 1)], ag_recv)
    own_delta = low_rank_terms(own_part, own_slot)
    code_f = jnp.where(
        is_far, owner * 8 + lax.rem(r, 2) * 4 + turn * 2, -1000
    ).astype(F32)
    code_col = jnp.sum(jnp.where(eye_r, code_f, 0.0), axis=1, keepdims=True)
    code_col = jnp.concatenate([code_col, code_col + 1.0], axis=0).astype(jnp.int32)
    back = jnp.where(iota((rows2, nr * 8), 1) == code_col, 1.0, 0.0).astype(BF16)
    wait_bytes(ret_got.at[pl.ds(0, (nr - 1) * 8), :], re_recv)
    returned = ret_got[...]
    high = returned.astype(BF16)
    low = (returned - high.astype(F32)).astype(BF16)
    far_delta = jnp.dot(back, high, preferred_element_type=F32) + jnp.dot(
        back, low, preferred_element_type=F32
    )
    new_values = (acc_kv[:, HD : 2 * HD] + inverse * (far_delta + own_delta)).astype(
        BF16
    )
    nv_ref[...] = new_values
    att_acc[...] += jnp.dot(fresh_w[...], new_values, preferred_element_type=F32)
    for step in range(2):
        for g in range(GROUP):
            att_ref[step * rows : (step + 1) * rows, g * HD : (g + 1) * HD] = att_acc[
                pl.ds(step * GROUP + g, rows, stride=per_row), :
            ].astype(BF16)

    for h in range(1, half + 1):
        for way, c in hops(h):
            hop(way, h, c).wait_send()
    wait_bytes(stats.at[pl.ds(0, nt - 1)], st_send)
    wait_bytes(msg.at[pl.ds(0, (nr - 1) * SENT), :], a2a_send)
    wait_bytes(visit_part.at[pl.ds(0, nt - 1)], rs_send)
    wait_bytes(own_part.at[pl.ds(0, nt - 1)], ag_send)
    wait_bytes(ret_got.at[pl.ds(0, (nr - 1) * 8), :], re_send)


def write_out(a, b, c, a_out, b_out, c_out, sem):
    copies = [
        pltpu.make_async_copy(src, dst, sem.at[k])
        for k, (src, dst) in enumerate([(a, a_out), (b, b_out), (c, c_out)])
    ]
    for copy in copies:
        copy.start()
    for copy in copies:
        copy.wait()


def shards(
    features,
    gain,
    w_key,
    w_value,
    pool_a,
    pool_b,
    placement,
    need_lists,
    row_adapter,
    lengths,
    queries,
    cache_k,
    cache_v,
):
    nr, nt = lax.axis_size("replica"), lax.axis_size("tp")
    steps, rows, width = features.shape
    pool, _, rank = pool_a.shape
    cache_len = cache_k.shape[1]
    rows2 = steps * rows
    nvis = nr * 4
    ntot = nvis + rows2
    per_row = steps * GROUP
    half = HD // 2
    frequency = np.float32(THETA) ** (-(np.arange(half, dtype=np.float32) * 2.0) / HD)
    frequency = np.concatenate([frequency, frequency]).astype(np.float32)[None, :]
    vmem = pl.BlockSpec(memory_space=pltpu.VMEM)
    hbm = pl.BlockSpec(memory_space=pltpu.HBM)
    dma = pltpu.SemaphoreType.DMA
    att, nk, nv = pl.pallas_call(
        functools.partial(kernel, nr, nt),
        out_shape=(
            jax.ShapeDtypeStruct((rows2, width), BF16),
            jax.ShapeDtypeStruct((rows2, HD), BF16),
            jax.ShapeDtypeStruct((rows2, HD), BF16),
        ),
        in_specs=[hbm] * 15,
        out_specs=(vmem, vmem, vmem),
        scratch_shapes=[
            pltpu.VMEM((rows2, width), BF16),
            pltpu.VMEM((width // HD, HD), BF16),
            pltpu.VMEM((1, placement.shape[0]), jnp.int32),
            pltpu.VMEM(need_lists.shape[::-1], jnp.int32),
            pltpu.VMEM((1, rows), jnp.int32),
            pltpu.SMEM((rows,), jnp.int32),
            pltpu.VMEM((1, rows), jnp.int32),
            pltpu.VMEM((1, HD), F32),
            pltpu.VMEM((rows2, width), BF16),
            pltpu.VMEM((rows * per_row, HD), F32),
            pltpu.VMEM((rows, per_row, HD), BF16),
            pltpu.VMEM((nt * width, 2 * HD), BF16),
            pltpu.VMEM((pool * rank, width), BF16),
            pltpu.VMEM((pool * rank, HD), BF16),
            pltpu.VMEM((HD, pool * rank), BF16),
            pltpu.VMEM((rows, cache_len, HD), BF16),
            pltpu.VMEM((rows, cache_len, HD), BF16),
            pltpu.VMEM((nt, 16, HD), F32),
            pltpu.VMEM((nr * SENT, HD), BF16),
            pltpu.VMEM((nr * SENT, HD), F32),
            pltpu.VMEM((nr * SENT, HD), BF16),
            pltpu.VMEM((ntot, width), BF16),
            pltpu.VMEM((nt, rows2, width), BF16),
            pltpu.VMEM((nt, rank, nvis), BF16),
            pltpu.VMEM((nt, rank, rows2), BF16),
            pltpu.VMEM((pool * rank, nvis), BF16),
            pltpu.VMEM((nvis, HD), F32),
            pltpu.VMEM((nr * 8, HD), F32),
            pltpu.VMEM((rows, per_row, cache_len), F32),
            pltpu.VMEM((rows, per_row, cache_len), BF16),
            pltpu.VMEM((rows * per_row, rows2), BF16),
            pltpu.VMEM((rows2, 2 * HD), F32),
            pltpu.VMEM((rows * per_row, HD), F32),
            pltpu.VMEM((rows * per_row, 1), F32),
            pltpu.VMEM((rows * per_row, 1), F32),
            pltpu.VMEM((rows2, HD), F32),
            pltpu.VMEM((rows2, HD), F32),
            dma((9,)),
            dma((6,)),
            dma,
            dma,
            dma,
            dma,
            dma((2, max(nt // 2, 1), 2)),
            dma((nt, 2)),
            dma,
            dma,
            dma,
            dma,
            dma,
            dma,
        ],
        compiler_params=pltpu.CompilerParams(
            collective_id=0, has_side_effects=True, vmem_limit_bytes=60 * 2**20
        ),
        cost_estimate=pl.CostEstimate(
            flops=2 * 64 * 8192 * 256, bytes_accessed=12 * 2**20, transcendentals=0
        ),
    )(
        features.reshape(rows2, width),
        gain.reshape(width // HD, HD),
        placement.reshape(1, -1),
        need_lists.T,
        row_adapter.reshape(1, rows),
        lengths,
        lengths.reshape(1, rows),
        jnp.asarray(frequency),
        queries.reshape(rows2, width),
        w_key,
        w_value,
        pool_a.swapaxes(1, 2).reshape(pool * rank, width),
        pool_b.reshape(pool * rank, HD),
        cache_k,
        cache_v,
    )
    shapes = tuple(jax.ShapeDtypeStruct(x.shape, BF16) for x in (att, nk, nv))
    att, nk, nv = pl.pallas_call(
        write_out,
        out_shape=shapes,
        in_specs=[vmem] * 3,
        out_specs=(hbm,) * 3,
        scratch_shapes=[dma((3,))],
        compiler_params=pltpu.CompilerParams(vmem_limit_bytes=60 * 2**20),
    )(att, nk, nv)
    return (
        att.reshape(steps, rows, width),
        nk.reshape(steps, rows, HD),
        nv.reshape(steps, rows, HD),
    )


def solution(mesh):
    placed = (
        P(None, "replica", "tp"),
        P("tp"),
        P(None, "tp"),
        P(None, "tp"),
        P("replica", "tp", None),
        P("replica", None, "tp"),
        P(),
        P(),
        P("replica"),
        P("replica"),
        P(None, "replica", "tp"),
        P("replica", None, "tp"),
        P("replica", None, "tp"),
    )
    return jax.shard_map(
        shards,
        mesh=mesh,
        in_specs=placed,
        out_specs=(P(None, "replica", "tp"), P(None, "replica", "tp"), P(None, "replica", "tp")),
        check_vma=False,
    )
```

```python
import functools
import math

import jax
import jax.numpy as jnp
import numpy as np
from jax import lax
from jax.experimental import pallas as pl
from jax.experimental.pallas import tpu as pltpu
from jax.sharding import PartitionSpec as P

HD = 128
GROUP = 8
EPS = 1e-05
THETA = 500000.0
NEG = -1e30
MESH = pl.DeviceIdType.MESH
F32 = jnp.float32
BF16 = jnp.bfloat16
SENT = 32
NT = (((1,), (1,)), ((), ()))


def iota(shape, dim):
    return lax.broadcasted_iota(jnp.int32, shape, dim)


def kernel(
    nr,
    nt,
    f_hbm,
    gain_hbm,
    place_hbm,
    need_hbm,
    ra_hbm,
    len_s_hbm,
    len_hbm,
    freq_hbm,
    q_hbm,
    wk_hbm,
    wv_hbm,
    pa_hbm,
    pb_hbm,
    ck_hbm,
    cv_hbm,
    att_ref,
    nk_ref,
    nv_ref,
    f_ref,
    gain_ref,
    place_ref,
    need_ref,
    ra_ref,
    len_s,
    len_ref,
    freq_ref,
    q_in,
    q_wide,
    q_ref,
    wbuf,
    pa,
    pb,
    pbt,
    ck,
    cv,
    stats,
    msg,
    wide_rows,
    got,
    xall,
    ring,
    visit_part,
    own_part,
    expand,
    ret_send,
    ret_got,
    scores,
    weights,
    fresh_w,
    acc_kv,
    att_acc,
    top_ref,
    bottom_ref,
    cos_ref,
    sin_ref,
    small_sem,
    load_sem,
    st_send,
    st_recv,
    a2a_send,
    a2a_recv,
    ring_send,
    ring_recv,
    rs_send,
    rs_recv,
    ag_send,
    ag_recv,
    re_send,
    re_recv,
):
    r = lax.axis_index("replica")
    t = lax.axis_index("tp")
    rows2, width = f_ref.shape
    rows = rows2 // 2
    need_count = need_ref.shape[0]
    adapters = place_ref.shape[1]
    pool = adapters // nr
    rank = visit_part.shape[1]
    nvis = nr * 4
    ntot = nvis + rows2

    small = [
        pltpu.make_async_copy(a, b, small_sem.at[k])
        for k, (a, b) in enumerate(
            [
                (ra_hbm, ra_ref),
                (need_hbm, need_ref),
                (place_hbm, place_ref),
                (gain_hbm, gain_ref),
                (f_hbm, f_ref),
                (len_s_hbm, len_s),
                (len_hbm, len_ref),
                (freq_hbm, freq_ref),
                (q_hbm, q_in),
            ]
        )
    ]
    loads = [
        pltpu.make_async_copy(ck_hbm, ck, load_sem.at[0]),
        pltpu.make_async_copy(pa_hbm, pa, load_sem.at[1]),
        pltpu.make_async_copy(wk_hbm, wbuf.at[:, pl.ds(0, HD)], load_sem.at[2]),
        pltpu.make_async_copy(wv_hbm, wbuf.at[:, pl.ds(HD, HD)], load_sem.at[3]),
        pltpu.make_async_copy(pb_hbm, pb, load_sem.at[4]),
        pltpu.make_async_copy(cv_hbm, cv, load_sem.at[5]),
    ]
    for load in small:
        load.start()

    barrier = pltpu.get_barrier_semaphore()

    @pl.loop(1, nr)
    def _(k):
        pl.semaphore_signal(
            barrier, inc=1, device_id=(lax.rem(r + k, nr), t), device_id_type=MESH
        )

    @pl.loop(1, nt)
    def _(k):
        pl.semaphore_signal(
            barrier, inc=1, device_id=(r, lax.rem(t + k, nt)), device_id_type=MESH
        )

    for load in loads:
        load.start()

    for load in small[:3]:
        load.wait()
    ra = ra_ref[...]
    need = need_ref[...]
    mine = jnp.sum(
        jnp.where(iota(need.shape, 1) == r, need, 0).astype(F32), axis=1, keepdims=True
    )
    entry = iota((need_count, rows), 0) == ra
    wanted = jnp.sum(jnp.where(entry, mine, 0.0), axis=0, keepdims=True)
    place = place_ref[...]
    home = place // pool
    local = place - home * pool
    at_me = jnp.where(home == r, local + 1, 0)
    table = jnp.concatenate(
        [
            jnp.broadcast_to(x.astype(F32), (8, adapters))
            for x in (home, local, at_me)
        ],
        axis=0,
    ).astype(BF16)
    which = iota((adapters, rows), 0) == wanted.astype(jnp.int32)
    found = jnp.dot(
        table, jnp.where(which, 1.0, 0.0).astype(BF16), preferred_element_type=F32
    )
    owner = found[0:1].astype(jnp.int32)
    eye_r = iota((rows, rows), 0) == iota((rows, rows), 1)
    ra_f = ra.astype(F32)
    ra_col = jnp.sum(jnp.where(eye_r, ra_f, 0.0), axis=1, keepdims=True)
    twin = (ra_col == ra_f) & (iota((rows, rows), 0) < iota((rows, rows), 1))
    turn = jnp.sum(jnp.where(twin, 1.0, 0.0), axis=0, keepdims=True).astype(jnp.int32)
    is_far = ra < need_count
    code = jnp.where(is_far, owner * 4 + turn * 2, -1000)
    code2 = jnp.concatenate([code, code + 1], axis=1)
    pick = jnp.where(iota((nvis, rows2), 0) == code2, 1.0, 0.0).astype(BF16)

    small[3].wait()
    small[4].wait()
    pl.semaphore_wait(barrier, nr - 1 + nt - 1)
    right = (r, lax.rem(t + 1, nt))
    left = (r, lax.rem(t + nt - 1, nt))
    half = nt // 2

    def hop(which_way, h, c):
        if which_way == 0:
            have, there, to = (nt - (h - 1)) % nt, nt - h, right
        else:
            have, there, to = h - 1, h, left
        piece = pl.ds(c * rows, rows)
        src = f_ref.at[piece, :] if have == 0 else ring.at[have, piece, :]
        return pltpu.make_async_remote_copy(
            src_ref=src,
            dst_ref=ring.at[there, piece, :],
            send_sem=ring_send.at[which_way, h - 1, c],
            recv_sem=ring_recv.at[there, c],
            device_id=to,
            device_id_type=MESH,
        )

    def hops(h):
        if h < half:
            return [(0, 0), (1, 0), (0, 1), (1, 1)]
        return [(0, 0), (1, 1)]

    for way, c in hops(1):
        hop(way, 1, c).start()

    gain_rows = gain_ref[...].astype(F32)
    f32 = f_ref[...].astype(F32)
    lanes = HD
    chunks = width // lanes
    eye = iota((rows2, lanes), 0) == iota((rows2, lanes), 1)
    square_sum = jnp.sum(f32 * f32, axis=1, keepdims=True)
    square_row = jnp.sum(jnp.where(eye, square_sum, 0.0), axis=0, keepdims=True)
    stats[t] = jnp.concatenate(
        [gain_rows, jnp.broadcast_to(square_row, (8, lanes))], axis=0
    )
    own = jnp.concatenate(
        [
            f32[:, c * lanes : (c + 1) * lanes] * gain_rows[c : c + 1]
            for c in range(chunks)
        ],
        axis=1,
    ).astype(BF16)
    xall[pl.ds(nvis, rows2), :] = own

    picked_rows = jnp.dot(pick, own, preferred_element_type=F32)
    for j in range(chunks):
        wide_rows[pl.ds(j, nvis, stride=chunks), :] = picked_rows[
            :, j * lanes : (j + 1) * lanes
        ]
    msg[...] = wide_rows[...].astype(BF16)
    got[pl.ds(pl.multiple_of(r * SENT, SENT), SENT), :] = jnp.zeros((SENT, HD), BF16)
    ret_got[pl.ds(pl.multiple_of(r * 8, 8), 8), :] = jnp.zeros((8, HD), F32)

    @pl.loop(1, nr)
    def _(k):
        to = lax.rem(r + k, nr)
        pltpu.make_async_remote_copy(
            src_ref=msg.at[pl.ds(pl.multiple_of(to * SENT, SENT), SENT), :],
            dst_ref=got.at[pl.ds(pl.multiple_of(r * SENT, SENT), SENT), :],
            send_sem=a2a_send,
            recv_sem=a2a_recv,
            device_id=(to, t),
            device_id_type=MESH,
        ).start()

    @pl.loop(1, nt)
    def _(k):
        pltpu.make_async_remote_copy(
            src_ref=stats.at[t],
            dst_ref=stats.at[t],
            send_sem=st_send,
            recv_sem=st_recv,
            device_id=(r, lax.rem(t + k, nt)),
            device_id_type=MESH,
        ).start()

    def wait_bytes(ref, sem):
        pltpu.make_async_copy(ref, ref, sem).wait()

    packs = max(1, min(HD // nr, need_count))
    while need_count % packs:
        packs -= 1
    tall = need_count // packs
    packed = jnp.concatenate(
        [need[k * tall : (k + 1) * tall, :] for k in range(packs)], axis=1
    )
    p_iota = iota((adapters, packs * nr), 0)
    asked = p_iota == packed[0:1, :]
    for e in range(1, tall):
        asked = asked | (p_iota == packed[e : e + 1, :])
    visit = jnp.dot(
        table, jnp.where(asked, 1.0, 0.0).astype(BF16), preferred_element_type=F32
    )[16:24]
    wide = (packs * nr, nvis)
    spread = jnp.where(iota(wide, 1) // 4 == iota(wide, 0) % nr, 1.0, 0.0)
    visit_slot = jnp.dot(
        visit.astype(BF16), spread.astype(BF16), preferred_element_type=F32
    )[0:1].astype(jnp.int32) - 1
    own_slot = jnp.where(is_far, -1, ra - need_count)
    own_slot = jnp.concatenate([own_slot, own_slot], axis=1)
    slot_row = jnp.concatenate([visit_slot, own_slot], axis=1)

    scale = 1.0 / math.sqrt(HD)
    cache_len = ck.shape[1]
    per_row = 2 * GROUP

    def cached_scores(lo, hi):
        @pl.loop(lo, hi, unroll=8)
        def _(i):
            s = (
                lax.dot_general(q_ref[i], ck[i], NT, preferred_element_type=F32) * scale
            )
            live = iota(s.shape, 1) < len_s[i]
            scores[i] = jnp.where(live, s, NEG)

    def ring_stage(h, which_chunks=(0, 1)):
        for way, c in hops(h):
            if c not in which_chunks:
                continue
            hop(way, h, c).wait_recv()
            if (way, c) in (hops(h + 1) if h < half else []):
                hop(way, h + 1, c).start()

    for load in small[5:]:
        load.wait()
    for step in range(2):
        for g in range(GROUP):
            q_wide[pl.ds(step * GROUP + g, rows, stride=per_row), :] = q_in[
                step * rows : (step + 1) * rows, g * HD : (g + 1) * HD
            ].astype(F32)
    q_ref[...] = q_wide[...].astype(BF16).reshape(rows, per_row, HD)
    loads[0].wait()
    cached_scores(0, rows // 4)
    ring_stage(1, (0,))
    cached_scores(rows // 4, rows // 2)
    ring_stage(1, (1,))
    cached_scores(rows // 2, rows)

    length_row = len_ref[...].astype(F32)
    positions = jnp.sum(
        jnp.where(eye_r, length_row, 0.0), axis=1, keepdims=True
    )
    positions = jnp.concatenate([positions, positions + 1.0], axis=0)
    angle = positions * freq_ref[...]
    sign = jnp.where(iota((rows2, HD), 1) < HD // 2, -1.0, 1.0)
    cos_ref[...] = jnp.cos(angle)
    sin_ref[...] = jnp.sin(angle) * sign


    loads[4].wait()
    pbt[...] = pb[...].T
    loads[1].wait()
    wait_bytes(got.at[pl.ds(0, (nr - 1) * SENT), :], a2a_recv)
    wide_rows[...] = got[...].astype(F32)
    for j in range(chunks):
        xall[pl.ds(0, nvis), j * lanes : (j + 1) * lanes] = wide_rows[
            pl.ds(j, nvis, stride=chunks), :
        ].astype(BF16)
    x = xall[...]
    group = 8
    picked = jnp.zeros((rank, ntot), F32)
    for base in range(0, pool, group):
        block = lax.dot_general(
            pa[base * rank : (base + group) * rank, :],
            x,
            NT,
            preferred_element_type=F32,
        )
        for s in range(group):
            picked += jnp.where(
                slot_row == base + s, block[s * rank : (s + 1) * rank], 0.0
            )
    visit_part[t] = picked[:, 0:nvis].astype(BF16)
    own_part[t] = picked[:, nvis:ntot].astype(BF16)

    def hand_round(ref, send_sem, recv_sem):
        @pl.loop(1, nt)
        def _(k):
            pltpu.make_async_remote_copy(
                src_ref=ref.at[t],
                dst_ref=ref.at[t],
                send_sem=send_sem,
                recv_sem=recv_sem,
                device_id=(r, lax.rem(t + k, nt)),
                device_id_type=MESH,
            ).start()

    hand_round(visit_part, rs_send, rs_recv)
    hand_round(own_part, ag_send, ag_recv)

    if half > 2:
        ring_stage(2, (0,))

    qrows = 8
    span = qrows * per_row
    for b in range(rows // qrows):
        s = scores[b * qrows : (b + 1) * qrows].reshape(span, cache_len)
        top = jnp.max(s, axis=1, keepdims=True)
        e_cache = jnp.exp(s - top)
        top_ref[b * span : (b + 1) * span, :] = top
        bottom_ref[b * span : (b + 1) * span, :] = jnp.sum(
            e_cache, axis=1, keepdims=True
        )
        weights[b * qrows : (b + 1) * qrows] = e_cache.astype(BF16).reshape(
            qrows, per_row, cache_len
        )

    if half > 2:
        ring_stage(2, (1,))

    wait_bytes(stats.at[pl.ds(0, nt - 1)], st_recv)
    square = stats[0, 8:16, :]
    for k in range(1, nt):
        square += stats[k, 8:16, :]
    inverse_row = lax.rsqrt(square[0:1] / (width * nt) + EPS)
    inverse = jnp.sum(jnp.where(eye, inverse_row, 0.0), axis=1, keepdims=True)

    def project(o):
        source = lax.rem(t + o, nt)
        block = f_ref[...] if o == 0 else ring[o]
        block = block.astype(F32) * inverse
        gains = stats[source][0:8]
        normed = jnp.concatenate(
            [
                block[:, c * lanes : (c + 1) * lanes] * gains[c : c + 1]
                for c in range(chunks)
            ],
            axis=1,
        ).astype(BF16)
        w = wbuf[pl.ds(pl.multiple_of(source * width, width), width), :]
        return jnp.dot(normed, w, preferred_element_type=F32)

    loads[2].wait()
    loads[3].wait()
    first = project(0) + project(nt - 1)
    if half > 1:
        first += project(1)
    acc_kv[...] = first

    loads[5].wait()

    @pl.loop(0, rows, unroll=8)
    def _(i):
        att_acc[pl.ds(pl.multiple_of(i * per_row, per_row), per_row), :] = jnp.dot(
            weights[i], cv[i], preferred_element_type=F32
        )

    for h in range(3, half):
        ring_stage(h, (0,))

    def low_rank_terms(part, slots):
        total = part[0].astype(F32)
        for k in range(1, nt):
            total += part[k].astype(F32)
        coeffs = total.astype(BF16).astype(F32)
        count = slots.shape[1]
        for s in range(pool):
            expand[s * rank : (s + 1) * rank, 0:count] = jnp.where(
                slots == s, coeffs, 0.0
            ).astype(BF16)
        return jnp.dot(
            pbt[...], expand[:, 0:count], preferred_element_type=F32
        ).T

    wait_bytes(visit_part.at[pl.ds(0, nt - 1)], rs_recv)
    ret_send[...] = low_rank_terms(visit_part, visit_slot)

    @pl.loop(1, nr)
    def _(k):
        to = lax.rem(r + k, nr)
        pltpu.make_async_remote_copy(
            src_ref=ret_send.at[pl.ds(pl.multiple_of(to // 2 * 8, 8), 8), :],
            dst_ref=ret_got.at[pl.ds(pl.multiple_of(r * 8, 8), 8), :],
            send_sem=re_send,
            recv_sem=re_recv,
            device_id=(to, t),
            device_id_type=MESH,
        ).start()

    for h in range(3, half):
        ring_stage(h, (1,))
        acc_kv[...] += project(nt - h + 1) + project(h - 1)
    wait_bytes(own_part.at[pl.ds(0, nt - 1)], ag_recv)
    own_delta = low_rank_terms(own_part, own_slot)
    if half > 2:
        acc_kv[...] += project(nt - half + 1) + project(half - 1)
    ring_stage(half)
    acc_kv[...] += project(half)

    key = acc_kv[:, 0:HD]
    turned = key * cos_ref[...] + pltpu.roll(key, HD // 2, 1) * sin_ref[...]
    new_keys = turned.astype(BF16)
    nk_ref[...] = new_keys

    for b in range(rows // qrows):
        part_rows = slice(b * span, (b + 1) * span)
        q = q_ref[b * qrows : (b + 1) * qrows].reshape(span, HD)
        fresh = (
            lax.dot_general(q, new_keys, NT, preferred_element_type=F32) * scale
        )
        row_of = iota(fresh.shape, 0) // per_row + b * qrows
        step_of = iota(fresh.shape, 0) % per_row // GROUP
        column = iota(fresh.shape, 1)
        seen = (column == row_of) | ((column == row_of + rows) & (step_of == 1))
        fresh = jnp.where(seen, fresh, NEG)
        cache_top = top_ref[part_rows, :]
        top = jnp.maximum(cache_top, jnp.max(fresh, axis=1, keepdims=True))
        shrink = jnp.exp(cache_top - top)
        e_fresh = jnp.exp(fresh - top)
        bottom = bottom_ref[part_rows, :] * shrink + jnp.sum(
            e_fresh, axis=1, keepdims=True
        )
        share = 1.0 / bottom
        fresh_w[part_rows, :] = (e_fresh * share).astype(BF16)
        att_acc[part_rows, :] = att_acc[part_rows, :] * (shrink * share)

    code_f = jnp.where(
        is_far, owner * 8 + lax.rem(r, 2) * 4 + turn * 2, -1000
    ).astype(F32)
    code_col = jnp.sum(jnp.where(eye_r, code_f, 0.0), axis=1, keepdims=True)
    code_col = jnp.concatenate([code_col, code_col + 1.0], axis=0).astype(jnp.int32)
    back = jnp.where(iota((rows2, nr * 8), 1) == code_col, 1.0, 0.0).astype(BF16)
    wait_bytes(ret_got.at[pl.ds(0, (nr - 1) * 8), :], re_recv)
    returned = ret_got[...]
    high = returned.astype(BF16)
    low = (returned - high.astype(F32)).astype(BF16)
    far_delta = jnp.dot(back, high, preferred_element_type=F32) + jnp.dot(
        back, low, preferred_element_type=F32
    )
    new_values = (acc_kv[:, HD : 2 * HD] + inverse * (far_delta + own_delta)).astype(
        BF16
    )
    nv_ref[...] = new_values
    att_acc[...] += jnp.dot(fresh_w[...], new_values, preferred_element_type=F32)
    for step in range(2):
        for g in range(GROUP):
            att_ref[step * rows : (step + 1) * rows, g * HD : (g + 1) * HD] = att_acc[
                pl.ds(step * GROUP + g, rows, stride=per_row), :
            ].astype(BF16)

    for h in range(1, half + 1):
        for way, c in hops(h):
            hop(way, h, c).wait_send()
    wait_bytes(stats.at[pl.ds(0, nt - 1)], st_send)
    wait_bytes(msg.at[pl.ds(0, (nr - 1) * SENT), :], a2a_send)
    wait_bytes(visit_part.at[pl.ds(0, nt - 1)], rs_send)
    wait_bytes(own_part.at[pl.ds(0, nt - 1)], ag_send)
    wait_bytes(ret_got.at[pl.ds(0, (nr - 1) * 8), :], re_send)


def write_out(a, b, c, a_out, b_out, c_out, sem):
    copies = [
        pltpu.make_async_copy(src, dst, sem.at[k])
        for k, (src, dst) in enumerate([(a, a_out), (b, b_out), (c, c_out)])
    ]
    for copy in copies:
        copy.start()
    for copy in copies:
        copy.wait()


def shards(
    features,
    gain,
    w_key,
    w_value,
    pool_a,
    pool_b,
    placement,
    need_lists,
    row_adapter,
    lengths,
    queries,
    cache_k,
    cache_v,
):
    nr, nt = lax.axis_size("replica"), lax.axis_size("tp")
    steps, rows, width = features.shape
    pool, _, rank = pool_a.shape
    cache_len = cache_k.shape[1]
    rows2 = steps * rows
    nvis = nr * 4
    ntot = nvis + rows2
    per_row = steps * GROUP
    half = HD // 2
    frequency = np.float32(THETA) ** (-(np.arange(half, dtype=np.float32) * 2.0) / HD)
    frequency = np.concatenate([frequency, frequency]).astype(np.float32)[None, :]
    vmem = pl.BlockSpec(memory_space=pltpu.VMEM)
    hbm = pl.BlockSpec(memory_space=pltpu.HBM)
    dma = pltpu.SemaphoreType.DMA
    att, nk, nv = pl.pallas_call(
        functools.partial(kernel, nr, nt),
        out_shape=(
            jax.ShapeDtypeStruct((rows2, width), BF16),
            jax.ShapeDtypeStruct((rows2, HD), BF16),
            jax.ShapeDtypeStruct((rows2, HD), BF16),
        ),
        in_specs=[hbm] * 15,
        out_specs=(vmem, vmem, vmem),
        scratch_shapes=[
            pltpu.VMEM((rows2, width), BF16),
            pltpu.VMEM((width // HD, HD), BF16),
            pltpu.VMEM((1, placement.shape[0]), jnp.int32),
            pltpu.VMEM(need_lists.shape[::-1], jnp.int32),
            pltpu.VMEM((1, rows), jnp.int32),
            pltpu.SMEM((rows,), jnp.int32),
            pltpu.VMEM((1, rows), jnp.int32),
            pltpu.VMEM((1, HD), F32),
            pltpu.VMEM((rows2, width), BF16),
            pltpu.VMEM((rows * per_row, HD), F32),
            pltpu.VMEM((rows, per_row, HD), BF16),
            pltpu.VMEM((nt * width, 2 * HD), BF16),
            pltpu.VMEM((pool * rank, width), BF16),
            pltpu.VMEM((pool * rank, HD), BF16),
            pltpu.VMEM((HD, pool * rank), BF16),
            pltpu.VMEM((rows, cache_len, HD), BF16),
            pltpu.VMEM((rows, cache_len, HD), BF16),
            pltpu.VMEM((nt, 16, HD), F32),
            pltpu.VMEM((nr * SENT, HD), BF16),
            pltpu.VMEM((nr * SENT, HD), F32),
            pltpu.VMEM((nr * SENT, HD), BF16),
            pltpu.VMEM((ntot, width), BF16),
            pltpu.VMEM((nt, rows2, width), BF16),
            pltpu.VMEM((nt, rank, nvis), BF16),
            pltpu.VMEM((nt, rank, rows2), BF16),
            pltpu.VMEM((pool * rank, nvis), BF16),
            pltpu.VMEM((nvis, HD), F32),
            pltpu.VMEM((nr * 8, HD), F32),
            pltpu.VMEM((rows, per_row, cache_len), F32),
            pltpu.VMEM((rows, per_row, cache_len), BF16),
            pltpu.VMEM((rows * per_row, rows2), BF16),
            pltpu.VMEM((rows2, 2 * HD), F32),
            pltpu.VMEM((rows * per_row, HD), F32),
            pltpu.VMEM((rows * per_row, 1), F32),
            pltpu.VMEM((rows * per_row, 1), F32),
            pltpu.VMEM((rows2, HD), F32),
            pltpu.VMEM((rows2, HD), F32),
            dma((9,)),
            dma((6,)),
            dma,
            dma,
            dma,
            dma,
            dma((2, max(nt // 2, 1), 2)),
            dma((nt, 2)),
            dma,
            dma,
            dma,
            dma,
            dma,
            dma,
        ],
        compiler_params=pltpu.CompilerParams(
            collective_id=0, has_side_effects=True, vmem_limit_bytes=60 * 2**20
        ),
        cost_estimate=pl.CostEstimate(
            flops=2 * 64 * 8192 * 256, bytes_accessed=12 * 2**20, transcendentals=0
        ),
    )(
        features.reshape(rows2, width),
        gain.reshape(width // HD, HD),
        placement.reshape(1, -1),
        need_lists.T,
        row_adapter.reshape(1, rows),
        lengths,
        lengths.reshape(1, rows),
        jnp.asarray(frequency),
        queries.reshape(rows2, width),
        w_key,
        w_value,
        pool_a.swapaxes(1, 2).reshape(pool * rank, width),
        pool_b.reshape(pool * rank, HD),
        cache_k,
        cache_v,
    )
    shapes = tuple(jax.ShapeDtypeStruct(x.shape, BF16) for x in (att, nk, nv))
    att, nk, nv = pl.pallas_call(
        write_out,
        out_shape=shapes,
        in_specs=[vmem] * 3,
        out_specs=(hbm,) * 3,
        scratch_shapes=[dma((3,))],
        compiler_params=pltpu.CompilerParams(vmem_limit_bytes=60 * 2**20),
    )(att, nk, nv)
    return (
        att.reshape(steps, rows, width),
        nk.reshape(steps, rows, HD),
        nv.reshape(steps, rows, HD),
    )


def solution(mesh):
    placed = (
        P(None, "replica", "tp"),
        P("tp"),
        P(None, "tp"),
        P(None, "tp"),
        P("replica", "tp", None),
        P("replica", None, "tp"),
        P(),
        P(),
        P("replica"),
        P("replica"),
        P(None, "replica", "tp"),
        P("replica", None, "tp"),
        P("replica", None, "tp"),
    )
    return jax.shard_map(
        shards,
        mesh=mesh,
        in_specs=placed,
        out_specs=(P(None, "replica", "tp"), P(None, "replica", "tp"), P(None, "replica", "tp")),
        check_vma=False,
    )
```

```python
import functools
import math

import jax
import jax.numpy as jnp
import numpy as np
from jax import lax
from jax.experimental import pallas as pl
from jax.experimental.pallas import tpu as pltpu
from jax.sharding import PartitionSpec as P

HD = 128
GROUP = 8
EPS = 1e-05
THETA = 500000.0
NEG = -1e30
MESH = pl.DeviceIdType.MESH
F32 = jnp.float32
BF16 = jnp.bfloat16
SENT = 32
NT = (((1,), (1,)), ((), ()))


def iota(shape, dim):
    return lax.broadcasted_iota(jnp.int32, shape, dim)


def kernel(
    nr,
    nt,
    f_hbm,
    gain_hbm,
    place_hbm,
    need_hbm,
    ra_hbm,
    len_s_hbm,
    len_hbm,
    freq_hbm,
    q_hbm,
    wk_hbm,
    wv_hbm,
    pa_hbm,
    pb_hbm,
    ck_hbm,
    cv_hbm,
    att_ref,
    nk_ref,
    nv_ref,
    f_ref,
    gain_ref,
    place_ref,
    need_ref,
    ra_ref,
    len_s,
    len_ref,
    freq_ref,
    q_in,
    q_wide,
    q_ref,
    wbuf,
    pa,
    pb,
    pbt,
    ck,
    cv,
    stats,
    msg,
    wide_rows,
    got,
    xall,
    ring,
    visit_part,
    own_part,
    expand,
    ret_send,
    ret_got,
    scores,
    weights,
    fresh_w,
    acc_kv,
    att_acc,
    top_ref,
    bottom_ref,
    cos_ref,
    sin_ref,
    small_sem,
    load_sem,
    st_send,
    st_recv,
    a2a_send,
    a2a_recv,
    ring_send,
    ring_recv,
    rs_send,
    rs_recv,
    ag_send,
    ag_recv,
    re_send,
    re_recv,
):
    r = lax.axis_index("replica")
    t = lax.axis_index("tp")
    rows2, width = f_ref.shape
    rows = rows2 // 2
    need_count = need_ref.shape[0]
    adapters = place_ref.shape[1]
    pool = adapters // nr
    rank = visit_part.shape[1]
    nvis = nr * 4
    ntot = nvis + rows2

    small = [
        pltpu.make_async_copy(a, b, small_sem.at[k])
        for k, (a, b) in enumerate(
            [
                (ra_hbm, ra_ref),
                (need_hbm, need_ref),
                (place_hbm, place_ref),
                (gain_hbm, gain_ref),
                (f_hbm, f_ref),
                (len_s_hbm, len_s),
                (len_hbm, len_ref),
                (freq_hbm, freq_ref),
                (q_hbm, q_in),
            ]
        )
    ]
    loads = [
        pltpu.make_async_copy(ck_hbm, ck, load_sem.at[0]),
        pltpu.make_async_copy(pa_hbm, pa, load_sem.at[1]),
        pltpu.make_async_copy(wk_hbm, wbuf.at[:, pl.ds(0, HD)], load_sem.at[2]),
        pltpu.make_async_copy(wv_hbm, wbuf.at[:, pl.ds(HD, HD)], load_sem.at[3]),
        pltpu.make_async_copy(pb_hbm, pb, load_sem.at[4]),
        pltpu.make_async_copy(cv_hbm, cv, load_sem.at[5]),
    ]
    for load in small:
        load.start()

    barrier = pltpu.get_barrier_semaphore()

    @pl.loop(1, nr)
    def _(k):
        pl.semaphore_signal(
            barrier, inc=1, device_id=(lax.rem(r + k, nr), t), device_id_type=MESH
        )

    @pl.loop(1, nt)
    def _(k):
        pl.semaphore_signal(
            barrier, inc=1, device_id=(r, lax.rem(t + k, nt)), device_id_type=MESH
        )

    for load in loads:
        load.start()

    for load in small[:3]:
        load.wait()
    ra = ra_ref[...]
    need = need_ref[...]
    mine = jnp.sum(
        jnp.where(iota(need.shape, 1) == r, need, 0).astype(F32), axis=1, keepdims=True
    )
    entry = iota((need_count, rows), 0) == ra
    wanted = jnp.sum(jnp.where(entry, mine, 0.0), axis=0, keepdims=True)
    place = place_ref[...]
    home = place // pool
    local = place - home * pool
    at_me = jnp.where(home == r, local + 1, 0)
    table = jnp.concatenate(
        [
            jnp.broadcast_to(x.astype(F32), (8, adapters))
            for x in (home, local, at_me)
        ],
        axis=0,
    ).astype(BF16)
    which = iota((adapters, rows), 0) == wanted.astype(jnp.int32)
    found = jnp.dot(
        table, jnp.where(which, 1.0, 0.0).astype(BF16), preferred_element_type=F32
    )
    owner = found[0:1].astype(jnp.int32)
    eye_r = iota((rows, rows), 0) == iota((rows, rows), 1)
    ra_f = ra.astype(F32)
    ra_col = jnp.sum(jnp.where(eye_r, ra_f, 0.0), axis=1, keepdims=True)
    twin = (ra_col == ra_f) & (iota((rows, rows), 0) < iota((rows, rows), 1))
    turn = jnp.sum(jnp.where(twin, 1.0, 0.0), axis=0, keepdims=True).astype(jnp.int32)
    is_far = ra < need_count
    code = jnp.where(is_far, owner * 4 + turn * 2, -1000)
    code2 = jnp.concatenate([code, code + 1], axis=1)
    pick = jnp.where(iota((nvis, rows2), 0) == code2, 1.0, 0.0).astype(BF16)

    small[3].wait()
    small[4].wait()
    pl.semaphore_wait(barrier, nr - 1 + nt - 1)
    right = (r, lax.rem(t + 1, nt))
    left = (r, lax.rem(t + nt - 1, nt))
    half = nt // 2

    def hop(which_way, h, c):
        if which_way == 0:
            have, there, to = (nt - (h - 1)) % nt, nt - h, right
        else:
            have, there, to = h - 1, h, left
        piece = pl.ds(c * rows, rows)
        src = f_ref.at[piece, :] if have == 0 else ring.at[have, piece, :]
        return pltpu.make_async_remote_copy(
            src_ref=src,
            dst_ref=ring.at[there, piece, :],
            send_sem=ring_send.at[which_way, h - 1, c],
            recv_sem=ring_recv.at[there, c],
            device_id=to,
            device_id_type=MESH,
        )

    def hops(h):
        if h < half:
            return [(0, 0), (1, 0), (0, 1), (1, 1)]
        return [(0, 0), (1, 1)]

    for way, c in hops(1):
        hop(way, 1, c).start()

    gain_rows = gain_ref[...].astype(F32)
    f32 = f_ref[...].astype(F32)
    lanes = HD
    chunks = width // lanes
    eye = iota((rows2, lanes), 0) == iota((rows2, lanes), 1)
    square_sum = jnp.sum(f32 * f32, axis=1, keepdims=True)
    square_row = jnp.sum(jnp.where(eye, square_sum, 0.0), axis=0, keepdims=True)
    stats[t] = jnp.concatenate(
        [gain_rows, jnp.broadcast_to(square_row, (8, lanes))], axis=0
    )
    own = jnp.concatenate(
        [
            f32[:, c * lanes : (c + 1) * lanes] * gain_rows[c : c + 1]
            for c in range(chunks)
        ],
        axis=1,
    ).astype(BF16)
    xall[pl.ds(nvis, rows2), :] = own

    picked_rows = jnp.dot(pick, own, preferred_element_type=F32)
    for j in range(chunks):
        wide_rows[pl.ds(j, nvis, stride=chunks), :] = picked_rows[
            :, j * lanes : (j + 1) * lanes
        ]
    msg[...] = wide_rows[...].astype(BF16)
    got[pl.ds(pl.multiple_of(r * SENT, SENT), SENT), :] = jnp.zeros((SENT, HD), BF16)
    ret_got[pl.ds(pl.multiple_of(r * 8, 8), 8), :] = jnp.zeros((8, HD), F32)

    @pl.loop(1, nr)
    def _(k):
        to = lax.rem(r + k, nr)
        pltpu.make_async_remote_copy(
            src_ref=msg.at[pl.ds(pl.multiple_of(to * SENT, SENT), SENT), :],
            dst_ref=got.at[pl.ds(pl.multiple_of(r * SENT, SENT), SENT), :],
            send_sem=a2a_send,
            recv_sem=a2a_recv,
            device_id=(to, t),
            device_id_type=MESH,
        ).start()

    @pl.loop(1, nt)
    def _(k):
        pltpu.make_async_remote_copy(
            src_ref=stats.at[t],
            dst_ref=stats.at[t],
            send_sem=st_send,
            recv_sem=st_recv,
            device_id=(r, lax.rem(t + k, nt)),
            device_id_type=MESH,
        ).start()

    def wait_bytes(ref, sem):
        pltpu.make_async_copy(ref, ref, sem).wait()

    packs = max(1, min(HD // nr, need_count))
    while need_count % packs:
        packs -= 1
    tall = need_count // packs
    packed = jnp.concatenate(
        [need[k * tall : (k + 1) * tall, :] for k in range(packs)], axis=1
    )
    p_iota = iota((adapters, packs * nr), 0)
    asked = p_iota == packed[0:1, :]
    for e in range(1, tall):
        asked = asked | (p_iota == packed[e : e + 1, :])
    visit = jnp.dot(
        table, jnp.where(asked, 1.0, 0.0).astype(BF16), preferred_element_type=F32
    )[16:24]
    wide = (packs * nr, nvis)
    spread = jnp.where(iota(wide, 1) // 4 == iota(wide, 0) % nr, 1.0, 0.0)
    visit_slot = jnp.dot(
        visit.astype(BF16), spread.astype(BF16), preferred_element_type=F32
    )[0:1].astype(jnp.int32) - 1
    own_slot = jnp.where(is_far, -1, ra - need_count)
    own_slot = jnp.concatenate([own_slot, own_slot], axis=1)
    slot_row = jnp.concatenate([visit_slot, own_slot], axis=1)

    scale = 1.0 / math.sqrt(HD)
    cache_len = ck.shape[1]
    per_row = 2 * GROUP

    def cached_scores(lo, hi):
        @pl.loop(lo, hi, unroll=8)
        def _(i):
            s = (
                lax.dot_general(q_ref[i], ck[i], NT, preferred_element_type=F32) * scale
            )
            live = iota(s.shape, 1) < len_s[i]
            scores[i] = jnp.where(live, s, NEG)

    def ring_stage(h, which_chunks=(0, 1)):
        for way, c in hops(h):
            if c not in which_chunks:
                continue
            hop(way, h, c).wait_recv()
            if (way, c) in (hops(h + 1) if h < half else []):
                hop(way, h + 1, c).start()

    for load in small[5:]:
        load.wait()
    for step in range(2):
        for g in range(GROUP):
            q_wide[pl.ds(step * GROUP + g, rows, stride=per_row), :] = q_in[
                step * rows : (step + 1) * rows, g * HD : (g + 1) * HD
            ].astype(F32)
    q_ref[...] = q_wide[...].astype(BF16).reshape(rows, per_row, HD)
    loads[0].wait()
    cached_scores(0, rows // 4)
    ring_stage(1, (0,))
    ring_stage(1, (1,))

    loads[1].wait()
    wait_bytes(got.at[pl.ds(0, (nr - 1) * SENT), :], a2a_recv)
    wide_rows[...] = got[...].astype(F32)
    for j in range(chunks):
        xall[pl.ds(0, nvis), j * lanes : (j + 1) * lanes] = wide_rows[
            pl.ds(j, nvis, stride=chunks), :
        ].astype(BF16)
    x = xall[...]
    group = 8
    picked = jnp.zeros((rank, ntot), F32)
    for base in range(0, pool, group):
        block = lax.dot_general(
            pa[base * rank : (base + group) * rank, :],
            x,
            NT,
            preferred_element_type=F32,
        )
        for s in range(group):
            picked += jnp.where(
                slot_row == base + s, block[s * rank : (s + 1) * rank], 0.0
            )
    visit_part[t] = picked[:, 0:nvis].astype(BF16)
    own_part[t] = picked[:, nvis:ntot].astype(BF16)

    def hand_round(ref, send_sem, recv_sem):
        @pl.loop(1, nt)
        def _(k):
            pltpu.make_async_remote_copy(
                src_ref=ref.at[t],
                dst_ref=ref.at[t],
                send_sem=send_sem,
                recv_sem=recv_sem,
                device_id=(r, lax.rem(t + k, nt)),
                device_id_type=MESH,
            ).start()

    hand_round(visit_part, rs_send, rs_recv)
    hand_round(own_part, ag_send, ag_recv)

    if half > 2:
        ring_stage(2, (0,))
    cached_scores(rows // 4, rows // 2)
    loads[4].wait()
    pbt[...] = pb[...].T
    if half > 2:
        ring_stage(2, (1,))

    def low_rank_terms(part, slots):
        total = part[0].astype(F32)
        for k in range(1, nt):
            total += part[k].astype(F32)
        coeffs = total.astype(BF16).astype(F32)
        count = slots.shape[1]
        for s in range(pool):
            expand[s * rank : (s + 1) * rank, 0:count] = jnp.where(
                slots == s, coeffs, 0.0
            ).astype(BF16)
        return jnp.dot(
            pbt[...], expand[:, 0:count], preferred_element_type=F32
        ).T

    wait_bytes(visit_part.at[pl.ds(0, nt - 1)], rs_recv)
    ret_send[...] = low_rank_terms(visit_part, visit_slot)

    @pl.loop(1, nr)
    def _(k):
        to = lax.rem(r + k, nr)
        pltpu.make_async_remote_copy(
            src_ref=ret_send.at[pl.ds(pl.multiple_of(to // 2 * 8, 8), 8), :],
            dst_ref=ret_got.at[pl.ds(pl.multiple_of(r * 8, 8), 8), :],
            send_sem=re_send,
            recv_sem=re_recv,
            device_id=(to, t),
            device_id_type=MESH,
        ).start()

    cached_scores(rows // 2, rows)
    for h in range(3, half):
        ring_stage(h)

    qrows = 8
    span = qrows * per_row
    for b in range(rows // qrows):
        s = scores[b * qrows : (b + 1) * qrows].reshape(span, cache_len)
        top = jnp.max(s, axis=1, keepdims=True)
        e_cache = jnp.exp(s - top)
        top_ref[b * span : (b + 1) * span, :] = top
        bottom_ref[b * span : (b + 1) * span, :] = jnp.sum(
            e_cache, axis=1, keepdims=True
        )
        weights[b * qrows : (b + 1) * qrows] = e_cache.astype(BF16).reshape(
            qrows, per_row, cache_len
        )

    wait_bytes(stats.at[pl.ds(0, nt - 1)], st_recv)
    square = stats[0, 8:16, :]
    for k in range(1, nt):
        square += stats[k, 8:16, :]
    inverse_row = lax.rsqrt(square[0:1] / (width * nt) + EPS)
    inverse = jnp.sum(jnp.where(eye, inverse_row, 0.0), axis=1, keepdims=True)

    def project(o):
        source = lax.rem(t + o, nt)
        block = f_ref[...] if o == 0 else ring[o]
        block = block.astype(F32) * inverse
        gains = stats[source][0:8]
        normed = jnp.concatenate(
            [
                block[:, c * lanes : (c + 1) * lanes] * gains[c : c + 1]
                for c in range(chunks)
            ],
            axis=1,
        ).astype(BF16)
        w = wbuf[pl.ds(pl.multiple_of(source * width, width), width), :]
        return jnp.dot(normed, w, preferred_element_type=F32)

    loads[2].wait()
    loads[3].wait()
    first = project(0) + project(nt - 1)
    if half > 1:
        first += project(1)
    acc_kv[...] = first

    length_row = len_ref[...].astype(F32)
    positions = jnp.sum(
        jnp.where(eye_r, length_row, 0.0), axis=1, keepdims=True
    )
    positions = jnp.concatenate([positions, positions + 1.0], axis=0)
    angle = positions * freq_ref[...]
    sign = jnp.where(iota((rows2, HD), 1) < HD // 2, -1.0, 1.0)
    cos_ref[...] = jnp.cos(angle)
    sin_ref[...] = jnp.sin(angle) * sign

    for h in range(3, half):
        acc_kv[...] += project(nt - h + 1) + project(h - 1)

    loads[5].wait()

    @pl.loop(0, rows, unroll=8)
    def _(i):
        att_acc[pl.ds(pl.multiple_of(i * per_row, per_row), per_row), :] = jnp.dot(
            weights[i], cv[i], preferred_element_type=F32
        )

    wait_bytes(own_part.at[pl.ds(0, nt - 1)], ag_recv)
    own_delta = low_rank_terms(own_part, own_slot)
    if half > 2:
        acc_kv[...] += project(nt - half + 1) + project(half - 1)
    ring_stage(half)
    acc_kv[...] += project(half)

    key = acc_kv[:, 0:HD]
    turned = key * cos_ref[...] + pltpu.roll(key, HD // 2, 1) * sin_ref[...]
    new_keys = turned.astype(BF16)
    nk_ref[...] = new_keys

    for b in range(rows // qrows):
        part_rows = slice(b * span, (b + 1) * span)
        q = q_ref[b * qrows : (b + 1) * qrows].reshape(span, HD)
        fresh = (
            lax.dot_general(q, new_keys, NT, preferred_element_type=F32) * scale
        )
        row_of = iota(fresh.shape, 0) // per_row + b * qrows
        step_of = iota(fresh.shape, 0) % per_row // GROUP
        column = iota(fresh.shape, 1)
        seen = (column == row_of) | ((column == row_of + rows) & (step_of == 1))
        fresh = jnp.where(seen, fresh, NEG)
        cache_top = top_ref[part_rows, :]
        top = jnp.maximum(cache_top, jnp.max(fresh, axis=1, keepdims=True))
        shrink = jnp.exp(cache_top - top)
        e_fresh = jnp.exp(fresh - top)
        bottom = bottom_ref[part_rows, :] * shrink + jnp.sum(
            e_fresh, axis=1, keepdims=True
        )
        share = 1.0 / bottom
        fresh_w[part_rows, :] = (e_fresh * share).astype(BF16)
        att_acc[part_rows, :] = att_acc[part_rows, :] * (shrink * share)

    code_f = jnp.where(
        is_far, owner * 8 + lax.rem(r, 2) * 4 + turn * 2, -1000
    ).astype(F32)
    code_col = jnp.sum(jnp.where(eye_r, code_f, 0.0), axis=1, keepdims=True)
    code_col = jnp.concatenate([code_col, code_col + 1.0], axis=0).astype(jnp.int32)
    back = jnp.where(iota((rows2, nr * 8), 1) == code_col, 1.0, 0.0).astype(BF16)
    wait_bytes(ret_got.at[pl.ds(0, (nr - 1) * 8), :], re_recv)
    returned = ret_got[...]
    high = returned.astype(BF16)
    low = (returned - high.astype(F32)).astype(BF16)
    far_delta = jnp.dot(back, high, preferred_element_type=F32) + jnp.dot(
        back, low, preferred_element_type=F32
    )
    new_values = (acc_kv[:, HD : 2 * HD] + inverse * (far_delta + own_delta)).astype(
        BF16
    )
    nv_ref[...] = new_values
    att_acc[...] += jnp.dot(fresh_w[...], new_values, preferred_element_type=F32)
    for step in range(2):
        for g in range(GROUP):
            att_ref[step * rows : (step + 1) * rows, g * HD : (g + 1) * HD] = att_acc[
                pl.ds(step * GROUP + g, rows, stride=per_row), :
            ].astype(BF16)

    for h in range(1, half + 1):
        for way, c in hops(h):
            hop(way, h, c).wait_send()
    wait_bytes(stats.at[pl.ds(0, nt - 1)], st_send)
    wait_bytes(msg.at[pl.ds(0, (nr - 1) * SENT), :], a2a_send)
    wait_bytes(visit_part.at[pl.ds(0, nt - 1)], rs_send)
    wait_bytes(own_part.at[pl.ds(0, nt - 1)], ag_send)
    wait_bytes(ret_got.at[pl.ds(0, (nr - 1) * 8), :], re_send)


def write_out(a, b, c, a_out, b_out, c_out, sem):
    copies = [
        pltpu.make_async_copy(src, dst, sem.at[k])
        for k, (src, dst) in enumerate([(a, a_out), (b, b_out), (c, c_out)])
    ]
    for copy in copies:
        copy.start()
    for copy in copies:
        copy.wait()


def shards(
    features,
    gain,
    w_key,
    w_value,
    pool_a,
    pool_b,
    placement,
    need_lists,
    row_adapter,
    lengths,
    queries,
    cache_k,
    cache_v,
):
    nr, nt = lax.axis_size("replica"), lax.axis_size("tp")
    steps, rows, width = features.shape
    pool, _, rank = pool_a.shape
    cache_len = cache_k.shape[1]
    rows2 = steps * rows
    nvis = nr * 4
    ntot = nvis + rows2
    per_row = steps * GROUP
    half = HD // 2
    frequency = np.float32(THETA) ** (-(np.arange(half, dtype=np.float32) * 2.0) / HD)
    frequency = np.concatenate([frequency, frequency]).astype(np.float32)[None, :]
    vmem = pl.BlockSpec(memory_space=pltpu.VMEM)
    hbm = pl.BlockSpec(memory_space=pltpu.HBM)
    dma = pltpu.SemaphoreType.DMA
    att, nk, nv = pl.pallas_call(
        functools.partial(kernel, nr, nt),
        out_shape=(
            jax.ShapeDtypeStruct((rows2, width), BF16),
            jax.ShapeDtypeStruct((rows2, HD), BF16),
            jax.ShapeDtypeStruct((rows2, HD), BF16),
        ),
        in_specs=[hbm] * 15,
        out_specs=(vmem, vmem, vmem),
        scratch_shapes=[
            pltpu.VMEM((rows2, width), BF16),
            pltpu.VMEM((width // HD, HD), BF16),
            pltpu.VMEM((1, placement.shape[0]), jnp.int32),
            pltpu.VMEM(need_lists.shape[::-1], jnp.int32),
            pltpu.VMEM((1, rows), jnp.int32),
            pltpu.SMEM((rows,), jnp.int32),
            pltpu.VMEM((1, rows), jnp.int32),
            pltpu.VMEM((1, HD), F32),
            pltpu.VMEM((rows2, width), BF16),
            pltpu.VMEM((rows * per_row, HD), F32),
            pltpu.VMEM((rows, per_row, HD), BF16),
            pltpu.VMEM((nt * width, 2 * HD), BF16),
            pltpu.VMEM((pool * rank, width), BF16),
            pltpu.VMEM((pool * rank, HD), BF16),
            pltpu.VMEM((HD, pool * rank), BF16),
            pltpu.VMEM((rows, cache_len, HD), BF16),
            pltpu.VMEM((rows, cache_len, HD), BF16),
            pltpu.VMEM((nt, 16, HD), F32),
            pltpu.VMEM((nr * SENT, HD), BF16),
            pltpu.VMEM((nr * SENT, HD), F32),
            pltpu.VMEM((nr * SENT, HD), BF16),
            pltpu.VMEM((ntot, width), BF16),
            pltpu.VMEM((nt, rows2, width), BF16),
            pltpu.VMEM((nt, rank, nvis), BF16),
            pltpu.VMEM((nt, rank, rows2), BF16),
            pltpu.VMEM((pool * rank, nvis), BF16),
            pltpu.VMEM((nvis, HD), F32),
            pltpu.VMEM((nr * 8, HD), F32),
            pltpu.VMEM((rows, per_row, cache_len), F32),
            pltpu.VMEM((rows, per_row, cache_len), BF16),
            pltpu.VMEM((rows * per_row, rows2), BF16),
            pltpu.VMEM((rows2, 2 * HD), F32),
            pltpu.VMEM((rows * per_row, HD), F32),
            pltpu.VMEM((rows * per_row, 1), F32),
            pltpu.VMEM((rows * per_row, 1), F32),
            pltpu.VMEM((rows2, HD), F32),
            pltpu.VMEM((rows2, HD), F32),
            dma((9,)),
            dma((6,)),
            dma,
            dma,
            dma,
            dma,
            dma((2, max(nt // 2, 1), 2)),
            dma((nt, 2)),
            dma,
            dma,
            dma,
            dma,
            dma,
            dma,
        ],
        compiler_params=pltpu.CompilerParams(
            collective_id=0, has_side_effects=True, vmem_limit_bytes=60 * 2**20
        ),
        cost_estimate=pl.CostEstimate(
            flops=2 * 64 * 8192 * 256, bytes_accessed=12 * 2**20, transcendentals=0
        ),
    )(
        features.reshape(rows2, width),
        gain.reshape(width // HD, HD),
        placement.reshape(1, -1),
        need_lists.T,
        row_adapter.reshape(1, rows),
        lengths,
        lengths.reshape(1, rows),
        jnp.asarray(frequency),
        queries.reshape(rows2, width),
        w_key,
        w_value,
        pool_a.swapaxes(1, 2).reshape(pool * rank, width),
        pool_b.reshape(pool * rank, HD),
        cache_k,
        cache_v,
    )
    shapes = tuple(jax.ShapeDtypeStruct(x.shape, BF16) for x in (att, nk, nv))
    att, nk, nv = pl.pallas_call(
        write_out,
        out_shape=shapes,
        in_specs=[vmem] * 3,
        out_specs=(hbm,) * 3,
        scratch_shapes=[dma((3,))],
        compiler_params=pltpu.CompilerParams(vmem_limit_bytes=60 * 2**20),
    )(att, nk, nv)
    return (
        att.reshape(steps, rows, width),
        nk.reshape(steps, rows, HD),
        nv.reshape(steps, rows, HD),
    )


def solution(mesh):
    placed = (
        P(None, "replica", "tp"),
        P("tp"),
        P(None, "tp"),
        P(None, "tp"),
        P("replica", "tp", None),
        P("replica", None, "tp"),
        P(),
        P(),
        P("replica"),
        P("replica"),
        P(None, "replica", "tp"),
        P("replica", None, "tp"),
        P("replica", None, "tp"),
    )
    return jax.shard_map(
        shards,
        mesh=mesh,
        in_specs=placed,
        out_specs=(P(None, "replica", "tp"), P(None, "replica", "tp"), P(None, "replica", "tp")),
        check_vma=False,
    )
```

```python
import functools
import math

import jax
import jax.numpy as jnp
import numpy as np
from jax import lax
from jax.experimental import pallas as pl
from jax.experimental.pallas import tpu as pltpu
from jax.sharding import PartitionSpec as P

HD = 128
GROUP = 8
EPS = 1e-05
THETA = 500000.0
NEG = -1e30
MESH = pl.DeviceIdType.MESH
F32 = jnp.float32
BF16 = jnp.bfloat16
SENT = 32
NT = (((1,), (1,)), ((), ()))


def iota(shape, dim):
    return lax.broadcasted_iota(jnp.int32, shape, dim)


def kernel(
    nr,
    nt,
    f_hbm,
    gain_hbm,
    place_hbm,
    need_hbm,
    ra_hbm,
    len_s_hbm,
    len_hbm,
    freq_hbm,
    q_hbm,
    wk_hbm,
    wv_hbm,
    pa_hbm,
    pb_hbm,
    ck_hbm,
    cv_hbm,
    att_ref,
    nk_ref,
    nv_ref,
    f_ref,
    gain_ref,
    place_ref,
    need_ref,
    ra_ref,
    len_s,
    len_ref,
    freq_ref,
    q_in,
    q_wide,
    q_ref,
    wbuf,
    pa,
    pb,
    pbt,
    ck,
    cv,
    stats,
    msg,
    wide_rows,
    got,
    xall,
    ring,
    visit_part,
    own_part,
    expand,
    ret_send,
    ret_got,
    scores,
    weights,
    fresh_w,
    acc_kv,
    att_acc,
    top_ref,
    bottom_ref,
    cos_ref,
    sin_ref,
    small_sem,
    load_sem,
    st_send,
    st_recv,
    a2a_send,
    a2a_recv,
    ring_send,
    ring_recv,
    rs_send,
    rs_recv,
    ag_send,
    ag_recv,
    re_send,
    re_recv,
):
    r = lax.axis_index("replica")
    t = lax.axis_index("tp")
    rows2, width = f_ref.shape
    rows = rows2 // 2
    need_count = need_ref.shape[0]
    adapters = place_ref.shape[1]
    pool = adapters // nr
    rank = visit_part.shape[1]
    nvis = nr * 4
    ntot = nvis + rows2

    small = [
        pltpu.make_async_copy(a, b, small_sem.at[k])
        for k, (a, b) in enumerate(
            [
                (ra_hbm, ra_ref),
                (need_hbm, need_ref),
                (place_hbm, place_ref),
                (gain_hbm, gain_ref),
                (f_hbm, f_ref),
                (len_s_hbm, len_s),
                (len_hbm, len_ref),
                (freq_hbm, freq_ref),
                (q_hbm, q_in),
            ]
        )
    ]
    loads = [
        pltpu.make_async_copy(ck_hbm, ck, load_sem.at[0]),
        pltpu.make_async_copy(pa_hbm, pa, load_sem.at[1]),
        pltpu.make_async_copy(wk_hbm, wbuf.at[:, pl.ds(0, HD)], load_sem.at[2]),
        pltpu.make_async_copy(wv_hbm, wbuf.at[:, pl.ds(HD, HD)], load_sem.at[3]),
        pltpu.make_async_copy(pb_hbm, pb, load_sem.at[4]),
        pltpu.make_async_copy(cv_hbm, cv, load_sem.at[5]),
    ]
    for load in small:
        load.start()

    barrier = pltpu.get_barrier_semaphore()

    @pl.loop(1, nr, unroll=True)
    def _(k):
        pl.semaphore_signal(
            barrier, inc=1, device_id=(lax.rem(r + k, nr), t), device_id_type=MESH
        )

    @pl.loop(1, nt)
    def _(k):
        pl.semaphore_signal(
            barrier, inc=1, device_id=(r, lax.rem(t + k, nt)), device_id_type=MESH
        )

    for load in loads:
        load.start()

    for load in small[:3]:
        load.wait()
    ra = ra_ref[...]
    need = need_ref[...]
    mine = jnp.sum(
        jnp.where(iota(need.shape, 1) == r, need, 0).astype(F32), axis=1, keepdims=True
    )
    entry = iota((need_count, rows), 0) == ra
    wanted = jnp.sum(jnp.where(entry, mine, 0.0), axis=0, keepdims=True)
    place = place_ref[...]
    home = place // pool
    local = place - home * pool
    at_me = jnp.where(home == r, local + 1, 0)
    table = jnp.concatenate(
        [
            jnp.broadcast_to(x.astype(F32), (8, adapters))
            for x in (home, local, at_me)
        ],
        axis=0,
    ).astype(BF16)
    which = iota((adapters, rows), 0) == wanted.astype(jnp.int32)
    found = jnp.dot(
        table, jnp.where(which, 1.0, 0.0).astype(BF16), preferred_element_type=F32
    )
    owner = found[0:1].astype(jnp.int32)
    eye_r = iota((rows, rows), 0) == iota((rows, rows), 1)
    ra_f = ra.astype(F32)
    ra_col = jnp.sum(jnp.where(eye_r, ra_f, 0.0), axis=1, keepdims=True)
    twin = (ra_col == ra_f) & (iota((rows, rows), 0) < iota((rows, rows), 1))
    turn = jnp.sum(jnp.where(twin, 1.0, 0.0), axis=0, keepdims=True).astype(jnp.int32)
    is_far = ra < need_count
    code = jnp.where(is_far, owner * 4 + turn * 2, -1000)
    code2 = jnp.concatenate([code, code + 1], axis=1)
    pick = jnp.where(iota((nvis, rows2), 0) == code2, 1.0, 0.0).astype(BF16)

    small[3].wait()
    small[4].wait()
    pl.semaphore_wait(barrier, nr - 1 + nt - 1)
    right = (r, lax.rem(t + 1, nt))
    left = (r, lax.rem(t + nt - 1, nt))
    half = nt // 2

    def hop(which_way, h, c):
        if which_way == 0:
            have, there, to = (nt - (h - 1)) % nt, nt - h, right
        else:
            have, there, to = h - 1, h, left
        piece = pl.ds(c * rows, rows)
        src = f_ref.at[piece, :] if have == 0 else ring.at[have, piece, :]
        return pltpu.make_async_remote_copy(
            src_ref=src,
            dst_ref=ring.at[there, piece, :],
            send_sem=ring_send.at[which_way, h - 1, c],
            recv_sem=ring_recv.at[there, c],
            device_id=to,
            device_id_type=MESH,
        )

    def hops(h):
        if h < half:
            return [(0, 0), (1, 0), (0, 1), (1, 1)]
        return [(0, 0), (1, 1)]

    for way, c in hops(1):
        hop(way, 1, c).start()

    gain_rows = gain_ref[...].astype(F32)
    f32 = f_ref[...].astype(F32)
    lanes = HD
    chunks = width // lanes
    eye = iota((rows2, lanes), 0) == iota((rows2, lanes), 1)
    square_sum = jnp.sum(f32 * f32, axis=1, keepdims=True)
    square_row = jnp.sum(jnp.where(eye, square_sum, 0.0), axis=0, keepdims=True)
    stats[t] = jnp.concatenate(
        [gain_rows, jnp.broadcast_to(square_row, (8, lanes))], axis=0
    )
    own = jnp.concatenate(
        [
            f32[:, c * lanes : (c + 1) * lanes] * gain_rows[c : c + 1]
            for c in range(chunks)
        ],
        axis=1,
    ).astype(BF16)
    xall[pl.ds(nvis, rows2), :] = own

    picked_rows = jnp.dot(pick, own, preferred_element_type=F32)
    for j in range(chunks):
        wide_rows[pl.ds(j, nvis, stride=chunks), :] = picked_rows[
            :, j * lanes : (j + 1) * lanes
        ]
    msg[...] = wide_rows[...].astype(BF16)
    got[pl.ds(pl.multiple_of(r * SENT, SENT), SENT), :] = jnp.zeros((SENT, HD), BF16)
    ret_got[pl.ds(pl.multiple_of(r * 8, 8), 8), :] = jnp.zeros((8, HD), F32)

    @pl.loop(1, nr, unroll=True)
    def _(k):
        to = lax.rem(r + k, nr)
        pltpu.make_async_remote_copy(
            src_ref=msg.at[pl.ds(pl.multiple_of(to * SENT, SENT), SENT), :],
            dst_ref=got.at[pl.ds(pl.multiple_of(r * SENT, SENT), SENT), :],
            send_sem=a2a_send,
            recv_sem=a2a_recv,
            device_id=(to, t),
            device_id_type=MESH,
        ).start()

    @pl.loop(1, nt)
    def _(k):
        pltpu.make_async_remote_copy(
            src_ref=stats.at[t],
            dst_ref=stats.at[t],
            send_sem=st_send,
            recv_sem=st_recv,
            device_id=(r, lax.rem(t + k, nt)),
            device_id_type=MESH,
        ).start()

    def wait_bytes(ref, sem):
        pltpu.make_async_copy(ref, ref, sem).wait()

    packs = max(1, min(HD // nr, need_count))
    while need_count % packs:
        packs -= 1
    tall = need_count // packs
    packed = jnp.concatenate(
        [need[k * tall : (k + 1) * tall, :] for k in range(packs)], axis=1
    )
    p_iota = iota((adapters, packs * nr), 0)
    asked = p_iota == packed[0:1, :]
    for e in range(1, tall):
        asked = asked | (p_iota == packed[e : e + 1, :])
    visit = jnp.dot(
        table, jnp.where(asked, 1.0, 0.0).astype(BF16), preferred_element_type=F32
    )[16:24]
    wide = (packs * nr, nvis)
    spread = jnp.where(iota(wide, 1) // 4 == iota(wide, 0) % nr, 1.0, 0.0)
    visit_slot = jnp.dot(
        visit.astype(BF16), spread.astype(BF16), preferred_element_type=F32
    )[0:1].astype(jnp.int32) - 1
    own_slot = jnp.where(is_far, -1, ra - need_count)
    own_slot = jnp.concatenate([own_slot, own_slot], axis=1)
    slot_row = jnp.concatenate([visit_slot, own_slot], axis=1)

    scale = 1.0 / math.sqrt(HD)
    cache_len = ck.shape[1]
    per_row = 2 * GROUP

    def cached_scores(lo, hi):
        @pl.loop(lo, hi, unroll=8)
        def _(i):
            s = (
                lax.dot_general(q_ref[i], ck[i], NT, preferred_element_type=F32) * scale
            )
            live = iota(s.shape, 1) < len_s[i]
            scores[i] = jnp.where(live, s, NEG)

    def ring_stage(h, which_chunks=(0, 1)):
        for way, c in hops(h):
            if c not in which_chunks:
                continue
            hop(way, h, c).wait_recv()
            if (way, c) in (hops(h + 1) if h < half else []):
                hop(way, h + 1, c).start()

    for load in small[5:]:
        load.wait()
    for step in range(2):
        for g in range(GROUP):
            q_wide[pl.ds(step * GROUP + g, rows, stride=per_row), :] = q_in[
                step * rows : (step + 1) * rows, g * HD : (g + 1) * HD
            ].astype(F32)
    q_ref[...] = q_wide[...].astype(BF16).reshape(rows, per_row, HD)
    loads[0].wait()
    cached_scores(0, rows // 4)
    ring_stage(1, (0,))
    ring_stage(1, (1,))

    loads[1].wait()
    wait_bytes(got.at[pl.ds(0, (nr - 1) * SENT), :], a2a_recv)
    wide_rows[...] = got[...].astype(F32)
    for j in range(chunks):
        xall[pl.ds(0, nvis), j * lanes : (j + 1) * lanes] = wide_rows[
            pl.ds(j, nvis, stride=chunks), :
        ].astype(BF16)
    x = xall[...]
    group = 8
    picked = jnp.zeros((rank, ntot), F32)
    for base in range(0, pool, group):
        block = lax.dot_general(
            pa[base * rank : (base + group) * rank, :],
            x,
            NT,
            preferred_element_type=F32,
        )
        for s in range(group):
            picked += jnp.where(
                slot_row == base + s, block[s * rank : (s + 1) * rank], 0.0
            )
    visit_part[t] = picked[:, 0:nvis].astype(BF16)
    own_part[t] = picked[:, nvis:ntot].astype(BF16)

    def hand_round(ref, send_sem, recv_sem):
        @pl.loop(1, nt, unroll=True)
        def _(k):
            pltpu.make_async_remote_copy(
                src_ref=ref.at[t],
                dst_ref=ref.at[t],
                send_sem=send_sem,
                recv_sem=recv_sem,
                device_id=(r, lax.rem(t + k, nt)),
                device_id_type=MESH,
            ).start()

    hand_round(visit_part, rs_send, rs_recv)
    hand_round(own_part, ag_send, ag_recv)

    if half > 2:
        ring_stage(2, (0,))
    cached_scores(rows // 4, rows // 2)
    loads[4].wait()
    pbt[...] = pb[...].T
    if half > 2:
        ring_stage(2, (1,))

    def low_rank_terms(part, slots):
        total = part[0].astype(F32)
        for k in range(1, nt):
            total += part[k].astype(F32)
        coeffs = total.astype(BF16).astype(F32)
        count = slots.shape[1]
        for s in range(pool):
            expand[s * rank : (s + 1) * rank, 0:count] = jnp.where(
                slots == s, coeffs, 0.0
            ).astype(BF16)
        return jnp.dot(
            pbt[...], expand[:, 0:count], preferred_element_type=F32
        ).T

    wait_bytes(visit_part.at[pl.ds(0, nt - 1)], rs_recv)
    ret_send[...] = low_rank_terms(visit_part, visit_slot)

    @pl.loop(1, nr, unroll=True)
    def _(k):
        to = lax.rem(r + k, nr)
        pltpu.make_async_remote_copy(
            src_ref=ret_send.at[pl.ds(pl.multiple_of(to // 2 * 8, 8), 8), :],
            dst_ref=ret_got.at[pl.ds(pl.multiple_of(r * 8, 8), 8), :],
            send_sem=re_send,
            recv_sem=re_recv,
            device_id=(to, t),
            device_id_type=MESH,
        ).start()

    cached_scores(rows // 2, rows)
    for h in range(3, half):
        ring_stage(h)

    qrows = 8
    span = qrows * per_row
    for b in range(rows // qrows):
        s = scores[b * qrows : (b + 1) * qrows].reshape(span, cache_len)
        top = jnp.max(s, axis=1, keepdims=True)
        e_cache = jnp.exp(s - top)
        top_ref[b * span : (b + 1) * span, :] = top
        bottom_ref[b * span : (b + 1) * span, :] = jnp.sum(
            e_cache, axis=1, keepdims=True
        )
        weights[b * qrows : (b + 1) * qrows] = e_cache.astype(BF16).reshape(
            qrows, per_row, cache_len
        )

    wait_bytes(stats.at[pl.ds(0, nt - 1)], st_recv)
    square = stats[0, 8:16, :]
    for k in range(1, nt):
        square += stats[k, 8:16, :]
    inverse_row = lax.rsqrt(square[0:1] / (width * nt) + EPS)
    inverse = jnp.sum(jnp.where(eye, inverse_row, 0.0), axis=1, keepdims=True)

    def project(o):
        source = lax.rem(t + o, nt)
        block = f_ref[...] if o == 0 else ring[o]
        block = block.astype(F32) * inverse
        gains = stats[source][0:8]
        normed = jnp.concatenate(
            [
                block[:, c * lanes : (c + 1) * lanes] * gains[c : c + 1]
                for c in range(chunks)
            ],
            axis=1,
        ).astype(BF16)
        w = wbuf[pl.ds(pl.multiple_of(source * width, width), width), :]
        return jnp.dot(normed, w, preferred_element_type=F32)

    loads[2].wait()
    loads[3].wait()
    first = project(0) + project(nt - 1)
    if half > 1:
        first += project(1)
    acc_kv[...] = first

    length_row = len_ref[...].astype(F32)
    positions = jnp.sum(
        jnp.where(eye_r, length_row, 0.0), axis=1, keepdims=True
    )
    front = iota((rows, HD), 1) < HD // 2
    angle = (positions + jnp.where(front, 0.0, 1.0)) * freq_ref[...]
    cosine = jnp.cos(angle)
    sine = jnp.sin(angle)
    cosine_turned = pltpu.roll(cosine, HD // 2, 1)
    sine_turned = pltpu.roll(sine, HD // 2, 1)
    cos_ref[0:rows, :] = jnp.where(front, cosine, cosine_turned)
    cos_ref[rows:rows2, :] = jnp.where(front, cosine_turned, cosine)
    sin_ref[0:rows, :] = jnp.where(front, -sine, sine_turned)
    sin_ref[rows:rows2, :] = jnp.where(front, -sine_turned, sine)

    for h in range(3, half):
        acc_kv[...] += project(nt - h + 1) + project(h - 1)

    loads[5].wait()

    @pl.loop(0, rows, unroll=8)
    def _(i):
        att_acc[pl.ds(pl.multiple_of(i * per_row, per_row), per_row), :] = jnp.dot(
            weights[i], cv[i], preferred_element_type=F32
        )

    wait_bytes(own_part.at[pl.ds(0, nt - 1)], ag_recv)
    own_delta = low_rank_terms(own_part, own_slot)
    if half > 2:
        acc_kv[...] += project(nt - half + 1) + project(half - 1)
    ring_stage(half)
    acc_kv[...] += project(half)

    key = acc_kv[:, 0:HD]
    turned = key * cos_ref[...] + pltpu.roll(key, HD // 2, 1) * sin_ref[...]
    new_keys = turned.astype(BF16)
    nk_ref[...] = new_keys

    for b in range(rows // qrows):
        part_rows = slice(b * span, (b + 1) * span)
        q = q_ref[b * qrows : (b + 1) * qrows].reshape(span, HD)
        fresh = (
            lax.dot_general(q, new_keys, NT, preferred_element_type=F32) * scale
        )
        row_of = iota(fresh.shape, 0) // per_row + b * qrows
        step_of = iota(fresh.shape, 0) % per_row // GROUP
        column = iota(fresh.shape, 1)
        seen = (column == row_of) | ((column == row_of + rows) & (step_of == 1))
        fresh = jnp.where(seen, fresh, NEG)
        cache_top = top_ref[part_rows, :]
        top = jnp.maximum(cache_top, jnp.max(fresh, axis=1, keepdims=True))
        shrink = jnp.exp(cache_top - top)
        e_fresh = jnp.exp(fresh - top)
        bottom = bottom_ref[part_rows, :] * shrink + jnp.sum(
            e_fresh, axis=1, keepdims=True
        )
        share = 1.0 / bottom
        fresh_w[part_rows, :] = (e_fresh * share).astype(BF16)
        att_acc[part_rows, :] = att_acc[part_rows, :] * (shrink * share)

    code_f = jnp.where(
        is_far, owner * 8 + lax.rem(r, 2) * 4 + turn * 2, -1000
    ).astype(F32)
    code_col = jnp.sum(jnp.where(eye_r, code_f, 0.0), axis=1, keepdims=True)
    code_col = jnp.concatenate([code_col, code_col + 1.0], axis=0).astype(jnp.int32)
    back = jnp.where(iota((rows2, nr * 8), 1) == code_col, 1.0, 0.0).astype(BF16)
    wait_bytes(ret_got.at[pl.ds(0, (nr - 1) * 8), :], re_recv)
    returned = ret_got[...]
    high = returned.astype(BF16)
    low = (returned - high.astype(F32)).astype(BF16)
    far_delta = jnp.dot(back, high, preferred_element_type=F32) + jnp.dot(
        back, low, preferred_element_type=F32
    )
    new_values = (acc_kv[:, HD : 2 * HD] + inverse * (far_delta + own_delta)).astype(
        BF16
    )
    nv_ref[...] = new_values
    att_acc[...] += jnp.dot(fresh_w[...], new_values, preferred_element_type=F32)
    for step in range(2):
        for g in range(GROUP):
            att_ref[step * rows : (step + 1) * rows, g * HD : (g + 1) * HD] = att_acc[
                pl.ds(step * GROUP + g, rows, stride=per_row), :
            ].astype(BF16)

    for h in range(1, half + 1):
        for way, c in hops(h):
            hop(way, h, c).wait_send()
    wait_bytes(stats.at[pl.ds(0, nt - 1)], st_send)
    wait_bytes(msg.at[pl.ds(0, (nr - 1) * SENT), :], a2a_send)
    wait_bytes(visit_part.at[pl.ds(0, nt - 1)], rs_send)
    wait_bytes(own_part.at[pl.ds(0, nt - 1)], ag_send)
    wait_bytes(ret_got.at[pl.ds(0, (nr - 1) * 8), :], re_send)


def write_out(a, b, c, a_out, b_out, c_out, sem):
    copies = [
        pltpu.make_async_copy(src, dst, sem.at[k])
        for k, (src, dst) in enumerate([(a, a_out), (b, b_out), (c, c_out)])
    ]
    for copy in copies:
        copy.start()
    for copy in copies:
        copy.wait()


def shards(
    features,
    gain,
    w_key,
    w_value,
    pool_a,
    pool_b,
    placement,
    need_lists,
    row_adapter,
    lengths,
    queries,
    cache_k,
    cache_v,
):
    nr, nt = lax.axis_size("replica"), lax.axis_size("tp")
    steps, rows, width = features.shape
    pool, _, rank = pool_a.shape
    cache_len = cache_k.shape[1]
    rows2 = steps * rows
    nvis = nr * 4
    ntot = nvis + rows2
    per_row = steps * GROUP
    half = HD // 2
    frequency = np.float32(THETA) ** (-(np.arange(half, dtype=np.float32) * 2.0) / HD)
    frequency = np.concatenate([frequency, frequency]).astype(np.float32)[None, :]
    vmem = pl.BlockSpec(memory_space=pltpu.VMEM)
    hbm = pl.BlockSpec(memory_space=pltpu.HBM)
    dma = pltpu.SemaphoreType.DMA
    att, nk, nv = pl.pallas_call(
        functools.partial(kernel, nr, nt),
        out_shape=(
            jax.ShapeDtypeStruct((rows2, width), BF16),
            jax.ShapeDtypeStruct((rows2, HD), BF16),
            jax.ShapeDtypeStruct((rows2, HD), BF16),
        ),
        in_specs=[hbm] * 15,
        out_specs=(vmem, vmem, vmem),
        scratch_shapes=[
            pltpu.VMEM((rows2, width), BF16),
            pltpu.VMEM((width // HD, HD), BF16),
            pltpu.VMEM((1, placement.shape[0]), jnp.int32),
            pltpu.VMEM(need_lists.shape[::-1], jnp.int32),
            pltpu.VMEM((1, rows), jnp.int32),
            pltpu.SMEM((rows,), jnp.int32),
            pltpu.VMEM((1, rows), jnp.int32),
            pltpu.VMEM((1, HD), F32),
            pltpu.VMEM((rows2, width), BF16),
            pltpu.VMEM((rows * per_row, HD), F32),
            pltpu.VMEM((rows, per_row, HD), BF16),
            pltpu.VMEM((nt * width, 2 * HD), BF16),
            pltpu.VMEM((pool * rank, width), BF16),
            pltpu.VMEM((pool * rank, HD), BF16),
            pltpu.VMEM((HD, pool * rank), BF16),
            pltpu.VMEM((rows, cache_len, HD), BF16),
            pltpu.VMEM((rows, cache_len, HD), BF16),
            pltpu.VMEM((nt, 16, HD), F32),
            pltpu.VMEM((nr * SENT, HD), BF16),
            pltpu.VMEM((nr * SENT, HD), F32),
            pltpu.VMEM((nr * SENT, HD), BF16),
            pltpu.VMEM((ntot, width), BF16),
            pltpu.VMEM((nt, rows2, width), BF16),
            pltpu.VMEM((nt, rank, nvis), BF16),
            pltpu.VMEM((nt, rank, rows2), BF16),
            pltpu.VMEM((pool * rank, nvis), BF16),
            pltpu.VMEM((nvis, HD), F32),
            pltpu.VMEM((nr * 8, HD), F32),
            pltpu.VMEM((rows, per_row, cache_len), F32),
            pltpu.VMEM((rows, per_row, cache_len), BF16),
            pltpu.VMEM((rows * per_row, rows2), BF16),
            pltpu.VMEM((rows2, 2 * HD), F32),
            pltpu.VMEM((rows * per_row, HD), F32),
            pltpu.VMEM((rows * per_row, 1), F32),
            pltpu.VMEM((rows * per_row, 1), F32),
            pltpu.VMEM((rows2, HD), F32),
            pltpu.VMEM((rows2, HD), F32),
            dma((9,)),
            dma((6,)),
            dma,
            dma,
            dma,
            dma,
            dma((2, max(nt // 2, 1), 2)),
            dma((nt, 2)),
            dma,
            dma,
            dma,
            dma,
            dma,
            dma,
        ],
        compiler_params=pltpu.CompilerParams(
            collective_id=0, has_side_effects=True, vmem_limit_bytes=60 * 2**20
        ),
        cost_estimate=pl.CostEstimate(
            flops=2 * 64 * 8192 * 256, bytes_accessed=12 * 2**20, transcendentals=0
        ),
    )(
        features.reshape(rows2, width),
        gain.reshape(width // HD, HD),
        placement.reshape(1, -1),
        need_lists.T,
        row_adapter.reshape(1, rows),
        lengths,
        lengths.reshape(1, rows),
        jnp.asarray(frequency),
        queries.reshape(rows2, width),
        w_key,
        w_value,
        pool_a.swapaxes(1, 2).reshape(pool * rank, width),
        pool_b.reshape(pool * rank, HD),
        cache_k,
        cache_v,
    )
    shapes = tuple(jax.ShapeDtypeStruct(x.shape, BF16) for x in (att, nk, nv))
    att, nk, nv = pl.pallas_call(
        write_out,
        out_shape=shapes,
        in_specs=[vmem] * 3,
        out_specs=(hbm,) * 3,
        scratch_shapes=[dma((3,))],
        compiler_params=pltpu.CompilerParams(vmem_limit_bytes=60 * 2**20),
    )(att, nk, nv)
    return (
        att.reshape(steps, rows, width),
        nk.reshape(steps, rows, HD),
        nv.reshape(steps, rows, HD),
    )


def solution(mesh):
    placed = (
        P(None, "replica", "tp"),
        P("tp"),
        P(None, "tp"),
        P(None, "tp"),
        P("replica", "tp", None),
        P("replica", None, "tp"),
        P(),
        P(),
        P("replica"),
        P("replica"),
        P(None, "replica", "tp"),
        P("replica", None, "tp"),
        P("replica", None, "tp"),
    )
    return jax.shard_map(
        shards,
        mesh=mesh,
        in_specs=placed,
        out_specs=(P(None, "replica", "tp"), P(None, "replica", "tp"), P(None, "replica", "tp")),
        check_vma=False,
    )
```

```python
import functools
import math

import jax
import jax.numpy as jnp
import numpy as np
from jax import lax
from jax.experimental import pallas as pl
from jax.experimental.pallas import tpu as pltpu
from jax.sharding import PartitionSpec as P

HD = 128
GROUP = 8
EPS = 1e-05
THETA = 500000.0
NEG = -1e30
MESH = pl.DeviceIdType.MESH
F32 = jnp.float32
BF16 = jnp.bfloat16
SENT = 32
NT = (((1,), (1,)), ((), ()))


def iota(shape, dim):
    return lax.broadcasted_iota(jnp.int32, shape, dim)


def kernel(
    nr,
    nt,
    f_hbm,
    gain_hbm,
    place_hbm,
    need_hbm,
    ra_hbm,
    len_s_hbm,
    len_hbm,
    freq_hbm,
    q_hbm,
    wk_hbm,
    wv_hbm,
    pa_hbm,
    pb_hbm,
    ck_hbm,
    cv_hbm,
    att_ref,
    nk_ref,
    nv_ref,
    f_ref,
    gain_ref,
    place_ref,
    need_ref,
    ra_ref,
    len_s,
    len_ref,
    freq_ref,
    q_in,
    q_wide,
    q_ref,
    wbuf,
    pa,
    pb,
    pbt,
    ck,
    cv,
    stats,
    msg,
    wide_rows,
    got,
    xall,
    ring,
    visit_part,
    own_part,
    expand,
    ret_send,
    ret_got,
    scores,
    weights,
    fresh_w,
    acc_kv,
    att_acc,
    top_ref,
    bottom_ref,
    cos_ref,
    sin_ref,
    small_sem,
    load_sem,
    st_send,
    st_recv,
    a2a_send,
    a2a_recv,
    ring_send,
    ring_recv,
    rs_send,
    rs_recv,
    ag_send,
    ag_recv,
    re_send,
    re_recv,
):
    r = lax.axis_index("replica")
    t = lax.axis_index("tp")
    rows2, width = f_ref.shape
    rows = rows2 // 2
    need_count = need_ref.shape[0]
    adapters = place_ref.shape[1]
    pool = adapters // nr
    rank = visit_part.shape[1]
    nvis = nr * 4
    ntot = nvis + rows2

    small = [
        pltpu.make_async_copy(a, b, small_sem.at[k])
        for k, (a, b) in enumerate(
            [
                (ra_hbm, ra_ref),
                (need_hbm, need_ref),
                (place_hbm, place_ref),
                (gain_hbm, gain_ref),
                (f_hbm, f_ref),
                (len_s_hbm, len_s),
                (len_hbm, len_ref),
                (freq_hbm, freq_ref),
                (q_hbm, q_in),
            ]
        )
    ]
    loads = [
        pltpu.make_async_copy(ck_hbm, ck, load_sem.at[0]),
        pltpu.make_async_copy(pa_hbm, pa, load_sem.at[1]),
        pltpu.make_async_copy(wk_hbm, wbuf.at[:, pl.ds(0, HD)], load_sem.at[2]),
        pltpu.make_async_copy(wv_hbm, wbuf.at[:, pl.ds(HD, HD)], load_sem.at[3]),
        pltpu.make_async_copy(pb_hbm, pb, load_sem.at[4]),
        pltpu.make_async_copy(cv_hbm, cv, load_sem.at[5]),
    ]
    for load in small:
        load.start()

    barrier = pltpu.get_barrier_semaphore()

    @pl.loop(1, nr, unroll=True)
    def _(k):
        pl.semaphore_signal(
            barrier, inc=1, device_id=(lax.rem(r + k, nr), t), device_id_type=MESH
        )

    @pl.loop(1, nt)
    def _(k):
        pl.semaphore_signal(
            barrier, inc=1, device_id=(r, lax.rem(t + k, nt)), device_id_type=MESH
        )

    for load in loads:
        load.start()

    for load in small[:3]:
        load.wait()
    ra = ra_ref[...]
    need = need_ref[...]
    mine = jnp.sum(
        jnp.where(iota(need.shape, 1) == r, need, 0).astype(F32), axis=1, keepdims=True
    )
    entry = iota((need_count, rows), 0) == ra
    wanted = jnp.sum(jnp.where(entry, mine, 0.0), axis=0, keepdims=True)
    place = place_ref[...]
    home = place // pool
    local = place - home * pool
    at_me = jnp.where(home == r, local + 1, 0)
    table = jnp.concatenate(
        [
            jnp.broadcast_to(x.astype(F32), (8, adapters))
            for x in (home, local, at_me)
        ],
        axis=0,
    ).astype(BF16)
    which = iota((adapters, rows), 0) == wanted.astype(jnp.int32)
    found = jnp.dot(
        table, jnp.where(which, 1.0, 0.0).astype(BF16), preferred_element_type=F32
    )
    owner = found[0:1].astype(jnp.int32)
    eye_r = iota((rows, rows), 0) == iota((rows, rows), 1)
    ra_f = ra.astype(F32)
    ra_col = jnp.sum(jnp.where(eye_r, ra_f, 0.0), axis=1, keepdims=True)
    twin = (ra_col == ra_f) & (iota((rows, rows), 0) < iota((rows, rows), 1))
    turn = jnp.sum(jnp.where(twin, 1.0, 0.0), axis=0, keepdims=True).astype(jnp.int32)
    is_far = ra < need_count
    code = jnp.where(is_far, owner * 4 + turn * 2, -1000)
    code2 = jnp.concatenate([code, code + 1], axis=1)
    pick = jnp.where(iota((nvis, rows2), 0) == code2, 1.0, 0.0).astype(BF16)

    small[3].wait()
    small[4].wait()
    pl.semaphore_wait(barrier, nr - 1 + nt - 1)
    right = (r, lax.rem(t + 1, nt))
    left = (r, lax.rem(t + nt - 1, nt))
    half = nt // 2

    def hop(which_way, h, c):
        if which_way == 0:
            have, there, to = (nt - (h - 1)) % nt, nt - h, right
        else:
            have, there, to = h - 1, h, left
        piece = pl.ds(c * rows, rows)
        src = f_ref.at[piece, :] if have == 0 else ring.at[have, piece, :]
        return pltpu.make_async_remote_copy(
            src_ref=src,
            dst_ref=ring.at[there, piece, :],
            send_sem=ring_send.at[which_way, h - 1, c],
            recv_sem=ring_recv.at[there, c],
            device_id=to,
            device_id_type=MESH,
        )

    def hops(h):
        if h < half:
            return [(0, 0), (1, 0), (0, 1), (1, 1)]
        return [(0, 0), (1, 1)]

    for way, c in hops(1):
        hop(way, 1, c).start()

    gain_rows = gain_ref[...].astype(F32)
    f32 = f_ref[...].astype(F32)
    lanes = HD
    chunks = width // lanes
    eye = iota((rows2, lanes), 0) == iota((rows2, lanes), 1)
    square_sum = jnp.sum(f32 * f32, axis=1, keepdims=True)
    square_row = jnp.sum(jnp.where(eye, square_sum, 0.0), axis=0, keepdims=True)
    stats[t] = jnp.concatenate(
        [gain_rows, jnp.broadcast_to(square_row, (8, lanes))], axis=0
    )
    own = jnp.concatenate(
        [
            f32[:, c * lanes : (c + 1) * lanes] * gain_rows[c : c + 1]
            for c in range(chunks)
        ],
        axis=1,
    ).astype(BF16)
    xall[pl.ds(nvis, rows2), :] = own

    picked_rows = jnp.dot(pick, own, preferred_element_type=F32)
    for j in range(chunks):
        wide_rows[pl.ds(j, nvis, stride=chunks), :] = picked_rows[
            :, j * lanes : (j + 1) * lanes
        ]
    msg[...] = wide_rows[...].astype(BF16)
    got[pl.ds(pl.multiple_of(r * SENT, SENT), SENT), :] = jnp.zeros((SENT, HD), BF16)
    ret_got[pl.ds(pl.multiple_of(r * 8, 8), 8), :] = jnp.zeros((8, HD), F32)

    @pl.loop(1, nr, unroll=True)
    def _(k):
        to = lax.rem(r + k, nr)
        pltpu.make_async_remote_copy(
            src_ref=msg.at[pl.ds(pl.multiple_of(to * SENT, SENT), SENT), :],
            dst_ref=got.at[pl.ds(pl.multiple_of(r * SENT, SENT), SENT), :],
            send_sem=a2a_send,
            recv_sem=a2a_recv,
            device_id=(to, t),
            device_id_type=MESH,
        ).start()

    @pl.loop(1, nt)
    def _(k):
        pltpu.make_async_remote_copy(
            src_ref=stats.at[t],
            dst_ref=stats.at[t],
            send_sem=st_send,
            recv_sem=st_recv,
            device_id=(r, lax.rem(t + k, nt)),
            device_id_type=MESH,
        ).start()

    def wait_bytes(ref, sem):
        pltpu.make_async_copy(ref, ref, sem).wait()

    packs = max(1, min(HD // nr, need_count))
    while need_count % packs:
        packs -= 1
    tall = need_count // packs
    packed = jnp.concatenate(
        [need[k * tall : (k + 1) * tall, :] for k in range(packs)], axis=1
    )
    p_iota = iota((adapters, packs * nr), 0)
    asked = p_iota == packed[0:1, :]
    for e in range(1, tall):
        asked = asked | (p_iota == packed[e : e + 1, :])
    visit = jnp.dot(
        table, jnp.where(asked, 1.0, 0.0).astype(BF16), preferred_element_type=F32
    )[16:24]
    wide = (packs * nr, nvis)
    spread = jnp.where(iota(wide, 1) // 4 == iota(wide, 0) % nr, 1.0, 0.0)
    visit_slot = jnp.dot(
        visit.astype(BF16), spread.astype(BF16), preferred_element_type=F32
    )[0:1].astype(jnp.int32) - 1
    own_slot = jnp.where(is_far, -1, ra - need_count)
    own_slot = jnp.concatenate([own_slot, own_slot], axis=1)
    slot_row = jnp.concatenate([visit_slot, own_slot], axis=1)

    scale = 1.0 / math.sqrt(HD)
    cache_len = ck.shape[1]
    per_row = 2 * GROUP

    def cached_scores(lo, hi):
        @pl.loop(lo, hi, unroll=8)
        def _(i):
            s = (
                lax.dot_general(q_ref[i], ck[i], NT, preferred_element_type=F32) * scale
            )
            live = iota(s.shape, 1) < len_s[i]
            scores[i] = jnp.where(live, s, NEG)

    def ring_stage(h, which_chunks=(0, 1)):
        for way, c in hops(h):
            if c not in which_chunks:
                continue
            hop(way, h, c).wait_recv()
            if (way, c) in (hops(h + 1) if h < half else []):
                hop(way, h + 1, c).start()

    ring_stage(1, (0,))
    ring_stage(1, (1,))

    loads[1].wait()
    wait_bytes(got.at[pl.ds(0, (nr - 1) * SENT), :], a2a_recv)
    wide_rows[...] = got[...].astype(F32)
    for j in range(chunks):
        xall[pl.ds(0, nvis), j * lanes : (j + 1) * lanes] = wide_rows[
            pl.ds(j, nvis, stride=chunks), :
        ].astype(BF16)
    x = xall[...]
    group = 8
    picked = jnp.zeros((rank, ntot), F32)
    for base in range(0, pool, group):
        block = lax.dot_general(
            pa[base * rank : (base + group) * rank, :],
            x,
            NT,
            preferred_element_type=F32,
        )
        for s in range(group):
            picked += jnp.where(
                slot_row == base + s, block[s * rank : (s + 1) * rank], 0.0
            )
    visit_part[t] = picked[:, 0:nvis].astype(BF16)
    own_part[t] = picked[:, nvis:ntot].astype(BF16)

    def hand_round(ref, send_sem, recv_sem):
        @pl.loop(1, nt, unroll=True)
        def _(k):
            pltpu.make_async_remote_copy(
                src_ref=ref.at[t],
                dst_ref=ref.at[t],
                send_sem=send_sem,
                recv_sem=recv_sem,
                device_id=(r, lax.rem(t + k, nt)),
                device_id_type=MESH,
            ).start()

    hand_round(visit_part, rs_send, rs_recv)
    hand_round(own_part, ag_send, ag_recv)

    if half > 2:
        ring_stage(2, (0,))
    for load in small[5:]:
        load.wait()
    for step in range(2):
        for g in range(GROUP):
            q_wide[pl.ds(step * GROUP + g, rows, stride=per_row), :] = q_in[
                step * rows : (step + 1) * rows, g * HD : (g + 1) * HD
            ].astype(F32)
    q_ref[...] = q_wide[...].astype(BF16).reshape(rows, per_row, HD)
    loads[0].wait()
    cached_scores(0, rows // 2)
    loads[4].wait()
    pbt[...] = pb[...].T
    if half > 2:
        ring_stage(2, (1,))

    def low_rank_terms(part, slots):
        total = part[0].astype(F32)
        for k in range(1, nt):
            total += part[k].astype(F32)
        coeffs = total.astype(BF16).astype(F32)
        count = slots.shape[1]
        for s in range(pool):
            expand[s * rank : (s + 1) * rank, 0:count] = jnp.where(
                slots == s, coeffs, 0.0
            ).astype(BF16)
        return jnp.dot(
            pbt[...], expand[:, 0:count], preferred_element_type=F32
        ).T

    wait_bytes(visit_part.at[pl.ds(0, nt - 1)], rs_recv)
    ret_send[...] = low_rank_terms(visit_part, visit_slot)

    @pl.loop(1, nr, unroll=True)
    def _(k):
        to = lax.rem(r + k, nr)
        pltpu.make_async_remote_copy(
            src_ref=ret_send.at[pl.ds(pl.multiple_of(to // 2 * 8, 8), 8), :],
            dst_ref=ret_got.at[pl.ds(pl.multiple_of(r * 8, 8), 8), :],
            send_sem=re_send,
            recv_sem=re_recv,
            device_id=(to, t),
            device_id_type=MESH,
        ).start()

    cached_scores(rows // 2, rows)
    for h in range(3, half):
        ring_stage(h)

    qrows = 8
    span = qrows * per_row
    for b in range(rows // qrows):
        s = scores[b * qrows : (b + 1) * qrows].reshape(span, cache_len)
        top = jnp.max(s, axis=1, keepdims=True)
        e_cache = jnp.exp(s - top)
        top_ref[b * span : (b + 1) * span, :] = top
        bottom_ref[b * span : (b + 1) * span, :] = jnp.sum(
            e_cache, axis=1, keepdims=True
        )
        weights[b * qrows : (b + 1) * qrows] = e_cache.astype(BF16).reshape(
            qrows, per_row, cache_len
        )

    wait_bytes(stats.at[pl.ds(0, nt - 1)], st_recv)
    square = stats[0, 8:16, :]
    for k in range(1, nt):
        square += stats[k, 8:16, :]
    inverse_row = lax.rsqrt(square[0:1] / (width * nt) + EPS)
    inverse = jnp.sum(jnp.where(eye, inverse_row, 0.0), axis=1, keepdims=True)

    def project(o):
        source = lax.rem(t + o, nt)
        block = f_ref[...] if o == 0 else ring[o]
        block = block.astype(F32) * inverse
        gains = stats[source][0:8]
        normed = jnp.concatenate(
            [
                block[:, c * lanes : (c + 1) * lanes] * gains[c : c + 1]
                for c in range(chunks)
            ],
            axis=1,
        ).astype(BF16)
        w = wbuf[pl.ds(pl.multiple_of(source * width, width), width), :]
        return jnp.dot(normed, w, preferred_element_type=F32)

    loads[2].wait()
    loads[3].wait()
    first = project(0) + project(nt - 1)
    if half > 1:
        first += project(1)
    acc_kv[...] = first

    length_row = len_ref[...].astype(F32)
    positions = jnp.sum(
        jnp.where(eye_r, length_row, 0.0), axis=1, keepdims=True
    )
    front = iota((rows, HD), 1) < HD // 2
    angle = (positions + jnp.where(front, 0.0, 1.0)) * freq_ref[...]
    cosine = jnp.cos(angle)
    sine = jnp.sin(angle)
    cosine_turned = pltpu.roll(cosine, HD // 2, 1)
    sine_turned = pltpu.roll(sine, HD // 2, 1)
    cos_ref[0:rows, :] = jnp.where(front, cosine, cosine_turned)
    cos_ref[rows:rows2, :] = jnp.where(front, cosine_turned, cosine)
    sin_ref[0:rows, :] = jnp.where(front, -sine, sine_turned)
    sin_ref[rows:rows2, :] = jnp.where(front, -sine_turned, sine)

    for h in range(3, half):
        acc_kv[...] += project(nt - h + 1) + project(h - 1)

    loads[5].wait()

    @pl.loop(0, rows, unroll=8)
    def _(i):
        att_acc[pl.ds(pl.multiple_of(i * per_row, per_row), per_row), :] = jnp.dot(
            weights[i], cv[i], preferred_element_type=F32
        )

    wait_bytes(own_part.at[pl.ds(0, nt - 1)], ag_recv)
    own_delta = low_rank_terms(own_part, own_slot)
    if half > 2:
        acc_kv[...] += project(nt - half + 1) + project(half - 1)
    ring_stage(half)
    acc_kv[...] += project(half)

    key = acc_kv[:, 0:HD]
    turned = key * cos_ref[...] + pltpu.roll(key, HD // 2, 1) * sin_ref[...]
    new_keys = turned.astype(BF16)
    nk_ref[...] = new_keys

    for b in range(rows // qrows):
        part_rows = slice(b * span, (b + 1) * span)
        q = q_ref[b * qrows : (b + 1) * qrows].reshape(span, HD)
        fresh = (
            lax.dot_general(q, new_keys, NT, preferred_element_type=F32) * scale
        )
        row_of = iota(fresh.shape, 0) // per_row + b * qrows
        step_of = iota(fresh.shape, 0) % per_row // GROUP
        column = iota(fresh.shape, 1)
        seen = (column == row_of) | ((column == row_of + rows) & (step_of == 1))
        fresh = jnp.where(seen, fresh, NEG)
        cache_top = top_ref[part_rows, :]
        top = jnp.maximum(cache_top, jnp.max(fresh, axis=1, keepdims=True))
        shrink = jnp.exp(cache_top - top)
        e_fresh = jnp.exp(fresh - top)
        bottom = bottom_ref[part_rows, :] * shrink + jnp.sum(
            e_fresh, axis=1, keepdims=True
        )
        share = 1.0 / bottom
        fresh_w[part_rows, :] = (e_fresh * share).astype(BF16)
        att_acc[part_rows, :] = att_acc[part_rows, :] * (shrink * share)

    code_f = jnp.where(
        is_far, owner * 8 + lax.rem(r, 2) * 4 + turn * 2, -1000
    ).astype(F32)
    code_col = jnp.sum(jnp.where(eye_r, code_f, 0.0), axis=1, keepdims=True)
    code_col = jnp.concatenate([code_col, code_col + 1.0], axis=0).astype(jnp.int32)
    back = jnp.where(iota((rows2, nr * 8), 1) == code_col, 1.0, 0.0).astype(BF16)
    wait_bytes(ret_got.at[pl.ds(0, (nr - 1) * 8), :], re_recv)
    returned = ret_got[...]
    high = returned.astype(BF16)
    low = (returned - high.astype(F32)).astype(BF16)
    far_delta = jnp.dot(back, high, preferred_element_type=F32) + jnp.dot(
        back, low, preferred_element_type=F32
    )
    new_values = (acc_kv[:, HD : 2 * HD] + inverse * (far_delta + own_delta)).astype(
        BF16
    )
    nv_ref[...] = new_values
    att_acc[...] += jnp.dot(fresh_w[...], new_values, preferred_element_type=F32)
    for step in range(2):
        for g in range(GROUP):
            att_ref[step * rows : (step + 1) * rows, g * HD : (g + 1) * HD] = att_acc[
                pl.ds(step * GROUP + g, rows, stride=per_row), :
            ].astype(BF16)

    for h in range(1, half + 1):
        for way, c in hops(h):
            hop(way, h, c).wait_send()
    wait_bytes(stats.at[pl.ds(0, nt - 1)], st_send)
    wait_bytes(msg.at[pl.ds(0, (nr - 1) * SENT), :], a2a_send)
    wait_bytes(visit_part.at[pl.ds(0, nt - 1)], rs_send)
    wait_bytes(own_part.at[pl.ds(0, nt - 1)], ag_send)
    wait_bytes(ret_got.at[pl.ds(0, (nr - 1) * 8), :], re_send)


def write_out(a, b, c, a_out, b_out, c_out, sem):
    copies = [
        pltpu.make_async_copy(src, dst, sem.at[k])
        for k, (src, dst) in enumerate([(a, a_out), (b, b_out), (c, c_out)])
    ]
    for copy in copies:
        copy.start()
    for copy in copies:
        copy.wait()


def shards(
    features,
    gain,
    w_key,
    w_value,
    pool_a,
    pool_b,
    placement,
    need_lists,
    row_adapter,
    lengths,
    queries,
    cache_k,
    cache_v,
):
    nr, nt = lax.axis_size("replica"), lax.axis_size("tp")
    steps, rows, width = features.shape
    pool, _, rank = pool_a.shape
    cache_len = cache_k.shape[1]
    rows2 = steps * rows
    nvis = nr * 4
    ntot = nvis + rows2
    per_row = steps * GROUP
    half = HD // 2
    frequency = np.float32(THETA) ** (-(np.arange(half, dtype=np.float32) * 2.0) / HD)
    frequency = np.concatenate([frequency, frequency]).astype(np.float32)[None, :]
    vmem = pl.BlockSpec(memory_space=pltpu.VMEM)
    hbm = pl.BlockSpec(memory_space=pltpu.HBM)
    dma = pltpu.SemaphoreType.DMA
    att, nk, nv = pl.pallas_call(
        functools.partial(kernel, nr, nt),
        out_shape=(
            jax.ShapeDtypeStruct((rows2, width), BF16),
            jax.ShapeDtypeStruct((rows2, HD), BF16),
            jax.ShapeDtypeStruct((rows2, HD), BF16),
        ),
        in_specs=[hbm] * 15,
        out_specs=(vmem, vmem, vmem),
        scratch_shapes=[
            pltpu.VMEM((rows2, width), BF16),
            pltpu.VMEM((width // HD, HD), BF16),
            pltpu.VMEM((1, placement.shape[0]), jnp.int32),
            pltpu.VMEM(need_lists.shape[::-1], jnp.int32),
            pltpu.VMEM((1, rows), jnp.int32),
            pltpu.SMEM((rows,), jnp.int32),
            pltpu.VMEM((1, rows), jnp.int32),
            pltpu.VMEM((1, HD), F32),
            pltpu.VMEM((rows2, width), BF16),
            pltpu.VMEM((rows * per_row, HD), F32),
            pltpu.VMEM((rows, per_row, HD), BF16),
            pltpu.VMEM((nt * width, 2 * HD), BF16),
            pltpu.VMEM((pool * rank, width), BF16),
            pltpu.VMEM((pool * rank, HD), BF16),
            pltpu.VMEM((HD, pool * rank), BF16),
            pltpu.VMEM((rows, cache_len, HD), BF16),
            pltpu.VMEM((rows, cache_len, HD), BF16),
            pltpu.VMEM((nt, 16, HD), F32),
            pltpu.VMEM((nr * SENT, HD), BF16),
            pltpu.VMEM((nr * SENT, HD), F32),
            pltpu.VMEM((nr * SENT, HD), BF16),
            pltpu.VMEM((ntot, width), BF16),
            pltpu.VMEM((nt, rows2, width), BF16),
            pltpu.VMEM((nt, rank, nvis), BF16),
            pltpu.VMEM((nt, rank, rows2), BF16),
            pltpu.VMEM((pool * rank, nvis), BF16),
            pltpu.VMEM((nvis, HD), F32),
            pltpu.VMEM((nr * 8, HD), F32),
            pltpu.VMEM((rows, per_row, cache_len), F32),
            pltpu.VMEM((rows, per_row, cache_len), BF16),
            pltpu.VMEM((rows * per_row, rows2), BF16),
            pltpu.VMEM((rows2, 2 * HD), F32),
            pltpu.VMEM((rows * per_row, HD), F32),
            pltpu.VMEM((rows * per_row, 1), F32),
            pltpu.VMEM((rows * per_row, 1), F32),
            pltpu.VMEM((rows2, HD), F32),
            pltpu.VMEM((rows2, HD), F32),
            dma((9,)),
            dma((6,)),
            dma,
            dma,
            dma,
            dma,
            dma((2, max(nt // 2, 1), 2)),
            dma((nt, 2)),
            dma,
            dma,
            dma,
            dma,
            dma,
            dma,
        ],
        compiler_params=pltpu.CompilerParams(
            collective_id=0, has_side_effects=True, vmem_limit_bytes=60 * 2**20
        ),
        cost_estimate=pl.CostEstimate(
            flops=2 * 64 * 8192 * 256, bytes_accessed=12 * 2**20, transcendentals=0
        ),
    )(
        features.reshape(rows2, width),
        gain.reshape(width // HD, HD),
        placement.reshape(1, -1),
        need_lists.T,
        row_adapter.reshape(1, rows),
        lengths,
        lengths.reshape(1, rows),
        jnp.asarray(frequency),
        queries.reshape(rows2, width),
        w_key,
        w_value,
        pool_a.swapaxes(1, 2).reshape(pool * rank, width),
        pool_b.reshape(pool * rank, HD),
        cache_k,
        cache_v,
    )
    shapes = tuple(jax.ShapeDtypeStruct(x.shape, BF16) for x in (att, nk, nv))
    att, nk, nv = pl.pallas_call(
        write_out,
        out_shape=shapes,
        in_specs=[vmem] * 3,
        out_specs=(hbm,) * 3,
        scratch_shapes=[dma((3,))],
        compiler_params=pltpu.CompilerParams(vmem_limit_bytes=60 * 2**20),
    )(att, nk, nv)
    return (
        att.reshape(steps, rows, width),
        nk.reshape(steps, rows, HD),
        nv.reshape(steps, rows, HD),
    )


def solution(mesh):
    placed = (
        P(None, "replica", "tp"),
        P("tp"),
        P(None, "tp"),
        P(None, "tp"),
        P("replica", "tp", None),
        P("replica", None, "tp"),
        P(),
        P(),
        P("replica"),
        P("replica"),
        P(None, "replica", "tp"),
        P("replica", None, "tp"),
        P("replica", None, "tp"),
    )
    return jax.shard_map(
        shards,
        mesh=mesh,
        in_specs=placed,
        out_specs=(P(None, "replica", "tp"), P(None, "replica", "tp"), P(None, "replica", "tp")),
        check_vma=False,
    )
```

```python
import functools
import math

import jax
import jax.numpy as jnp
import numpy as np
from jax import lax
from jax.experimental import pallas as pl
from jax.experimental.pallas import tpu as pltpu
from jax.sharding import PartitionSpec as P

HD = 128
GROUP = 8
EPS = 1e-05
THETA = 500000.0
NEG = -1e30
MESH = pl.DeviceIdType.MESH
F32 = jnp.float32
BF16 = jnp.bfloat16
SENT = 32
NT = (((1,), (1,)), ((), ()))


def iota(shape, dim):
    return lax.broadcasted_iota(jnp.int32, shape, dim)


def kernel(
    nr,
    nt,
    f_hbm,
    gain_hbm,
    place_hbm,
    need_hbm,
    ra_hbm,
    len_s_hbm,
    len_hbm,
    freq_hbm,
    q_hbm,
    wk_hbm,
    wv_hbm,
    pa_hbm,
    pb_hbm,
    ck_hbm,
    cv_hbm,
    att_ref,
    nk_ref,
    nv_ref,
    f_ref,
    gain_ref,
    place_ref,
    need_ref,
    ra_ref,
    len_s,
    len_ref,
    freq_ref,
    q_in,
    q_wide,
    q_ref,
    wbuf,
    pa,
    pb,
    pbt,
    ck,
    cv,
    stats,
    msg,
    wide_rows,
    got,
    xall,
    ring,
    visit_part,
    own_part,
    expand,
    ret_send,
    ret_got,
    scores,
    weights,
    fresh_w,
    acc_kv,
    att_acc,
    top_ref,
    bottom_ref,
    cos_ref,
    sin_ref,
    small_sem,
    load_sem,
    st_send,
    st_recv,
    a2a_send,
    a2a_recv,
    ring_send,
    ring_recv,
    rs_send,
    rs_recv,
    ag_send,
    ag_recv,
    re_send,
    re_recv,
):
    r = lax.axis_index("replica")
    t = lax.axis_index("tp")
    rows2, width = f_ref.shape
    rows = rows2 // 2
    need_count = need_ref.shape[0]
    adapters = place_ref.shape[1]
    pool = adapters // nr
    rank = visit_part.shape[1]
    nvis = nr * 4
    ntot = nvis + rows2

    small = [
        pltpu.make_async_copy(a, b, small_sem.at[k])
        for k, (a, b) in enumerate(
            [
                (ra_hbm, ra_ref),
                (need_hbm, need_ref),
                (place_hbm, place_ref),
                (gain_hbm, gain_ref),
                (f_hbm, f_ref),
                (len_s_hbm, len_s),
                (len_hbm, len_ref),
                (freq_hbm, freq_ref),
                (q_hbm, q_in),
            ]
        )
    ]
    loads = [
        pltpu.make_async_copy(ck_hbm, ck, load_sem.at[0]),
        pltpu.make_async_copy(pa_hbm, pa, load_sem.at[1]),
        pltpu.make_async_copy(wk_hbm, wbuf.at[:, pl.ds(0, HD)], load_sem.at[2]),
        pltpu.make_async_copy(wv_hbm, wbuf.at[:, pl.ds(HD, HD)], load_sem.at[3]),
        pltpu.make_async_copy(pb_hbm, pb, load_sem.at[4]),
        pltpu.make_async_copy(cv_hbm, cv, load_sem.at[5]),
    ]
    for load in small:
        load.start()

    barrier = pltpu.get_barrier_semaphore()

    @pl.loop(1, nr, unroll=True)
    def _(k):
        pl.semaphore_signal(
            barrier, inc=1, device_id=(lax.rem(r + k, nr), t), device_id_type=MESH
        )

    @pl.loop(1, nt)
    def _(k):
        pl.semaphore_signal(
            barrier, inc=1, device_id=(r, lax.rem(t + k, nt)), device_id_type=MESH
        )

    for load in loads:
        load.start()

    for load in small[:3]:
        load.wait()
    ra = ra_ref[...]
    need = need_ref[...]
    mine = jnp.sum(
        jnp.where(iota(need.shape, 1) == r, need, 0).astype(F32), axis=1, keepdims=True
    )
    entry = iota((need_count, rows), 0) == ra
    wanted = jnp.sum(jnp.where(entry, mine, 0.0), axis=0, keepdims=True)
    place = place_ref[...]
    home = place // pool
    local = place - home * pool
    at_me = jnp.where(home == r, local + 1, 0)
    table = jnp.concatenate(
        [
            jnp.broadcast_to(x.astype(F32), (8, adapters))
            for x in (home, local, at_me)
        ],
        axis=0,
    ).astype(BF16)
    which = iota((adapters, rows), 0) == wanted.astype(jnp.int32)
    found = jnp.dot(
        table, jnp.where(which, 1.0, 0.0).astype(BF16), preferred_element_type=F32
    )
    owner = found[0:1].astype(jnp.int32)
    eye_r = iota((rows, rows), 0) == iota((rows, rows), 1)
    ra_f = ra.astype(F32)
    ra_col = jnp.sum(jnp.where(eye_r, ra_f, 0.0), axis=1, keepdims=True)
    twin = (ra_col == ra_f) & (iota((rows, rows), 0) < iota((rows, rows), 1))
    turn = jnp.sum(jnp.where(twin, 1.0, 0.0), axis=0, keepdims=True).astype(jnp.int32)
    is_far = ra < need_count
    code = jnp.where(is_far, owner * 4 + turn * 2, -1000)
    code2 = jnp.concatenate([code, code + 1], axis=1)
    pick = jnp.where(iota((nvis, rows2), 0) == code2, 1.0, 0.0).astype(BF16)

    small[3].wait()
    small[4].wait()
    pl.semaphore_wait(barrier, nr - 1 + nt - 1)
    right = (r, lax.rem(t + 1, nt))
    left = (r, lax.rem(t + nt - 1, nt))
    half = nt // 2

    def hop(which_way, h, c):
        if which_way == 0:
            have, there, to = (nt - (h - 1)) % nt, nt - h, right
        else:
            have, there, to = h - 1, h, left
        piece = pl.ds(c * rows, rows)
        src = f_ref.at[piece, :] if have == 0 else ring.at[have, piece, :]
        return pltpu.make_async_remote_copy(
            src_ref=src,
            dst_ref=ring.at[there, piece, :],
            send_sem=ring_send.at[which_way, h - 1, c],
            recv_sem=ring_recv.at[there, c],
            device_id=to,
            device_id_type=MESH,
        )

    def hops(h):
        if h < half:
            return [(0, 0), (1, 0), (0, 1), (1, 1)]
        return [(0, 0), (1, 1)]

    for way, c in hops(1):
        hop(way, 1, c).start()

    gain_rows = gain_ref[...].astype(F32)
    f32 = f_ref[...].astype(F32)
    lanes = HD
    chunks = width // lanes
    eye = iota((rows2, lanes), 0) == iota((rows2, lanes), 1)
    square_sum = jnp.sum(f32 * f32, axis=1, keepdims=True)
    square_row = jnp.sum(jnp.where(eye, square_sum, 0.0), axis=0, keepdims=True)
    stats[t] = jnp.concatenate(
        [gain_rows, jnp.broadcast_to(square_row, (8, lanes))], axis=0
    )
    own = jnp.concatenate(
        [
            f32[:, c * lanes : (c + 1) * lanes] * gain_rows[c : c + 1]
            for c in range(chunks)
        ],
        axis=1,
    ).astype(BF16)
    xall[pl.ds(nvis, rows2), :] = own

    picked_rows = jnp.dot(pick, own, preferred_element_type=F32)
    for j in range(chunks):
        wide_rows[pl.ds(j, nvis, stride=chunks), :] = picked_rows[
            :, j * lanes : (j + 1) * lanes
        ]
    msg[...] = wide_rows[...].astype(BF16)
    got[pl.ds(pl.multiple_of(r * SENT, SENT), SENT), :] = jnp.zeros((SENT, HD), BF16)
    ret_got[pl.ds(pl.multiple_of(r * 8, 8), 8), :] = jnp.zeros((8, HD), F32)

    @pl.loop(1, nr, unroll=True)
    def _(k):
        to = lax.rem(r + k, nr)
        pltpu.make_async_remote_copy(
            src_ref=msg.at[pl.ds(pl.multiple_of(to * SENT, SENT), SENT), :],
            dst_ref=got.at[pl.ds(pl.multiple_of(r * SENT, SENT), SENT), :],
            send_sem=a2a_send,
            recv_sem=a2a_recv,
            device_id=(to, t),
            device_id_type=MESH,
        ).start()

    @pl.loop(1, nt)
    def _(k):
        pltpu.make_async_remote_copy(
            src_ref=stats.at[t],
            dst_ref=stats.at[t],
            send_sem=st_send,
            recv_sem=st_recv,
            device_id=(r, lax.rem(t + k, nt)),
            device_id_type=MESH,
        ).start()

    def wait_bytes(ref, sem):
        pltpu.make_async_copy(ref, ref, sem).wait()

    packs = max(1, min(HD // nr, need_count))
    while need_count % packs:
        packs -= 1
    tall = need_count // packs
    packed = jnp.concatenate(
        [need[k * tall : (k + 1) * tall, :] for k in range(packs)], axis=1
    )
    p_iota = iota((adapters, packs * nr), 0)
    asked = p_iota == packed[0:1, :]
    for e in range(1, tall):
        asked = asked | (p_iota == packed[e : e + 1, :])
    visit = jnp.dot(
        table, jnp.where(asked, 1.0, 0.0).astype(BF16), preferred_element_type=F32
    )[16:24]
    wide = (packs * nr, nvis)
    spread = jnp.where(iota(wide, 1) // 4 == iota(wide, 0) % nr, 1.0, 0.0)
    visit_slot = jnp.dot(
        visit.astype(BF16), spread.astype(BF16), preferred_element_type=F32
    )[0:1].astype(jnp.int32) - 1
    own_slot = jnp.where(is_far, -1, ra - need_count)
    own_slot = jnp.concatenate([own_slot, own_slot], axis=1)
    slot_row = jnp.concatenate([visit_slot, own_slot], axis=1)

    scale = 1.0 / math.sqrt(HD)
    cache_len = ck.shape[1]
    per_row = 2 * GROUP

    def cached_scores(lo, hi):
        @pl.loop(lo, hi, unroll=8)
        def _(i):
            s = (
                lax.dot_general(q_ref[i], ck[i], NT, preferred_element_type=F32) * scale
            )
            live = iota(s.shape, 1) < len_s[i]
            scores[i] = jnp.where(live, s, NEG)

    def ring_stage(h, which_chunks=(0, 1)):
        for way, c in hops(h):
            if c not in which_chunks:
                continue
            hop(way, h, c).wait_recv()
            if (way, c) in (hops(h + 1) if h < half else []):
                hop(way, h + 1, c).start()

    ring_stage(1, (0,))
    ring_stage(1, (1,))

    loads[1].wait()
    wait_bytes(got.at[pl.ds(0, (nr - 1) * SENT), :], a2a_recv)
    wide_rows[...] = got[...].astype(F32)
    for j in range(chunks):
        xall[pl.ds(0, nvis), j * lanes : (j + 1) * lanes] = wide_rows[
            pl.ds(j, nvis, stride=chunks), :
        ].astype(BF16)
    x = xall[...]
    group = 8
    picked = jnp.zeros((rank, ntot), F32)
    for base in range(0, pool, group):
        block = lax.dot_general(
            pa[base * rank : (base + group) * rank, :],
            x,
            NT,
            preferred_element_type=F32,
        )
        for s in range(group):
            picked += jnp.where(
                slot_row == base + s, block[s * rank : (s + 1) * rank], 0.0
            )
    visit_part[t] = picked[:, 0:nvis].astype(BF16)
    own_part[t] = picked[:, nvis:ntot].astype(BF16)

    def hand_round(ref, send_sem, recv_sem):
        @pl.loop(1, nt, unroll=True)
        def _(k):
            pltpu.make_async_remote_copy(
                src_ref=ref.at[t],
                dst_ref=ref.at[t],
                send_sem=send_sem,
                recv_sem=recv_sem,
                device_id=(r, lax.rem(t + k, nt)),
                device_id_type=MESH,
            ).start()

    hand_round(visit_part, rs_send, rs_recv)

    if half > 2:
        ring_stage(2, (0,))
    hand_round(own_part, ag_send, ag_recv)
    for load in small[5:]:
        load.wait()
    for step in range(2):
        for g in range(GROUP):
            q_wide[pl.ds(step * GROUP + g, rows, stride=per_row), :] = q_in[
                step * rows : (step + 1) * rows, g * HD : (g + 1) * HD
            ].astype(F32)
    q_ref[...] = q_wide[...].astype(BF16).reshape(rows, per_row, HD)
    loads[0].wait()
    cached_scores(0, rows // 2)
    loads[4].wait()
    pbt[...] = pb[...].T
    if half > 2:
        ring_stage(2, (1,))

    def low_rank_terms(part, slots):
        total = part[0].astype(F32)
        for k in range(1, nt):
            total += part[k].astype(F32)
        coeffs = total.astype(BF16).astype(F32)
        count = slots.shape[1]
        for s in range(pool):
            expand[s * rank : (s + 1) * rank, 0:count] = jnp.where(
                slots == s, coeffs, 0.0
            ).astype(BF16)
        return jnp.dot(
            pbt[...], expand[:, 0:count], preferred_element_type=F32
        ).T

    wait_bytes(visit_part.at[pl.ds(0, nt - 1)], rs_recv)
    ret_send[...] = low_rank_terms(visit_part, visit_slot)

    @pl.loop(1, nr, unroll=True)
    def _(k):
        to = lax.rem(r + k, nr)
        pltpu.make_async_remote_copy(
            src_ref=ret_send.at[pl.ds(pl.multiple_of(to // 2 * 8, 8), 8), :],
            dst_ref=ret_got.at[pl.ds(pl.multiple_of(r * 8, 8), 8), :],
            send_sem=re_send,
            recv_sem=re_recv,
            device_id=(to, t),
            device_id_type=MESH,
        ).start()

    for h in range(3, half):
        ring_stage(h)

    cached_scores(rows // 2, rows)
    qrows = 8
    span = qrows * per_row
    for b in range(rows // qrows):
        s = scores[b * qrows : (b + 1) * qrows].reshape(span, cache_len)
        top = jnp.max(s, axis=1, keepdims=True)
        e_cache = jnp.exp(s - top)
        top_ref[b * span : (b + 1) * span, :] = top
        bottom_ref[b * span : (b + 1) * span, :] = jnp.sum(
            e_cache, axis=1, keepdims=True
        )
        weights[b * qrows : (b + 1) * qrows] = e_cache.astype(BF16).reshape(
            qrows, per_row, cache_len
        )

    wait_bytes(stats.at[pl.ds(0, nt - 1)], st_recv)
    square = stats[0, 8:16, :]
    for k in range(1, nt):
        square += stats[k, 8:16, :]
    inverse_row = lax.rsqrt(square[0:1] / (width * nt) + EPS)
    inverse = jnp.sum(jnp.where(eye, inverse_row, 0.0), axis=1, keepdims=True)

    def project(o):
        source = lax.rem(t + o, nt)
        block = f_ref[...] if o == 0 else ring[o]
        block = block.astype(F32) * inverse
        gains = stats[source][0:8]
        normed = jnp.concatenate(
            [
                block[:, c * lanes : (c + 1) * lanes] * gains[c : c + 1]
                for c in range(chunks)
            ],
            axis=1,
        ).astype(BF16)
        w = wbuf[pl.ds(pl.multiple_of(source * width, width), width), :]
        return jnp.dot(normed, w, preferred_element_type=F32)

    loads[2].wait()
    loads[3].wait()
    first = project(0) + project(nt - 1)
    if half > 1:
        first += project(1)
    acc_kv[...] = first

    length_row = len_ref[...].astype(F32)
    positions = jnp.sum(
        jnp.where(eye_r, length_row, 0.0), axis=1, keepdims=True
    )
    front = iota((rows, HD), 1) < HD // 2
    angle = (positions + jnp.where(front, 0.0, 1.0)) * freq_ref[...]
    cosine = jnp.cos(angle)
    sine = jnp.sin(angle)
    cosine_turned = pltpu.roll(cosine, HD // 2, 1)
    sine_turned = pltpu.roll(sine, HD // 2, 1)
    cos_ref[0:rows, :] = jnp.where(front, cosine, cosine_turned)
    cos_ref[rows:rows2, :] = jnp.where(front, cosine_turned, cosine)
    sin_ref[0:rows, :] = jnp.where(front, -sine, sine_turned)
    sin_ref[rows:rows2, :] = jnp.where(front, -sine_turned, sine)

    for h in range(3, half):
        acc_kv[...] += project(nt - h + 1) + project(h - 1)

    loads[5].wait()

    @pl.loop(0, rows, unroll=8)
    def _(i):
        att_acc[pl.ds(pl.multiple_of(i * per_row, per_row), per_row), :] = jnp.dot(
            weights[i], cv[i], preferred_element_type=F32
        )

    wait_bytes(own_part.at[pl.ds(0, nt - 1)], ag_recv)
    own_delta = low_rank_terms(own_part, own_slot)
    if half > 2:
        acc_kv[...] += project(nt - half + 1) + project(half - 1)
    ring_stage(half)
    acc_kv[...] += project(half)

    key = acc_kv[:, 0:HD]
    turned = key * cos_ref[...] + pltpu.roll(key, HD // 2, 1) * sin_ref[...]
    new_keys = turned.astype(BF16)
    nk_ref[...] = new_keys

    for b in range(rows // qrows):
        part_rows = slice(b * span, (b + 1) * span)
        q = q_ref[b * qrows : (b + 1) * qrows].reshape(span, HD)
        fresh = (
            lax.dot_general(q, new_keys, NT, preferred_element_type=F32) * scale
        )
        row_of = iota(fresh.shape, 0) // per_row + b * qrows
        step_of = iota(fresh.shape, 0) % per_row // GROUP
        column = iota(fresh.shape, 1)
        seen = (column == row_of) | ((column == row_of + rows) & (step_of == 1))
        fresh = jnp.where(seen, fresh, NEG)
        cache_top = top_ref[part_rows, :]
        top = jnp.maximum(cache_top, jnp.max(fresh, axis=1, keepdims=True))
        shrink = jnp.exp(cache_top - top)
        e_fresh = jnp.exp(fresh - top)
        bottom = bottom_ref[part_rows, :] * shrink + jnp.sum(
            e_fresh, axis=1, keepdims=True
        )
        share = 1.0 / bottom
        fresh_w[part_rows, :] = (e_fresh * share).astype(BF16)
        att_acc[part_rows, :] = att_acc[part_rows, :] * (shrink * share)

    code_f = jnp.where(
        is_far, owner * 8 + lax.rem(r, 2) * 4 + turn * 2, -1000
    ).astype(F32)
    code_col = jnp.sum(jnp.where(eye_r, code_f, 0.0), axis=1, keepdims=True)
    code_col = jnp.concatenate([code_col, code_col + 1.0], axis=0).astype(jnp.int32)
    back = jnp.where(iota((rows2, nr * 8), 1) == code_col, 1.0, 0.0).astype(BF16)
    wait_bytes(ret_got.at[pl.ds(0, (nr - 1) * 8), :], re_recv)
    returned = ret_got[...]
    high = returned.astype(BF16)
    low = (returned - high.astype(F32)).astype(BF16)
    far_delta = jnp.dot(back, high, preferred_element_type=F32) + jnp.dot(
        back, low, preferred_element_type=F32
    )
    new_values = (acc_kv[:, HD : 2 * HD] + inverse * (far_delta + own_delta)).astype(
        BF16
    )
    nv_ref[...] = new_values
    att_acc[...] += jnp.dot(fresh_w[...], new_values, preferred_element_type=F32)
    for step in range(2):
        for g in range(GROUP):
            att_ref[step * rows : (step + 1) * rows, g * HD : (g + 1) * HD] = att_acc[
                pl.ds(step * GROUP + g, rows, stride=per_row), :
            ].astype(BF16)

    for h in range(1, half + 1):
        for way, c in hops(h):
            hop(way, h, c).wait_send()
    wait_bytes(stats.at[pl.ds(0, nt - 1)], st_send)
    wait_bytes(msg.at[pl.ds(0, (nr - 1) * SENT), :], a2a_send)
    wait_bytes(visit_part.at[pl.ds(0, nt - 1)], rs_send)
    wait_bytes(own_part.at[pl.ds(0, nt - 1)], ag_send)
    wait_bytes(ret_got.at[pl.ds(0, (nr - 1) * 8), :], re_send)


def write_out(a, b, c, a_out, b_out, c_out, sem):
    copies = [
        pltpu.make_async_copy(src, dst, sem.at[k])
        for k, (src, dst) in enumerate([(a, a_out), (b, b_out), (c, c_out)])
    ]
    for copy in copies:
        copy.start()
    for copy in copies:
        copy.wait()


def shards(
    features,
    gain,
    w_key,
    w_value,
    pool_a,
    pool_b,
    placement,
    need_lists,
    row_adapter,
    lengths,
    queries,
    cache_k,
    cache_v,
):
    nr, nt = lax.axis_size("replica"), lax.axis_size("tp")
    steps, rows, width = features.shape
    pool, _, rank = pool_a.shape
    cache_len = cache_k.shape[1]
    rows2 = steps * rows
    nvis = nr * 4
    ntot = nvis + rows2
    per_row = steps * GROUP
    half = HD // 2
    frequency = np.float32(THETA) ** (-(np.arange(half, dtype=np.float32) * 2.0) / HD)
    frequency = np.concatenate([frequency, frequency]).astype(np.float32)[None, :]
    vmem = pl.BlockSpec(memory_space=pltpu.VMEM)
    hbm = pl.BlockSpec(memory_space=pltpu.HBM)
    dma = pltpu.SemaphoreType.DMA
    att, nk, nv = pl.pallas_call(
        functools.partial(kernel, nr, nt),
        out_shape=(
            jax.ShapeDtypeStruct((rows2, width), BF16),
            jax.ShapeDtypeStruct((rows2, HD), BF16),
            jax.ShapeDtypeStruct((rows2, HD), BF16),
        ),
        in_specs=[hbm] * 15,
        out_specs=(vmem, vmem, vmem),
        scratch_shapes=[
            pltpu.VMEM((rows2, width), BF16),
            pltpu.VMEM((width // HD, HD), BF16),
            pltpu.VMEM((1, placement.shape[0]), jnp.int32),
            pltpu.VMEM(need_lists.shape[::-1], jnp.int32),
            pltpu.VMEM((1, rows), jnp.int32),
            pltpu.SMEM((rows,), jnp.int32),
            pltpu.VMEM((1, rows), jnp.int32),
            pltpu.VMEM((1, HD), F32),
            pltpu.VMEM((rows2, width), BF16),
            pltpu.VMEM((rows * per_row, HD), F32),
            pltpu.VMEM((rows, per_row, HD), BF16),
            pltpu.VMEM((nt * width, 2 * HD), BF16),
            pltpu.VMEM((pool * rank, width), BF16),
            pltpu.VMEM((pool * rank, HD), BF16),
            pltpu.VMEM((HD, pool * rank), BF16),
            pltpu.VMEM((rows, cache_len, HD), BF16),
            pltpu.VMEM((rows, cache_len, HD), BF16),
            pltpu.VMEM((nt, 16, HD), F32),
            pltpu.VMEM((nr * SENT, HD), BF16),
            pltpu.VMEM((nr * SENT, HD), F32),
            pltpu.VMEM((nr * SENT, HD), BF16),
            pltpu.VMEM((ntot, width), BF16),
            pltpu.VMEM((nt, rows2, width), BF16),
            pltpu.VMEM((nt, rank, nvis), BF16),
            pltpu.VMEM((nt, rank, rows2), BF16),
            pltpu.VMEM((pool * rank, nvis), BF16),
            pltpu.VMEM((nvis, HD), F32),
            pltpu.VMEM((nr * 8, HD), F32),
            pltpu.VMEM((rows, per_row, cache_len), F32),
            pltpu.VMEM((rows, per_row, cache_len), BF16),
            pltpu.VMEM((rows * per_row, rows2), BF16),
            pltpu.VMEM((rows2, 2 * HD), F32),
            pltpu.VMEM((rows * per_row, HD), F32),
            pltpu.VMEM((rows * per_row, 1), F32),
            pltpu.VMEM((rows * per_row, 1), F32),
            pltpu.VMEM((rows2, HD), F32),
            pltpu.VMEM((rows2, HD), F32),
            dma((9,)),
            dma((6,)),
            dma,
            dma,
            dma,
            dma,
            dma((2, max(nt // 2, 1), 2)),
            dma((nt, 2)),
            dma,
            dma,
            dma,
            dma,
            dma,
            dma,
        ],
        compiler_params=pltpu.CompilerParams(
            collective_id=0, has_side_effects=True, vmem_limit_bytes=60 * 2**20
        ),
        cost_estimate=pl.CostEstimate(
            flops=2 * 64 * 8192 * 256, bytes_accessed=12 * 2**20, transcendentals=0
        ),
    )(
        features.reshape(rows2, width),
        gain.reshape(width // HD, HD),
        placement.reshape(1, -1),
        need_lists.T,
        row_adapter.reshape(1, rows),
        lengths,
        lengths.reshape(1, rows),
        jnp.asarray(frequency),
        queries.reshape(rows2, width),
        w_key,
        w_value,
        pool_a.swapaxes(1, 2).reshape(pool * rank, width),
        pool_b.reshape(pool * rank, HD),
        cache_k,
        cache_v,
    )
    shapes = tuple(jax.ShapeDtypeStruct(x.shape, BF16) for x in (att, nk, nv))
    att, nk, nv = pl.pallas_call(
        write_out,
        out_shape=shapes,
        in_specs=[vmem] * 3,
        out_specs=(hbm,) * 3,
        scratch_shapes=[dma((3,))],
        compiler_params=pltpu.CompilerParams(vmem_limit_bytes=60 * 2**20),
    )(att, nk, nv)
    return (
        att.reshape(steps, rows, width),
        nk.reshape(steps, rows, HD),
        nv.reshape(steps, rows, HD),
    )


def solution(mesh):
    placed = (
        P(None, "replica", "tp"),
        P("tp"),
        P(None, "tp"),
        P(None, "tp"),
        P("replica", "tp", None),
        P("replica", None, "tp"),
        P(),
        P(),
        P("replica"),
        P("replica"),
        P(None, "replica", "tp"),
        P("replica", None, "tp"),
        P("replica", None, "tp"),
    )
    return jax.shard_map(
        shards,
        mesh=mesh,
        in_specs=placed,
        out_specs=(P(None, "replica", "tp"), P(None, "replica", "tp"), P(None, "replica", "tp")),
        check_vma=False,
    )
```
